128 devices in a mesh: dp: 2 (over core), ctx: 16 (over z, x), tp: 4 (over y).
Axes of the slice: x: 4, y: 4, z: 4, core: 2. Of those that a mesh axis runs over, the one named last changes fastest.
Arguments:
- tokens: bfloat16 [8192, 4096], P(('ctx', 'tp'), 'dp'), may hold values from -6 to 6
- cotangent: bfloat16 [8192, 4096], P(('ctx', 'tp'), 'dp'), may hold values from -0.29882812 to 0.29882812
- probs: bfloat16 [8192, 8], P(('ctx', 'tp')), may hold values from 0.019897461 to 0.59765625
- expert_ids: int32 [8192, 8], P(('ctx', 'tp')), may hold values from 0 to 63, all different within a row; in each aligned block of 128 rows (0 to 127, 128 to 255, ...) at most 18 rows name the same one
- gate_weight: bfloat16 [64, 4096, 768], P(('ctx', 'tp'), 'dp'), may hold values from -0.09375 to 0.09375
- up_weight: bfloat16 [64, 4096, 768], P(('ctx', 'tp'), 'dp'), may hold values from -0.09375 to 0.09375
- down_weight: bfloat16 [64, 768, 4096], P(('ctx', 'tp'), None, 'dp'), may hold values from -0.21875 to 0.21875
Outputs:
- grad_tokens: bfloat16 [8192, 4096], P(('ctx', 'tp'), 'dp')
- grad_probs: bfloat16 [8192, 8], P(('ctx', 'tp'))
- grad_gate: bfloat16 [64, 4096, 768], P(('ctx', 'tp'), 'dp')
- grad_up: bfloat16 [64, 4096, 768], P(('ctx', 'tp'), 'dp')
- grad_down: bfloat16 [64, 768, 4096], P(('ctx', 'tp'), None, 'dp')
The draws below stay inside these ranges and needn't reach their ends.
Inputs may be any that keep to these rules, and one draw needn't show every extreme that they name: `expert_ids`: each row names 8 different experts; among the tokens of one index of ctx+tp no expert is named by more than 18 rows, and in every draw some expert is named exactly 18 times in some block.
All inputs are finite; a program needn't handle non-finite values.
Results may differ from the reference program's by a relative error of at most 0.023.
Values may be sent and summed in bfloat16 or wider, within the bound.
No kernel may reach another device: no remote copies, remote signals or barrier semaphores. Data moves between devices by JAX's collectives and lax.ppermute only.
A program may use at most 192 MiB of HBM per device.

```python
import math
import jax
import jax.numpy as jnp
import numpy as np
from jax import lax

D = 4096
FFW = 768
TOP = 8
TOK_DEV = 128
EXPERTS = 64
CAP = 18
TOKENS = 8192


def steps_of(own_key, extent, split, smallest, largest):
    loudness = 1.0
    for dim, parts in split:
        draws = jax.random.uniform(jax.random.fold_in(jax.random.fold_in(own_key, 6), dim), (parts,), jnp.float32, smallest / len(split), largest / len(split))
        loudness = loudness * jnp.repeat(jnp.exp(draws), extent[dim] // parts).reshape((-1,) + (1,) * (len(extent) - 1 - dim))
    return loudness


def shared_out(rng, own, number, rows, count, top, limit, skew):
    ranking = jax.random.permutation(rng, count)
    crowded, usual = shares(count, rows * top, limit, skew, True), shares(count, rows * top, limit, skew, False)
    places = jnp.arange(count)

    def named(lengths, offset_by):
        used = int((lengths > 0).sum())
        fixed = max(1, used // 4)
        moved = fixed + (places - fixed + offset_by * (used - fixed)) % max(1, count - fixed)
        return jnp.zeros((count,), jnp.int32).at[ranking[jnp.where(places < fixed, places, moved)]].set(jnp.asarray(lengths, jnp.int32))

    lengths = jnp.where(number % 4 == 0, named(crowded, number // 4), named(usual, number - number // 4 - 1))
    mixed = jax.random.permutation(jax.random.fold_in(own, 3), count)
    giver, receiver = mixed[0:count // 2 * 2:2], mixed[1:count // 2 * 2:2]
    room = jnp.minimum(lengths[giver] - 1, limit - lengths[receiver]) // 2
    room = jnp.where((giver == ranking[0]) | (receiver == ranking[0]) | (lengths[receiver] == 0), 0, jnp.maximum(room, 0))
    moved = jax.random.randint(jax.random.fold_in(own, 4), (count // 2,), 0, 1 << 20) % (room + 1)
    lengths = lengths.at[giver].add(-moved).at[receiver].add(moved)
    items = jnp.searchsorted(jnp.cumsum(lengths), jnp.arange(rows * top), side="right").astype(jnp.int32)
    table = items.reshape(top, rows).T
    table = table[jax.random.permutation(jax.random.fold_in(own, 1), rows)]
    offset_by = jax.random.randint(jax.random.fold_in(own, 2), (rows, 1), 0, top)
    return jnp.take_along_axis(table, (jnp.arange(top)[None, :] + offset_by) % top, axis=1)


def shares(amount, total, limit, skew, full):
    portions = [(1 << 20) // math.isqrt(standing ** skew) + 1 for standing in range(1, amount + 1)]
    largest = limit if full else min(limit, max(-(-total // amount), total * portions[0] // sum(portions)))
    least = 1 if total - largest >= amount - 1 else 0
    counts, rest = [largest] + [least] * (amount - 1), total - largest - least * (amount - 1)
    while rest > 0:
        movable = [i for i in range(1, amount) if counts[i] < largest] or [i for i in range(1, amount) if counts[i] < limit]
        mass, left = sum([portions[i] for i in movable]), rest
        for i in movable:
            more = min(limit - counts[i], max(1, left * portions[i] // mass), rest)
            counts[i] = counts[i] + more
            rest = rest - more
    return np.array(counts)


def centred(stream_key, extent, spread, bound, split=(), kind=jnp.bfloat16):
    array = spread * jax.random.normal(stream_key, extent, jnp.float32)
    if split:
        array = array * steps_of(stream_key, extent, split, -0.22, 0.18)
    return jnp.clip(array, -bound, bound).astype(kind)


def setup_inputs(seed: int = 0) -> dict:
    streams_of = jax.random.split(jax.random.key(seed), 8)
    tokens = centred(streams_of[0], (TOKENS, D), 1.0, 6.0, ((0, 64), (1, 2)))
    cotangent = centred(streams_of[1], (TOKENS, D), 0.05, 0.29882812, ((0, 64), (1, 2)))
    probs = jnp.clip(jnp.exp(math.log(0.59765625) - 3.4024236 * jax.random.uniform(streams_of[2], (TOKENS, TOP), jnp.float32) ** steps_of(streams_of[2], (TOKENS, TOP), ((0, 64),), -0.2, 0.2)), 0.019897461, 0.59765625).astype(jnp.bfloat16)
    expert_ids_keys = jax.random.split(jax.random.fold_in(streams_of[3], 1), TOKENS // TOK_DEV)
    expert_ids_turns = jax.random.permutation(jax.random.fold_in(streams_of[3], 3), TOKENS // TOK_DEV)
    expert_ids = jax.vmap(lambda own, number: shared_out(jax.random.fold_in(streams_of[3], 2), own, number, TOK_DEV, EXPERTS, TOP, CAP, 2))(expert_ids_keys, expert_ids_turns).reshape((TOKENS, TOP))
    gate_weight = centred(streams_of[4], (EXPERTS, D, FFW), D ** -0.5, 0.09375, ((0, 64), (1, 2)))
    up_weight = centred(streams_of[5], (EXPERTS, D, FFW), D ** -0.5, 0.09375, ((0, 64), (1, 2)))
    down_weight = centred(streams_of[6], (EXPERTS, FFW, D), FFW ** -0.5, 0.21875, ((0, 64), (2, 2)))
    return {"tokens": tokens, "cotangent": cotangent, "probs": probs, "expert_ids": expert_ids, "gate_weight": gate_weight, "up_weight": up_weight, "down_weight": down_weight}


def finish(gate_pre, up_pre, back_grad, weight):
    sigmoid_gate = jax.nn.sigmoid(gate_pre)
    silu_gate = gate_pre * sigmoid_gate
    activation = silu_gate * up_pre
    prob_grad = jnp.sum(activation * back_grad, axis=-1).astype(jnp.bfloat16)
    act_grad = weight[:, None] * back_grad
    gate_grad = (act_grad * up_pre * sigmoid_gate * (1.0 + gate_pre * (1.0 - sigmoid_gate))).astype(jnp.bfloat16)
    up_grad = (act_grad * silu_gate).astype(jnp.bfloat16)
    weighted = (weight[:, None] * activation).astype(jnp.bfloat16)
    return weighted, gate_grad, up_grad, prob_grad


def reference(tokens, cotangent, probs, expert_ids, gate_weight, up_weight, down_weight):
    token_count = tokens.shape[0]
    block_count = token_count // TOK_DEV
    pair_count = token_count * TOP
    flat_ids = expert_ids.reshape(block_count, TOK_DEV * TOP).astype(jnp.int32)
    onehot = (flat_ids[:, :, None] == jnp.arange(EXPERTS, dtype=jnp.int32)[None, None, :]).astype(jnp.int32)
    slot_rank = jnp.sum((jnp.cumsum(onehot, axis=1) - onehot) * onehot, axis=2)
    block_ids = jnp.arange(block_count, dtype=jnp.int32)[:, None]
    slot_index = (flat_ids * (block_count * CAP) + block_ids * CAP + slot_rank).reshape(-1).astype(jnp.int32)
    slot_owner = jnp.full((EXPERTS * block_count * CAP,), pair_count, jnp.int32)
    slot_owner = slot_owner.at[slot_index].set(jnp.arange(pair_count, dtype=jnp.int32))
    slot_owner = slot_owner.reshape(EXPERTS, block_count * CAP)
    prob_flat = probs.reshape(-1)

    def expert(operand):
        slot_rows, gate_mat, up_mat, down_mat = operand
        live_slot = slot_rows < pair_count
        safe_pair = jnp.minimum(slot_rows, pair_count - 1).astype(jnp.int32)
        token_row = (safe_pair // TOP).astype(jnp.int32)
        picked_in = jnp.where(live_slot[:, None], tokens[token_row], jnp.zeros((), jnp.bfloat16))
        picked_cot = jnp.where(live_slot[:, None], cotangent[token_row], jnp.zeros((), jnp.bfloat16))
        weight = jnp.where(live_slot, prob_flat[safe_pair].astype(jnp.float32), jnp.float32(0.0))
        gate_pre = jnp.dot(picked_in, gate_mat, preferred_element_type=jnp.float32)
        up_pre = jnp.dot(picked_in, up_mat, preferred_element_type=jnp.float32)
        back_grad = jnp.dot(picked_cot, down_mat.T, preferred_element_type=jnp.float32)
        weighted, gate_grad, up_grad, prob_grad = finish(gate_pre, up_pre, back_grad, weight)
        grad_down = jnp.dot(weighted.T, picked_cot, preferred_element_type=jnp.float32).astype(jnp.bfloat16)
        grad_gate = jnp.dot(picked_in.T, gate_grad, preferred_element_type=jnp.float32).astype(jnp.bfloat16)
        grad_up = jnp.dot(picked_in.T, up_grad, preferred_element_type=jnp.float32).astype(jnp.bfloat16)
        pair_grad = (jnp.dot(gate_grad, gate_mat.T, preferred_element_type=jnp.float32)
                     + jnp.dot(up_grad, up_mat.T, preferred_element_type=jnp.float32)).astype(jnp.bfloat16)
        return grad_gate, grad_up, grad_down, pair_grad, prob_grad

    grad_gate, grad_up, grad_down, pair_grad, prob_grad = lax.map(
        expert, (slot_owner, gate_weight, up_weight, down_weight))
    pair_rows = pair_grad.reshape(-1, D)[slot_index].reshape(token_count, TOP, D)
    grad_tokens = jnp.sum(pair_rows.astype(jnp.float32), axis=1).astype(jnp.bfloat16)
    grad_probs = prob_grad.reshape(-1)[slot_index].reshape(token_count, TOP)
    return grad_tokens, grad_probs, grad_gate, grad_up, grad_down
```

```python
import functools

import jax
import jax.numpy as jnp
from jax import lax
from jax.experimental import pallas as pl
from jax.experimental.pallas import tpu as pltpu
from jax.sharding import PartitionSpec as P

BF = jnp.bfloat16
F32 = jnp.float32
LANE = 128
MAIN = 16
EXTRA = 2
PEERS = 16
CAP = MAIN + EXTRA
ROWS = PEERS * CAP
VMEM = 60 * 2**20


def iota(shape, dim):
    return lax.broadcasted_iota(jnp.int32, shape, dim)


def dot(a, b):
    return jnp.dot(a, b, preferred_element_type=F32)


def expert_ranks(ids, experts):
    top, tokens = ids.shape
    expert = iota((experts, tokens), 0)
    hit = jnp.zeros((experts, tokens), F32)
    for k in range(top):
        hit = hit + jnp.where(ids[k : k + 1] == expert, 1.0, 0.0)
    earlier = jnp.where(iota((tokens, tokens), 0) < iota((tokens, tokens), 1), 1.0, 0.0)
    rank = dot(hit.astype(BF), earlier.astype(BF))
    return jnp.where(hit > 0.0, rank, -1.0)


def expert_probs(ids, probs, experts):
    top, tokens = ids.shape
    expert = iota((experts, tokens), 0)
    out = jnp.zeros((experts, tokens), F32)
    for k in range(top):
        out = out + jnp.where(ids[k : k + 1] == expert, probs[k : k + 1], 0.0)
    return out


def by_slot(a):
    return jnp.broadcast_to(a[:, None, :], (PEERS, MAIN, a.shape[1])).reshape(PEERS * MAIN, a.shape[1])


def extra_order(pack):
    shape = (PEERS * MAIN, PEERS * MAIN)
    row, col = iota(shape, 0), iota(shape, 1)
    if pack:
        source = (row % 16) // 2 * 32 + row // 16 * 2 + row % 2
    else:
        source = (row % 32) // 2 * 16 + row // 32 * 2 + row % 2
    return jnp.where(col == source, 1.0, 0.0).astype(BF)


def store_main(out_ref, values):
    for c in range(values.shape[1] // LANE):
        out_ref[:, c * MAIN : (c + 1) * MAIN, :] = values[:, c * LANE : (c + 1) * LANE].reshape(PEERS, MAIN, LANE)


def store_extra(out_ref, values, start):
    for g in range(values.shape[1] // LANE):
        at = start + g * MAIN
        out_ref[:, at : at + MAIN, :] = values[:, g * LANE : (g + 1) * LANE].reshape(PEERS, MAIN, LANE)


def unpack(in_ref, out_ref):
    width = out_ref.shape[1]
    tiles = width // LANE
    for c in range(tiles):
        out_ref[: PEERS * MAIN, c * LANE : (c + 1) * LANE] = in_ref[:, c * MAIN : (c + 1) * MAIN, :].reshape(
            PEERS * MAIN, LANE
        )
    groups = tiles // 8
    start = tiles * MAIN
    extra = jnp.concatenate(
        [
            in_ref[:, start + g * MAIN : start + (g + 1) * MAIN, :].reshape(PEERS * MAIN, LANE)
            for g in range(groups)
        ],
        axis=1,
    )
    ordered = dot(extra_order(False), extra).astype(BF)
    for g in range(groups):
        for c in range(8):
            at = (g * 8 + c) * LANE
            out_ref[PEERS * MAIN :, at : at + LANE] = ordered[
                c * 2 * PEERS : (c + 1) * 2 * PEERS, g * LANE : (g + 1) * LANE
            ]


def pack_kernel(weighted, ids_ref, probs_ref, x_ref, out_ref, rank_ref, prob_ref, side_ref):
    step = pl.program_id(0)
    tokens, width = x_ref.shape
    groups = width // LANE // 8
    experts = rank_ref.shape[0]

    @pl.when(step == 0)
    def _():
        rank_ref[...] = expert_ranks(ids_ref[...], experts)
        if weighted:
            prob_ref[...] = expert_probs(ids_ref[...], probs_ref[...].astype(F32), experts)
        for c in range(8):
            for g in range(groups):
                at = (g * 8 + c) * LANE
                side_ref[c * tokens : (c + 1) * tokens, g * LANE : (g + 1) * LANE] = x_ref[:, at : at + LANE]

    peers = pl.ds(pl.multiple_of(step * PEERS, PEERS), PEERS)
    rank = by_slot(rank_ref[peers, :])
    value = by_slot(prob_ref[peers, :]) if weighted else jnp.ones(rank.shape, F32)
    row = iota(rank.shape, 0)
    main = jnp.where(rank == (row % MAIN).astype(F32), value, 0.0).astype(BF)
    store_main(out_ref, dot(main, x_ref[...]).astype(BF))
    extra = jnp.where(rank == (MAIN + row % EXTRA).astype(F32), value, 0.0)
    column = (row % MAIN) // EXTRA
    spread = jnp.concatenate([jnp.where(column == c, extra, 0.0).astype(BF) for c in range(8)], axis=1)
    store_extra(out_ref, dot(spread, side_ref[...]).astype(BF), width // LANE * MAIN)


def pack(weighted, ids, probs, x, experts):
    tokens, width = x.shape
    rows = width // LANE * CAP
    return pl.pallas_call(
        functools.partial(pack_kernel, weighted),
        grid=(experts // PEERS,),
        out_shape=jax.ShapeDtypeStruct((experts, rows, LANE), BF),
        in_specs=[
            pl.BlockSpec(ids.shape, lambda i: (0, 0)),
            pl.BlockSpec(probs.shape, lambda i: (0, 0)),
            pl.BlockSpec(x.shape, lambda i: (0, 0)),
        ],
        out_specs=pl.BlockSpec((PEERS, rows, LANE), lambda i: (i, 0, 0)),
        scratch_shapes=[
            pltpu.VMEM((experts, tokens), F32),
            pltpu.VMEM((experts, tokens), F32),
            pltpu.VMEM((8 * tokens, width // 8), BF),
        ],
        compiler_params=pltpu.CompilerParams(vmem_limit_bytes=VMEM),
        cost_estimate=pl.CostEstimate(
            flops=4 * experts * MAIN * tokens * width, bytes_accessed=2 * experts * rows * LANE, transcendentals=0
        ),
        name="pack_cotangent" if weighted else "pack_tokens",
    )(ids, probs, x)


def project_kernel(in_ref, *refs):
    count = (len(refs) - 1) // 2
    weights, rows_ref, outs = refs[:count], refs[count], refs[count + 1 :]
    unpack(in_ref, rows_ref)
    for weight, out in zip(weights, outs):
        out[...] = dot(rows_ref[...], weight[...]).astype(BF)


def project(name, got, weights):
    experts, rows, _ = got.shape
    width = rows // CAP * LANE
    hidden = weights[0].shape[1]
    total = experts * CAP
    return pl.pallas_call(
        project_kernel,
        grid=(experts // PEERS,),
        out_shape=[jax.ShapeDtypeStruct((total, width), BF)]
        + [jax.ShapeDtypeStruct((total, hidden), BF) for _ in weights],
        in_specs=[pl.BlockSpec((PEERS, rows, LANE), lambda i: (i, 0, 0))]
        + [pl.BlockSpec(w.shape, lambda i: (0, 0)) for w in weights],
        out_specs=[pl.BlockSpec((ROWS, width), lambda i: (i, 0))]
        + [pl.BlockSpec((ROWS, hidden), lambda i: (i, 0)) for _ in weights],
        compiler_params=pltpu.CompilerParams(vmem_limit_bytes=VMEM),
        cost_estimate=pl.CostEstimate(
            flops=2 * total * width * hidden * len(weights),
            bytes_accessed=2 * (2 * total * width + len(weights) * (width + total) * hidden),
            transcendentals=0,
        ),
        name=name,
    )(got, *weights)


def pair_kernel(gate, gate_far, up, up_far, back, back_far, gate_t, up_t, out_ref, act_ref, gg_ref, ug_ref):
    g = gate[...].astype(F32) + gate_far[...].astype(F32)
    u = up[...].astype(F32) + up_far[...].astype(F32)
    b = back[...].astype(F32) + back_far[...].astype(F32)
    sigmoid = jax.nn.sigmoid(g)
    silu = g * sigmoid
    act = silu * u
    act_ref[...] = act.astype(BF)
    gg_ref[...] = (b * u * sigmoid * (1.0 + g * (1.0 - sigmoid))).astype(BF)
    ug_ref[...] = (b * silu).astype(BF)
    prob_grad = jnp.sum(act * b, axis=1, keepdims=True).astype(BF).astype(F32)
    y = (dot(gg_ref[...], gate_t[...]) + dot(ug_ref[...], up_t[...])).astype(BF)
    width = y.shape[1]
    tiles = width // LANE
    groups = tiles // 8
    store_main(out_ref, y[: PEERS * MAIN])
    extra = jnp.concatenate(
        [
            jnp.concatenate(
                [y[PEERS * MAIN :, (g * 8 + c) * LANE : (g * 8 + c + 1) * LANE] for g in range(groups)], axis=1
            )
            for c in range(8)
        ],
        axis=0,
    )
    store_extra(out_ref, dot(extra_order(True), extra).astype(BF), tiles * MAIN)
    row, lane = iota((ROWS, LANE), 0), iota((ROWS, LANE), 1)
    slot = jnp.where(row < PEERS * MAIN, row % MAIN, MAIN + row % EXTRA)
    by_lane = jnp.where(lane == slot, prob_grad, 0.0).astype(BF)
    peer, of = iota((PEERS, ROWS), 0), iota((PEERS, ROWS), 1)
    owner = jnp.where(of < PEERS * MAIN, of // MAIN, (of - PEERS * MAIN) // EXTRA)
    slots = dot(jnp.where(peer == owner, 1.0, 0.0).astype(BF), by_lane)
    out_ref[:, tiles * CAP :, :] = by_slot(slots).astype(BF).reshape(PEERS, MAIN, LANE)


def pair(gate, gate_far, up, up_far, back, back_far, gate_t, up_t):
    total, hidden = gate.shape
    width = gate_t.shape[1]
    experts = total // CAP
    rows = width // LANE * CAP + MAIN
    block = pl.BlockSpec((ROWS, hidden), lambda i: (i, 0))
    whole = pl.BlockSpec(gate_t.shape, lambda i: (0, 0))
    return pl.pallas_call(
        pair_kernel,
        grid=(experts // PEERS,),
        out_shape=[jax.ShapeDtypeStruct((experts, rows, LANE), BF)]
        + [jax.ShapeDtypeStruct((total, hidden), BF)] * 3,
        in_specs=[block] * 6 + [whole] * 2,
        out_specs=[pl.BlockSpec((PEERS, rows, LANE), lambda i: (i, 0, 0))] + [block] * 3,
        compiler_params=pltpu.CompilerParams(vmem_limit_bytes=VMEM),
        cost_estimate=pl.CostEstimate(
            flops=4 * total * width * hidden,
            bytes_accessed=2 * (total * width + 9 * total * hidden + 2 * width * hidden),
            transcendentals=total * hidden,
        ),
        name="pair_grad",
    )(gate, gate_far, up, up_far, back, back_far, gate_t, up_t)


def combine_kernel(ids_ref, probs_ref, in_ref, slots_ref, out_ref, probs_out_ref, rank_ref, rows_ref, total_ref):
    step = pl.program_id(0)
    experts, tokens = rank_ref.shape

    @pl.when(step == 0)
    def _():
        rank_ref[...] = expert_ranks(ids_ref[...], experts)
        total_ref[...] = jnp.zeros_like(total_ref)

    unpack(in_ref, rows_ref)
    some = rank_ref[pl.ds(pl.multiple_of(step * PEERS, PEERS), PEERS), :]
    rank = by_slot(some)
    row = iota(rank.shape, 0)
    main = jnp.where(rank == (row % MAIN).astype(F32), 1.0, 0.0)
    rank = jnp.broadcast_to(some[:, None, :], (PEERS, 8, tokens)).reshape(PEERS * 8, tokens)
    row = iota(rank.shape, 0)
    extra = jnp.where(rank == (MAIN + row % 8).astype(F32), 1.0, 0.0)
    shape = (PEERS * EXTRA, PEERS * 8)
    keep = jnp.where(iota(shape, 1) == iota(shape, 0) // EXTRA * 8 + iota(shape, 0) % EXTRA, 1.0, 0.0)
    extra = dot(keep.astype(BF), extra.astype(BF))
    which = jnp.concatenate([main, extra], axis=0).astype(BF)
    total_ref[...] += lax.dot_general(which, rows_ref[...], (((0,), (0,)), ((), ())), preferred_element_type=F32)

    @pl.when(step == pl.num_programs(0) - 1)
    def _():
        out_ref[...] = total_ref[...].astype(BF)
        slots = slots_ref[:, 0, :].astype(F32)
        rank = rank_ref[...]
        found = jnp.zeros((experts, tokens), F32)
        for s in range(CAP):
            found = found + jnp.where(rank == float(s), slots[:, s : s + 1], 0.0)
        ids = ids_ref[...]
        expert = iota((experts, tokens), 0)
        grads = [
            jnp.sum(jnp.where(ids[k : k + 1] == expert, found, 0.0), axis=0, keepdims=True)
            for k in range(ids.shape[0])
        ]
        probs_out_ref[...] = (jnp.concatenate(grads, axis=0) / probs_ref[...].astype(F32)).astype(BF)


def combine(ids, probs, got):
    experts, rows, _ = got.shape
    tiles = (rows - MAIN) // CAP
    top, tokens = ids.shape
    width = tiles * LANE
    small = pl.BlockSpec(ids.shape, lambda i: (0, 0))
    return pl.pallas_call(
        combine_kernel,
        grid=(experts // PEERS,),
        out_shape=[jax.ShapeDtypeStruct((tokens, width), BF), jax.ShapeDtypeStruct((top, tokens), BF)],
        in_specs=[
            small,
            small,
            pl.BlockSpec((PEERS, rows, LANE), lambda i: (i, 0, 0)),
            pl.BlockSpec((experts, MAIN, LANE), lambda i: (0, tiles * CAP // MAIN, 0)),
        ],
        out_specs=[pl.BlockSpec((tokens, width), lambda i: (0, 0)), small],
        scratch_shapes=[
            pltpu.VMEM((experts, tokens), F32),
            pltpu.VMEM((ROWS, width), BF),
            pltpu.VMEM((tokens, width), F32),
        ],
        compiler_params=pltpu.CompilerParams(vmem_limit_bytes=VMEM),
        cost_estimate=pl.CostEstimate(
            flops=2 * experts * CAP * tokens * width, bytes_accessed=2 * experts * rows * LANE, transcendentals=0
        ),
        name="combine",
    )(ids, probs, got, got)


def exchange(x):
    return lax.all_to_all(x, ("ctx", "tp"), split_axis=0, concat_axis=0, tiled=True)


def other_core(x):
    return lax.ppermute(x, "dp", [(0, 1), (1, 0)])


def contract_rows(left, right):
    return lax.dot_general(left, right, (((0,), (0,)), ((), ())), preferred_element_type=F32).astype(BF)


def per_device(tokens, cotangent, probs, expert_ids, gate_weight, up_weight, down_weight):
    experts = lax.axis_size("ctx") * lax.axis_size("tp")
    gate_mat, up_mat, down_mat = gate_weight[0], up_weight[0], down_weight[0]
    ids, weights = expert_ids.T, probs.T
    got_tokens = exchange(pack(False, ids, weights, tokens, experts))
    got_cot = exchange(pack(True, ids, weights, cotangent, experts))
    rows, gate, up = project("gate_up", got_tokens, (gate_mat, up_mat))
    gate_far, up_far = other_core(gate), other_core(up)
    cot_rows, back = project("back", got_cot, (down_mat.T,))
    back_far = other_core(back)
    sent, act, gate_grad, up_grad = pair(gate, gate_far, up, up_far, back, back_far, gate_mat.T, up_mat.T)
    got_pairs = exchange(sent)
    grad_down = contract_rows(act, cot_rows)
    grad_gate = contract_rows(rows, gate_grad)
    grad_up = contract_rows(rows, up_grad)
    grad_tokens, grad_probs = combine(ids, weights, got_pairs)
    return (grad_tokens, grad_probs.T, grad_gate[None], grad_up[None], grad_down[None])


def solution(mesh):
    return jax.shard_map(
        per_device,
        mesh=mesh,
        in_specs=(
            P(("ctx", "tp"), "dp"),
            P(("ctx", "tp"), "dp"),
            P(("ctx", "tp"), None),
            P(("ctx", "tp"), None),
            P(("ctx", "tp"), "dp", None),
            P(("ctx", "tp"), "dp", None),
            P(("ctx", "tp"), None, "dp"),
        ),
        out_specs=(
            P(("ctx", "tp"), "dp"),
            P(("ctx", "tp"), None),
            P(("ctx", "tp"), "dp", None),
            P(("ctx", "tp"), "dp", None),
            P(("ctx", "tp"), None, "dp"),
        ),
        check_vma=False,
    )
```

```python
import functools

import jax
import jax.numpy as jnp
from jax import lax
from jax.experimental import pallas as pl
from jax.experimental.pallas import tpu as pltpu
from jax.sharding import PartitionSpec as P

BF = jnp.bfloat16
F32 = jnp.float32
LANE = 128
MAIN = 16
EXTRA = 2
PACK_PEERS = 32
PEERS = 16
SUM_PEERS = 16
CAP = MAIN + EXTRA
VMEM = 32 * 2**20


def iota(shape, dim):
    return lax.broadcasted_iota(jnp.int32, shape, dim)


def dot(a, b):
    return jnp.dot(a, b, preferred_element_type=F32)


def expert_ranks(ids, experts):
    top, tokens = ids.shape
    expert = iota((experts, tokens), 0)
    hit = jnp.zeros((experts, tokens), F32)
    for k in range(top):
        hit = hit + jnp.where(ids[k : k + 1] == expert, 1.0, 0.0)
    earlier = jnp.where(iota((tokens, tokens), 0) < iota((tokens, tokens), 1), 1.0, 0.0)
    rank = dot(hit.astype(BF), earlier.astype(BF))
    return jnp.where(hit > 0.0, rank, -1.0)


def expert_probs(ids, probs, experts):
    top, tokens = ids.shape
    expert = iota((experts, tokens), 0)
    out = jnp.zeros((experts, tokens), F32)
    for k in range(top):
        out = out + jnp.where(ids[k : k + 1] == expert, probs[k : k + 1], 0.0)
    return out


def by_slot(a, slots=MAIN):
    peers, tokens = a.shape
    return jnp.broadcast_to(a[:, None, :], (peers, slots, tokens)).reshape(peers * slots, tokens)


def extra_order(peers, pack):
    shape = (peers * MAIN, peers * MAIN)
    row, col = iota(shape, 0), iota(shape, 1)
    step = peers * EXTRA
    if pack:
        source = (row % MAIN) // EXTRA * step + row // MAIN * EXTRA + row % EXTRA
    else:
        source = (row % step) // EXTRA * MAIN + row // step * EXTRA + row % EXTRA
    return jnp.where(col == source, 1.0, 0.0).astype(BF)


def store_main(out_ref, values):
    for c in range(values.shape[1] // LANE):
        out_ref[:, c * MAIN : (c + 1) * MAIN, :] = values[:, c * LANE : (c + 1) * LANE].reshape(-1, MAIN, LANE)


def store_extra(out_ref, values, start):
    for g in range(values.shape[1] // LANE):
        at = start + g * MAIN
        out_ref[:, at : at + MAIN, :] = values[:, g * LANE : (g + 1) * LANE].reshape(-1, MAIN, LANE)


def unpack(in_ref, out_ref):
    peers, width = in_ref.shape[0], out_ref.shape[1]
    tiles, main, step = width // LANE, peers * MAIN, peers * EXTRA
    for c in range(tiles):
        out_ref[:main, c * LANE : (c + 1) * LANE] = in_ref[:, c * MAIN : (c + 1) * MAIN, :].reshape(main, LANE)
    groups = tiles // 8
    start = tiles * MAIN
    extra = jnp.concatenate(
        [in_ref[:, start + g * MAIN : start + (g + 1) * MAIN, :].reshape(main, LANE) for g in range(groups)], axis=1
    )
    ordered = dot(extra_order(peers, False), extra).astype(BF)
    for g in range(groups):
        for c in range(8):
            at = (g * 8 + c) * LANE
            out_ref[main:, at : at + LANE] = ordered[c * step : (c + 1) * step, g * LANE : (g + 1) * LANE]


def pack_kernel(weighted, ids_ref, probs_ref, x_ref, out_ref, rank_ref, prob_ref, side_ref):
    step = pl.program_id(0)
    tokens, width = x_ref.shape
    groups = width // LANE // 8
    experts = rank_ref.shape[0]

    @pl.when(step == 0)
    def _():
        rank_ref[...] = expert_ranks(ids_ref[...], experts)
        if weighted:
            prob_ref[...] = expert_probs(ids_ref[...], probs_ref[...].astype(F32), experts)
        for c in range(8):
            for g in range(groups):
                at = (g * 8 + c) * LANE
                side_ref[c * tokens : (c + 1) * tokens, g * LANE : (g + 1) * LANE] = x_ref[:, at : at + LANE]

    count = out_ref.shape[0]
    peers = pl.ds(pl.multiple_of(step * count, count), count)
    rank = by_slot(rank_ref[peers, :])
    value = by_slot(prob_ref[peers, :]) if weighted else jnp.ones(rank.shape, F32)
    row = iota(rank.shape, 0)
    main = jnp.where(rank == (row % MAIN).astype(F32), value, 0.0).astype(BF)
    store_main(out_ref, dot(main, x_ref[...]).astype(BF))
    extra = jnp.where(rank == (MAIN + row % EXTRA).astype(F32), value, 0.0)
    column = (row % MAIN) // EXTRA
    spread = jnp.concatenate([jnp.where(column == c, extra, 0.0).astype(BF) for c in range(8)], axis=1)
    store_extra(out_ref, dot(spread, side_ref[...]).astype(BF), width // LANE * MAIN)


def pack(weighted, ids, probs, x, experts):
    tokens, width = x.shape
    rows = width // LANE * CAP
    return pl.pallas_call(
        functools.partial(pack_kernel, weighted),
        grid=(experts // PACK_PEERS,),
        out_shape=jax.ShapeDtypeStruct((experts, rows, LANE), BF),
        in_specs=[
            pl.BlockSpec(ids.shape, lambda i: (0, 0)),
            pl.BlockSpec(probs.shape, lambda i: (0, 0)),
            pl.BlockSpec(x.shape, lambda i: (0, 0)),
        ],
        out_specs=pl.BlockSpec((PACK_PEERS, rows, LANE), lambda i: (i, 0, 0)),
        scratch_shapes=[
            pltpu.VMEM((experts, tokens), F32),
            pltpu.VMEM((experts, tokens), F32),
            pltpu.VMEM((8 * tokens, width // 8), BF),
        ],
        compiler_params=pltpu.CompilerParams(vmem_limit_bytes=VMEM),
        cost_estimate=pl.CostEstimate(
            flops=4 * experts * MAIN * tokens * width, bytes_accessed=2 * experts * rows * LANE, transcendentals=0
        ),
        name="pack_cotangent" if weighted else "pack_tokens",
    )(ids, probs, x)


def project_kernel(in_ref, *refs):
    count = (len(refs) - 1) // 2
    weights, rows_ref, outs = refs[:count], refs[count], refs[count + 1 :]
    unpack(in_ref, rows_ref)
    for weight, out in zip(weights, outs):
        out[...] = dot(rows_ref[...], weight[...]).astype(BF)


def project(name, got, weights):
    experts, rows, _ = got.shape
    width = rows // CAP * LANE
    hidden = weights[0].shape[1]
    total = experts * CAP
    return pl.pallas_call(
        project_kernel,
        grid=(experts // PEERS,),
        out_shape=[jax.ShapeDtypeStruct((total, width), BF)]
        + [jax.ShapeDtypeStruct((total, hidden), BF) for _ in weights],
        in_specs=[pl.BlockSpec((PEERS, rows, LANE), lambda i: (i, 0, 0))]
        + [pl.BlockSpec(memory_space=pltpu.VMEM) for _ in weights],
        out_specs=[pl.BlockSpec((PEERS * CAP, width), lambda i: (i, 0))]
        + [pl.BlockSpec((PEERS * CAP, hidden), lambda i: (i, 0)) for _ in weights],
        compiler_params=pltpu.CompilerParams(vmem_limit_bytes=VMEM),
        cost_estimate=pl.CostEstimate(
            flops=2 * total * width * hidden * len(weights),
            bytes_accessed=2 * (2 * total * width + len(weights) * (width + total) * hidden),
            transcendentals=0,
        ),
        name=name,
    )(got, *weights)


def prepare_kernel(gate, gate_far, up, up_far, act_ref, slope_ref, silu_ref):
    g = gate[...].astype(F32) + gate_far[...].astype(F32)
    u = up[...].astype(F32) + up_far[...].astype(F32)
    sigmoid = jax.nn.sigmoid(g)
    silu = g * sigmoid
    act_ref[...] = (silu * u).astype(BF)
    slope_ref[...] = (u * sigmoid * (1.0 + g * (1.0 - sigmoid))).astype(BF)
    silu_ref[...] = silu.astype(BF)


def prepare(gate, gate_far, up, up_far):
    total, hidden = gate.shape
    block = pl.BlockSpec((PEERS * CAP, hidden), lambda i: (i, 0))
    return pl.pallas_call(
        prepare_kernel,
        grid=(total // (PEERS * CAP),),
        out_shape=[jax.ShapeDtypeStruct((total, hidden), BF)] * 3,
        in_specs=[block] * 4,
        out_specs=[block] * 3,
        compiler_params=pltpu.CompilerParams(vmem_limit_bytes=VMEM),
        cost_estimate=pl.CostEstimate(
            flops=12 * total * hidden, bytes_accessed=14 * total * hidden, transcendentals=total * hidden
        ),
        name="prepare",
    )(gate, gate_far, up, up_far)


def pair_kernel(act, slope, silu, back, back_far, gate_t, up_t, out_ref, gg_ref, ug_ref):
    peers = out_ref.shape[0]
    main, total = peers * MAIN, peers * CAP
    b = back[...].astype(F32) + back_far[...].astype(F32)
    gg_ref[...] = (b * slope[...].astype(F32)).astype(BF)
    ug_ref[...] = (b * silu[...].astype(F32)).astype(BF)
    prob_grad = jnp.sum(act[...].astype(F32) * b, axis=1, keepdims=True)
    y = (dot(gg_ref[...], gate_t[...]) + dot(ug_ref[...], up_t[...])).astype(BF)
    tiles = y.shape[1] // LANE
    groups = tiles // 8
    store_main(out_ref, y[:main])
    extra = jnp.concatenate(
        [
            jnp.concatenate([y[main:, (g * 8 + c) * LANE : (g * 8 + c + 1) * LANE] for g in range(groups)], axis=1)
            for c in range(8)
        ],
        axis=0,
    )
    store_extra(out_ref, dot(extra_order(peers, True), extra).astype(BF), tiles * MAIN)
    row, lane = iota((total, LANE), 0), iota((total, LANE), 1)
    slot = jnp.where(row < main, row % MAIN, MAIN + row % EXTRA)
    by_lane = jnp.where(lane == slot, prob_grad, 0.0).astype(BF)
    peer, of = iota((peers, total), 0), iota((peers, total), 1)
    owner = jnp.where(of < main, of // MAIN, (of - main) // EXTRA)
    slots = dot(jnp.where(peer == owner, 1.0, 0.0).astype(BF), by_lane)
    out_ref[:, tiles * CAP :, :] = by_slot(slots).astype(BF).reshape(peers, MAIN, LANE)


def pair(act, slope, silu, back, back_far, gate_t, up_t):
    total, hidden = act.shape
    width = gate_t.shape[1]
    experts = total // CAP
    rows = width // LANE * CAP + MAIN
    block = pl.BlockSpec((PEERS * CAP, hidden), lambda i: (i, 0))
    whole = pl.BlockSpec(memory_space=pltpu.VMEM)
    return pl.pallas_call(
        pair_kernel,
        grid=(experts // PEERS,),
        out_shape=[jax.ShapeDtypeStruct((experts, rows, LANE), BF)]
        + [jax.ShapeDtypeStruct((total, hidden), BF)] * 2,
        in_specs=[block] * 5 + [whole] * 2,
        out_specs=[pl.BlockSpec((PEERS, rows, LANE), lambda i: (i, 0, 0))] + [block] * 2,
        compiler_params=pltpu.CompilerParams(vmem_limit_bytes=VMEM),
        cost_estimate=pl.CostEstimate(
            flops=4 * total * width * hidden,
            bytes_accessed=2 * (total * width + 7 * total * hidden + 2 * width * hidden),
            transcendentals=0,
        ),
        name="pair_grad",
    )(act, slope, silu, back, back_far, gate_t, up_t)


def combine_kernel(ids_ref, probs_ref, in_ref, slots_ref, out_ref, probs_out_ref, rank_ref, rows_ref, total_ref):
    step = pl.program_id(0)
    experts, tokens = rank_ref.shape
    peers = in_ref.shape[0]

    @pl.when(step == 0)
    def _():
        rank_ref[...] = expert_ranks(ids_ref[...], experts)
        total_ref[...] = jnp.zeros_like(total_ref)

    unpack(in_ref, rows_ref)
    some = rank_ref[pl.ds(pl.multiple_of(step * peers, peers), peers), :]
    rank = by_slot(some)
    main = jnp.where(rank == (iota(rank.shape, 0) % MAIN).astype(F32), 1.0, 0.0)
    rank = by_slot(some, 8)
    extra = jnp.where(rank == (MAIN + iota(rank.shape, 0) % 8).astype(F32), 1.0, 0.0)
    shape = (peers * EXTRA, peers * 8)
    keep = jnp.where(iota(shape, 1) == iota(shape, 0) // EXTRA * 8 + iota(shape, 0) % EXTRA, 1.0, 0.0)
    extra = dot(keep.astype(BF), extra.astype(BF))
    which = jnp.concatenate([main, extra], axis=0).astype(BF)
    total_ref[...] += lax.dot_general(which, rows_ref[...], (((0,), (0,)), ((), ())), preferred_element_type=F32)

    @pl.when(step == pl.num_programs(0) - 1)
    def _():
        out_ref[...] = total_ref[...].astype(BF)
        slots = slots_ref[:, 0, :].astype(F32)
        rank = rank_ref[...]
        found = jnp.zeros((experts, tokens), F32)
        for s in range(CAP):
            found = found + jnp.where(rank == float(s), slots[:, s : s + 1], 0.0)
        ids = ids_ref[...]
        expert = iota((experts, tokens), 0)
        grads = [
            jnp.sum(jnp.where(ids[k : k + 1] == expert, found, 0.0), axis=0, keepdims=True)
            for k in range(ids.shape[0])
        ]
        probs_out_ref[...] = (jnp.concatenate(grads, axis=0) / probs_ref[...].astype(F32)).astype(BF)


def combine(ids, probs, got):
    experts, rows, _ = got.shape
    tiles = (rows - MAIN) // CAP
    top, tokens = ids.shape
    width = tiles * LANE
    small = pl.BlockSpec(ids.shape, lambda i: (0, 0))
    return pl.pallas_call(
        combine_kernel,
        grid=(experts // SUM_PEERS,),
        out_shape=[jax.ShapeDtypeStruct((tokens, width), BF), jax.ShapeDtypeStruct((top, tokens), BF)],
        in_specs=[
            small,
            small,
            pl.BlockSpec((SUM_PEERS, rows, LANE), lambda i: (i, 0, 0)),
            pl.BlockSpec((experts, MAIN, LANE), lambda i: (0, tiles * CAP // MAIN, 0)),
        ],
        out_specs=[pl.BlockSpec((tokens, width), lambda i: (0, 0)), small],
        scratch_shapes=[
            pltpu.VMEM((experts, tokens), F32),
            pltpu.VMEM((SUM_PEERS * CAP, width), BF),
            pltpu.VMEM((tokens, width), F32),
        ],
        compiler_params=pltpu.CompilerParams(vmem_limit_bytes=VMEM),
        cost_estimate=pl.CostEstimate(
            flops=2 * experts * CAP * tokens * width, bytes_accessed=2 * experts * rows * LANE, transcendentals=0
        ),
        name="combine",
    )(ids, probs, got, got)


def exchange(x):
    return lax.all_to_all(x, ("ctx", "tp"), split_axis=0, concat_axis=0, tiled=True)


def other_core(x):
    return lax.ppermute(x, "dp", [(0, 1), (1, 0)])


def contract_rows(left, right):
    return lax.dot_general(left, right, (((0,), (0,)), ((), ())), preferred_element_type=F32).astype(BF)


def per_device(tokens, cotangent, probs, expert_ids, gate_weight, up_weight, down_weight):
    experts = lax.axis_size("ctx") * lax.axis_size("tp")
    gate_mat, up_mat, down_mat = gate_weight[0], up_weight[0], down_weight[0]
    ids, weights = expert_ids.T, probs.T
    got_tokens = exchange(pack(False, ids, weights, tokens, experts))
    got_cot = exchange(pack(True, ids, weights, cotangent, experts))
    rows, gate, up = project("gate_up", got_tokens, (gate_mat, up_mat))
    act, slope, silu = prepare(gate, other_core(gate), up, other_core(up))
    got_cot, gate_t, up_t, down_t, act, slope, silu = lax.optimization_barrier(
        (got_cot, gate_mat.T, up_mat.T, down_mat.T, act, slope, silu)
    )
    cot_rows, back = project("back", got_cot, (down_t,))
    sent, gate_grad, up_grad = pair(act, slope, silu, back, other_core(back), gate_t, up_t)
    got_pairs = exchange(sent)
    grad_down = contract_rows(act, cot_rows)
    grad_gate = contract_rows(rows, gate_grad)
    grad_up = contract_rows(rows, up_grad)
    grad_tokens, grad_probs = combine(ids, weights, got_pairs)
    return (grad_tokens, grad_probs.T, grad_gate[None], grad_up[None], grad_down[None])


def solution(mesh):
    return jax.shard_map(
        per_device,
        mesh=mesh,
        in_specs=(
            P(("ctx", "tp"), "dp"),
            P(("ctx", "tp"), "dp"),
            P(("ctx", "tp"), None),
            P(("ctx", "tp"), None),
            P(("ctx", "tp"), "dp", None),
            P(("ctx", "tp"), "dp", None),
            P(("ctx", "tp"), None, "dp"),
        ),
        out_specs=(
            P(("ctx", "tp"), "dp"),
            P(("ctx", "tp"), None),
            P(("ctx", "tp"), "dp", None),
            P(("ctx", "tp"), "dp", None),
            P(("ctx", "tp"), None, "dp"),
        ),
        check_vma=False,
    )
```

```python
import functools

import jax
import jax.numpy as jnp
from jax import lax
from jax.experimental import pallas as pl
from jax.experimental.pallas import tpu as pltpu
from jax.sharding import PartitionSpec as P

BF = jnp.bfloat16
F32 = jnp.float32
LANE = 128
HALF = 8
EXTRA = 2
CAP = 2 * HALF + EXTRA
FIRST = HALF + EXTRA
TILE = 16
GROUP = 16
PEERS = 32
SUM_PEERS = 16
VMEM = 60 * 2**20


def iota(shape, dim):
    return lax.broadcasted_iota(jnp.int32, shape, dim)


def dot(a, b):
    return jnp.dot(a, b, preferred_element_type=F32)


def expert_ranks(ids, experts):
    top, tokens = ids.shape
    expert = iota((experts, tokens), 0)
    hit = jnp.zeros((experts, tokens), F32)
    for k in range(top):
        hit = hit + jnp.where(ids[k : k + 1] == expert, 1.0, 0.0)
    earlier = jnp.where(iota((tokens, tokens), 0) < iota((tokens, tokens), 1), 1.0, 0.0)
    rank = dot(hit.astype(BF), earlier.astype(BF))
    return jnp.where(hit > 0.0, rank, -1.0)


def expert_probs(ids, probs, experts):
    top, tokens = ids.shape
    expert = iota((experts, tokens), 0)
    out = jnp.zeros((experts, tokens), F32)
    for k in range(top):
        out = out + jnp.where(ids[k : k + 1] == expert, probs[k : k + 1], 0.0)
    return out


def by_slot(a, slots):
    peers, tokens = a.shape
    return jnp.broadcast_to(a[:, None, :], (peers, slots, tokens)).reshape(peers * slots, tokens)


def extra_order(pack):
    shape = (GROUP * TILE, GROUP * TILE)
    row, col = iota(shape, 0), iota(shape, 1)
    step = GROUP * EXTRA
    if pack:
        source = (row % TILE) // EXTRA * step + row // TILE * EXTRA + row % EXTRA
    else:
        source = (row % step) // EXTRA * TILE + row // step * EXTRA + row % EXTRA
    return jnp.where(col == source, 1.0, 0.0).astype(BF)


def store_half(out_ref, start, values):
    for c in range(0, values.shape[1] // LANE, 2):
        pair = [values[:, k * LANE : (k + 1) * LANE].reshape(-1, HALF, LANE) for k in (c, c + 1)]
        at = start + c * HALF
        out_ref[:, at : at + TILE, :] = jnp.concatenate(pair, axis=1).astype(BF)


def store_extra(out_ref, start, values):
    for g in range(values.shape[1] // LANE):
        at = start + g * TILE
        out_ref[:, at : at + TILE, :] = values[:, g * LANE : (g + 1) * LANE].reshape(-1, TILE, LANE)


def order_extra(out_ref, start, values):
    groups = values.shape[1] // LANE // 8
    order = extra_order(True)
    step = GROUP * EXTRA
    parts = []
    for p in range(values.shape[0] // step):
        some = values[p * step : (p + 1) * step]
        columns = [
            jnp.concatenate([some[:, (g * 8 + c) * LANE : (g * 8 + c + 1) * LANE] for g in range(groups)], axis=1)
            for c in range(8)
        ]
        parts.append(dot(order, jnp.concatenate(columns, axis=0)).astype(BF))
    store_extra(out_ref, start, jnp.concatenate(parts, axis=0))


def unpack_half(in_ref, start, out_ref, first, count):
    rows = in_ref.shape[0] * HALF
    for c in range(0, count, 2):
        at = start + c * HALF
        pair = in_ref[:, at : at + TILE, :].astype(F32)
        for k in range(2):
            column = first + c + k
            out_ref[:rows, column * LANE : (column + 1) * LANE] = (
                pair[:, k * HALF : (k + 1) * HALF, :].reshape(rows, LANE).astype(BF)
            )


def unpack_extra(in_ref, start, out_ref, base):
    groups = out_ref.shape[1] // LANE // 8
    order = extra_order(False)
    step = GROUP * EXTRA
    for p in range(in_ref.shape[0] // GROUP):
        some = in_ref.at[p * GROUP : (p + 1) * GROUP]
        values = jnp.concatenate(
            [some[:, start + g * TILE : start + (g + 1) * TILE, :].reshape(-1, LANE) for g in range(groups)], axis=1
        )
        ordered = dot(order, values).astype(BF)
        for g in range(groups):
            for c in range(8):
                at = (g * 8 + c) * LANE
                out_ref[base + p * step : base + (p + 1) * step, at : at + LANE] = ordered[
                    c * step : (c + 1) * step, g * LANE : (g + 1) * LANE
                ]


def half_rows(rank, value, start):
    rank = by_slot(rank, HALF)
    hit = rank == (start + iota(rank.shape, 0) % HALF).astype(F32)
    return jnp.where(hit, 1.0 if value is None else by_slot(value, HALF), 0.0).astype(BF)


def extra_rows(rank, value):
    rank = by_slot(rank, TILE)
    row = iota(rank.shape, 0)
    hit = rank == (2 * HALF + row % EXTRA).astype(F32)
    extra = jnp.where(hit, 1.0 if value is None else by_slot(value, TILE), 0.0)
    column = (row % TILE) // EXTRA
    return jnp.concatenate([jnp.where(column == c, extra, 0.0).astype(BF) for c in range(8)], axis=1)


def stack_columns(x_ref, side_ref):
    tokens, width = x_ref.shape
    groups = width // LANE // 8
    for c in range(8):
        for g in range(groups):
            at = (g * 8 + c) * LANE
            side_ref[c * tokens : (c + 1) * tokens, g * LANE : (g + 1) * LANE] = x_ref[:, at : at + LANE]


def pack_first_kernel(ids_ref, probs_ref, x_ref, cot_ref, out_ref, rank_ref, prob_ref, side_ref, cot_side_ref):
    step = pl.program_id(0)
    experts = rank_ref.shape[0]
    half = x_ref.shape[1] // LANE * HALF
    part = x_ref.shape[1] // LANE * FIRST

    @pl.when(step == 0)
    def _():
        rank_ref[...] = expert_ranks(ids_ref[...], experts)
        prob_ref[...] = expert_probs(ids_ref[...], probs_ref[...].astype(F32), experts)
        stack_columns(x_ref, side_ref)
        stack_columns(cot_ref, cot_side_ref)

    peers = pl.ds(pl.multiple_of(step * PEERS, PEERS), PEERS)
    rank, prob = rank_ref[peers, :], prob_ref[peers, :]
    store_half(out_ref, 0, dot(half_rows(rank, None, 0), x_ref[...]))
    store_extra(out_ref, half, dot(extra_rows(rank, None), side_ref[...]).astype(BF))
    store_half(out_ref, part, dot(half_rows(rank, prob, 0), cot_ref[...]))
    store_extra(out_ref, part + half, dot(extra_rows(rank, prob), cot_side_ref[...]).astype(BF))
    store_half(out_ref, 2 * part, dot(half_rows(rank, None, HALF), x_ref[...]))


def pack_second_kernel(ids_ref, probs_ref, cot_ref, out_ref, rank_ref, prob_ref):
    step = pl.program_id(0)
    experts = rank_ref.shape[0]

    @pl.when(step == 0)
    def _():
        rank_ref[...] = expert_ranks(ids_ref[...], experts)
        prob_ref[...] = expert_probs(ids_ref[...], probs_ref[...].astype(F32), experts)

    peers = pl.ds(pl.multiple_of(step * PEERS, PEERS), PEERS)
    store_half(out_ref, 0, dot(half_rows(rank_ref[peers, :], prob_ref[peers, :], HALF), cot_ref[...]))


def pack(name, kernel, slots, sides, ids, probs, values, experts):
    tokens, width = values[0].shape
    rows = width // LANE * slots
    return pl.pallas_call(
        kernel,
        grid=(experts // PEERS,),
        out_shape=jax.ShapeDtypeStruct((experts, rows, LANE), BF),
        in_specs=[pl.BlockSpec(a.shape, lambda i: (0, 0)) for a in (ids, probs, *values)],
        out_specs=pl.BlockSpec((PEERS, rows, LANE), lambda i: (i, 0, 0)),
        scratch_shapes=[pltpu.VMEM((experts, tokens), F32)] * 2 + [pltpu.VMEM((8 * tokens, width // 8), BF)] * sides,
        compiler_params=pltpu.CompilerParams(vmem_limit_bytes=VMEM),
        cost_estimate=pl.CostEstimate(
            flops=4 * experts * slots * tokens * width, bytes_accessed=2 * experts * rows * LANE, transcendentals=0
        ),
        name=name,
    )(ids, probs, *values)


def project_kernel(count, extra, *refs):
    ins, refs = refs[: len(refs) - 2 * count - 1], refs[len(refs) - 2 * count - 1 :]
    weights, rows_ref, outs = refs[:count], refs[count], refs[count + 1 :]
    peers = ins[0].shape[0]
    tiles = rows_ref.shape[1] // LANE
    for n, in_ref in enumerate(ins):
        unpack_half(in_ref, 0, rows_ref, n * tiles // len(ins), tiles // len(ins))
    if extra:
        unpack_extra(ins[0], tiles * HALF, rows_ref, peers * HALF)
    for weight, out in zip(weights, outs):
        out[...] = dot(rows_ref[...], weight[...]).astype(BF)


def project(name, got, parts, slots, weights):
    experts = got.shape[0]
    width, hidden = weights[0].shape
    total, rows = experts * slots, PEERS * slots
    return pl.pallas_call(
        functools.partial(project_kernel, len(weights), slots == FIRST),
        grid=(experts // PEERS,),
        out_shape=[jax.ShapeDtypeStruct((total, width), BF)]
        + [jax.ShapeDtypeStruct((total, hidden), BF) for _ in weights],
        in_specs=[pl.BlockSpec((PEERS, size, LANE), lambda i, at=at: (i, at, 0)) for size, at in parts]
        + [pl.BlockSpec(w.shape, lambda i: (0, 0)) for w in weights],
        out_specs=[pl.BlockSpec((rows, width), lambda i: (i, 0))]
        + [pl.BlockSpec((rows, hidden), lambda i: (i, 0)) for _ in weights],
        compiler_params=pltpu.CompilerParams(vmem_limit_bytes=VMEM),
        cost_estimate=pl.CostEstimate(
            flops=2 * total * width * hidden * len(weights),
            bytes_accessed=2 * (2 * total * width + len(weights) * (width + total) * hidden),
            transcendentals=0,
        ),
        name=name,
    )(*[got] * len(parts), *weights)


def prepare_kernel(gate, gate_far, up, up_far, act_ref, slope_ref, silu_ref):
    g = gate[...].astype(F32) + gate_far[...].astype(F32)
    u = up[...].astype(F32) + up_far[...].astype(F32)
    sigmoid = jax.nn.sigmoid(g)
    silu = g * sigmoid
    act_ref[...] = (silu * u).astype(BF)
    slope_ref[...] = (u * sigmoid * (1.0 + g * (1.0 - sigmoid))).astype(BF)
    silu_ref[...] = silu.astype(BF)


def prepare(name, gate, gate_far, up, up_far):
    total, hidden = gate.shape
    block = pl.BlockSpec((total // 2, hidden), lambda i: (i, 0))
    return pl.pallas_call(
        prepare_kernel,
        grid=(2,),
        out_shape=[jax.ShapeDtypeStruct((total, hidden), BF)] * 3,
        in_specs=[block] * 4,
        out_specs=[block] * 3,
        compiler_params=pltpu.CompilerParams(vmem_limit_bytes=VMEM),
        cost_estimate=pl.CostEstimate(
            flops=12 * total * hidden, bytes_accessed=14 * total * hidden, transcendentals=total * hidden
        ),
        name=name,
    )(gate, gate_far, up, up_far)


def pair_core(act, slope, silu, back, back_far, gate_t, up_t, gg_ref, ug_ref):
    b = back[...].astype(F32) + back_far[...].astype(F32)
    gg_ref[...] = (b * slope[...].astype(F32)).astype(BF)
    ug_ref[...] = (b * silu[...].astype(F32)).astype(BF)
    prob_grad = jnp.sum(act[...].astype(F32) * b, axis=1, keepdims=True)
    return dot(gg_ref[...], gate_t[...]) + dot(ug_ref[...], up_t[...]), prob_grad


def slots_of(prob_grad, peers, extra):
    total = prob_grad.shape[0]
    main = peers * HALF
    row, lane = iota((total, LANE), 0), iota((total, LANE), 1)
    peer, of = iota((peers, total), 0), iota((peers, total), 1)
    slot, owner = row % HALF, of // HALF
    if extra:
        slot = jnp.where(row < main, slot, 2 * HALF + row % EXTRA)
        owner = jnp.where(of < main, owner, (of - main) // EXTRA)
    else:
        slot = slot + HALF
    by_lane = jnp.where(lane == slot, prob_grad, 0.0).astype(BF)
    return dot(jnp.where(peer == owner, 1.0, 0.0).astype(BF), by_lane)


def pair_first_kernel(act, slope, silu, back, back_far, gate_t, up_t, out_ref, gg_ref, ug_ref, slots_ref):
    y, prob_grad = pair_core(act, slope, silu, back, back_far, gate_t, up_t, gg_ref, ug_ref)
    half = y.shape[1] // LANE * HALF
    start = half + TILE
    main = PEERS * HALF
    store_half(out_ref, start, y[:main])
    order_extra(out_ref, start + half, y[main:].astype(BF))
    slots_ref[...] = slots_of(prob_grad, PEERS, True)


def pair_second_kernel(act, slope, silu, back, back_far, gate_t, up_t, slots, sent, out_ref, gg_ref, ug_ref):
    y, prob_grad = pair_core(act, slope, silu, back, back_far, gate_t, up_t, gg_ref, ug_ref)
    half = y.shape[1] // LANE * HALF
    store_half(out_ref, 0, y)
    grads = slots[...] + slots_of(prob_grad, PEERS, False)
    out_ref[:, half:, :] = by_slot(grads, TILE).astype(BF).reshape(PEERS, TILE, LANE)


def pair(name, act, slope, silu, back, back_far, gate_t, up_t, slots=None, sent=None):
    total, hidden = act.shape
    width = gate_t.shape[1]
    count = FIRST if sent is None else HALF
    experts = total // count
    rows = width // LANE * CAP + TILE
    block = pl.BlockSpec((PEERS * count, hidden), lambda i: (i, 0))
    whole = pl.BlockSpec(gate_t.shape, lambda i: (0, 0))
    small = pl.BlockSpec((PEERS, LANE), lambda i: (i, 0))
    written = rows if sent is None else width // LANE * HALF + TILE
    out_shape = [jax.ShapeDtypeStruct((experts, rows, LANE), BF)] + [jax.ShapeDtypeStruct((total, hidden), BF)] * 2
    out_specs = [pl.BlockSpec((PEERS, written, LANE), lambda i: (i, 0, 0))] + [block] * 2
    in_specs = [block] * 5 + [whole] * 2
    if sent is None:
        out_shape.append(jax.ShapeDtypeStruct((experts, LANE), F32))
        out_specs.append(small)
        more, aliases = (), {}
    else:
        in_specs += [small, pl.BlockSpec(memory_space=pl.ANY)]
        more, aliases = (slots, sent), {8: 0}
    return pl.pallas_call(
        pair_first_kernel if sent is None else pair_second_kernel,
        grid=(experts // PEERS,),
        out_shape=out_shape,
        in_specs=in_specs,
        out_specs=out_specs,
        input_output_aliases=aliases,
        compiler_params=pltpu.CompilerParams(vmem_limit_bytes=VMEM),
        cost_estimate=pl.CostEstimate(
            flops=4 * total * width * hidden,
            bytes_accessed=2 * (total * width + 7 * total * hidden + 2 * width * hidden),
            transcendentals=0,
        ),
        name=name,
    )(act, slope, silu, back, back_far, gate_t, up_t, *more)


def combine_kernel(ids_ref, probs_ref, in_ref, slots_ref, out_ref, probs_out_ref, rank_ref, rows_ref, total_ref):
    step = pl.program_id(0)
    experts, tokens = rank_ref.shape
    peers, tiles = in_ref.shape[0], out_ref.shape[1] // LANE
    half = tiles * HALF

    @pl.when(step == 0)
    def _():
        rank_ref[...] = expert_ranks(ids_ref[...], experts)
        total_ref[...] = jnp.zeros_like(total_ref)

    rows_first, rows_second = rows_ref.at[: peers * FIRST], rows_ref.at[peers * FIRST :]
    unpack_half(in_ref, 0, rows_second, 0, tiles)
    unpack_half(in_ref, half + TILE, rows_first, 0, tiles)
    unpack_extra(in_ref, 2 * half + TILE, rows_first, peers * HALF)
    rank = rank_ref[pl.ds(pl.multiple_of(step * peers, peers), peers), :]
    extra = by_slot(rank, 8)
    extra = jnp.where(extra == (2 * HALF + iota(extra.shape, 0) % 8).astype(F32), 1.0, 0.0).astype(BF)
    shape = (peers * EXTRA, peers * 8)
    keep = jnp.where(iota(shape, 1) == iota(shape, 0) // EXTRA * 8 + iota(shape, 0) % EXTRA, 1.0, 0.0).astype(BF)
    which = jnp.concatenate(
        [half_rows(rank, None, 0), dot(keep, extra).astype(BF), half_rows(rank, None, HALF)], axis=0
    )
    total_ref[...] += lax.dot_general(which, rows_ref[...], (((0,), (0,)), ((), ())), preferred_element_type=F32)

    @pl.when(step == pl.num_programs(0) - 1)
    def _():
        out_ref[...] = total_ref[...].astype(BF)
        slots = slots_ref[:, 0, :].astype(F32)
        rank = rank_ref[...]
        found = jnp.zeros((experts, tokens), F32)
        for s in range(CAP):
            found = found + jnp.where(rank == float(s), slots[:, s : s + 1], 0.0)
        ids = ids_ref[...]
        expert = iota((experts, tokens), 0)
        grads = [
            jnp.sum(jnp.where(ids[k : k + 1] == expert, found, 0.0), axis=0, keepdims=True)
            for k in range(ids.shape[0])
        ]
        probs_out_ref[...] = (jnp.concatenate(grads, axis=0) / probs_ref[...].astype(F32)).astype(BF)


def combine(ids, probs, got):
    experts, rows, _ = got.shape
    tiles = (rows - TILE) // CAP
    top, tokens = ids.shape
    width = tiles * LANE
    small = pl.BlockSpec(ids.shape, lambda i: (0, 0))
    return pl.pallas_call(
        combine_kernel,
        grid=(experts // SUM_PEERS,),
        out_shape=[jax.ShapeDtypeStruct((tokens, width), BF), jax.ShapeDtypeStruct((top, tokens), BF)],
        in_specs=[
            small,
            small,
            pl.BlockSpec((SUM_PEERS, rows, LANE), lambda i: (i, 0, 0)),
            pl.BlockSpec((experts, TILE, LANE), lambda i: (0, tiles * HALF // TILE, 0)),
        ],
        out_specs=[pl.BlockSpec((tokens, width), lambda i: (0, 0)), small],
        scratch_shapes=[
            pltpu.VMEM((experts, tokens), F32),
            pltpu.VMEM((SUM_PEERS * CAP, width), BF),
            pltpu.VMEM((tokens, width), F32),
        ],
        compiler_params=pltpu.CompilerParams(vmem_limit_bytes=VMEM),
        cost_estimate=pl.CostEstimate(
            flops=2 * experts * CAP * tokens * width, bytes_accessed=2 * experts * rows * LANE, transcendentals=0
        ),
        name="combine",
    )(ids, probs, got, got)


def exchange(x):
    return lax.all_to_all(x, ("ctx", "tp"), split_axis=0, concat_axis=0, tiled=True)


def other_core(x):
    return lax.ppermute(x, "dp", [(0, 1), (1, 0)])


def contract_rows(left, right):
    return lax.dot_general(left, right, (((0,), (0,)), ((), ())), preferred_element_type=F32).astype(BF)


def per_device(tokens, cotangent, probs, expert_ids, gate_weight, up_weight, down_weight):
    experts = lax.axis_size("ctx") * lax.axis_size("tp")
    gate_mat, up_mat, down_mat = gate_weight[0], up_weight[0], down_weight[0]
    ids, weights = expert_ids.T, probs.T
    tiles = tokens.shape[1] // LANE
    first, second = tiles * FIRST, tiles * HALF
    got = exchange(
        pack("pack_first", pack_first_kernel, 2 * FIRST + HALF, 2, ids, weights, (tokens, cotangent), experts)
    )
    got_b = exchange(pack("pack_second", pack_second_kernel, HALF, 0, ids, weights, (cotangent,), experts))
    got, gate_t, up_t, down_t = lax.optimization_barrier((got, gate_mat.T, up_mat.T, down_mat.T))
    rows_a, gate_a, up_a = project("gate_up_a", got, [(first, 0)], FIRST, (gate_mat, up_mat))
    cot_a, back_a = project("back_a", got, [(first, 1)], FIRST, (down_t,))
    at = 2 * first // (second // 2)
    rows_b, gate_b, up_b = project(
        "gate_up_b", got, [(second // 2, at), (second // 2, at + 1)], HALF, (gate_mat, up_mat)
    )
    act_a, slope_a, silu_a = prepare("prepare_a", gate_a, other_core(gate_a), up_a, other_core(up_a))
    act_b, slope_b, silu_b = prepare("prepare_b", gate_b, other_core(gate_b), up_b, other_core(up_b))
    sent, gate_grad_a, up_grad_a, slots = pair(
        "pair_a", act_a, slope_a, silu_a, back_a, other_core(back_a), gate_t, up_t
    )
    got_b, sent, slots, act_b, slope_b, silu_b = lax.optimization_barrier((got_b, sent, slots, act_b, slope_b, silu_b))
    cot_b, back_b = project("back_b", got_b, [(second, 0)], HALF, (down_t,))
    sent, gate_grad_b, up_grad_b = pair(
        "pair_b", act_b, slope_b, silu_b, back_b, other_core(back_b), gate_t, up_t, slots, sent
    )
    got_pairs = exchange(sent)
    rows, cot_rows = jnp.concatenate([rows_a, rows_b]), jnp.concatenate([cot_a, cot_b])
    grad_down = contract_rows(jnp.concatenate([act_a, act_b]), cot_rows)
    grad_gate = contract_rows(rows, jnp.concatenate([gate_grad_a, gate_grad_b]))
    grad_up = contract_rows(rows, jnp.concatenate([up_grad_a, up_grad_b]))
    grad_tokens, grad_probs = combine(ids, weights, got_pairs)
    return (grad_tokens, grad_probs.T, grad_gate[None], grad_up[None], grad_down[None])


def solution(mesh):
    return jax.shard_map(
        per_device,
        mesh=mesh,
        in_specs=(
            P(("ctx", "tp"), "dp"),
            P(("ctx", "tp"), "dp"),
            P(("ctx", "tp"), None),
            P(("ctx", "tp"), None),
            P(("ctx", "tp"), "dp", None),
            P(("ctx", "tp"), "dp", None),
            P(("ctx", "tp"), None, "dp"),
        ),
        out_specs=(
            P(("ctx", "tp"), "dp"),
            P(("ctx", "tp"), None),
            P(("ctx", "tp"), "dp", None),
            P(("ctx", "tp"), "dp", None),
            P(("ctx", "tp"), None, "dp"),
        ),
        check_vma=False,
    )
```

```python
import functools

import jax
import jax.numpy as jnp
from jax import lax
from jax.experimental import pallas as pl
from jax.experimental.pallas import tpu as pltpu
from jax.sharding import PartitionSpec as P

BF = jnp.bfloat16
F32 = jnp.float32
LANE = 128
HALF = 8
EXTRA = 2
CAP = 2 * HALF + EXTRA
FIRST = HALF + EXTRA
TILE = 16
GROUP = 16
PEERS = 32
VMEM = 60 * 2**20


def iota(shape, dim):
    return lax.broadcasted_iota(jnp.int32, shape, dim)


def dot(a, b):
    return jnp.dot(a, b, preferred_element_type=F32)


def expert_ranks(ids, experts):
    top, tokens = ids.shape
    expert = iota((experts, tokens), 0)
    hit = jnp.zeros((experts, tokens), F32)
    for k in range(top):
        hit = hit + jnp.where(ids[k : k + 1] == expert, 1.0, 0.0)
    earlier = jnp.where(iota((tokens, tokens), 0) < iota((tokens, tokens), 1), 1.0, 0.0)
    rank = dot(hit.astype(BF), earlier.astype(BF))
    return jnp.where(hit > 0.0, rank, -1.0)


def expert_probs(ids, probs, experts):
    top, tokens = ids.shape
    expert = iota((experts, tokens), 0)
    out = jnp.zeros((experts, tokens), F32)
    for k in range(top):
        out = out + jnp.where(ids[k : k + 1] == expert, probs[k : k + 1], 0.0)
    return out


def by_slot(a, slots):
    peers, tokens = a.shape
    return jnp.broadcast_to(a[:, None, :], (peers, slots, tokens)).reshape(peers * slots, tokens)


def extra_order(pack):
    shape = (GROUP * TILE, GROUP * TILE)
    row, col = iota(shape, 0), iota(shape, 1)
    step = GROUP * EXTRA
    if pack:
        source = (row % TILE) // EXTRA * step + row // TILE * EXTRA + row % EXTRA
    else:
        source = (row % step) // EXTRA * TILE + row // step * EXTRA + row % EXTRA
    return jnp.where(col == source, 1.0, 0.0).astype(BF)


def store_half(out_ref, start, values):
    for c in range(0, values.shape[1] // LANE, 2):
        pair = [values[:, k * LANE : (k + 1) * LANE].reshape(-1, HALF, LANE) for k in (c, c + 1)]
        at = start + c * HALF
        out_ref[:, at : at + TILE, :] = jnp.concatenate(pair, axis=1).astype(BF)


def store_extra(out_ref, start, values):
    for g in range(values.shape[1] // LANE):
        at = start + g * TILE
        out_ref[:, at : at + TILE, :] = values[:, g * LANE : (g + 1) * LANE].reshape(-1, TILE, LANE)


def order_extra(out_ref, start, values):
    groups = values.shape[1] // LANE // 8
    order = extra_order(True)
    step = GROUP * EXTRA
    parts = []
    for p in range(values.shape[0] // step):
        some = values[p * step : (p + 1) * step]
        columns = [
            jnp.concatenate([some[:, (g * 8 + c) * LANE : (g * 8 + c + 1) * LANE] for g in range(groups)], axis=1)
            for c in range(8)
        ]
        parts.append(dot(order, jnp.concatenate(columns, axis=0)).astype(BF))
    store_extra(out_ref, start, jnp.concatenate(parts, axis=0))


def unpack_half(in_ref, start, out_ref, first, count):
    rows = in_ref.shape[0] * HALF
    for c in range(0, count, 2):
        at = start + c * HALF
        pair = in_ref[:, at : at + TILE, :].astype(F32)
        for k in range(2):
            column = first + c + k
            out_ref[:rows, column * LANE : (column + 1) * LANE] = (
                pair[:, k * HALF : (k + 1) * HALF, :].reshape(rows, LANE).astype(BF)
            )


def unpack_extra(in_ref, start, out_ref, base):
    groups = out_ref.shape[1] // LANE // 8
    order = extra_order(False)
    step = GROUP * EXTRA
    for p in range(in_ref.shape[0] // GROUP):
        some = in_ref.at[p * GROUP : (p + 1) * GROUP]
        values = jnp.concatenate(
            [some[:, start + g * TILE : start + (g + 1) * TILE, :].reshape(-1, LANE) for g in range(groups)], axis=1
        )
        ordered = dot(order, values).astype(BF)
        for g in range(groups):
            for c in range(8):
                at = (g * 8 + c) * LANE
                out_ref[base + p * step : base + (p + 1) * step, at : at + LANE] = ordered[
                    c * step : (c + 1) * step, g * LANE : (g + 1) * LANE
                ]


def half_rows(rank, value, start):
    rank = by_slot(rank, HALF)
    hit = rank == (start + iota(rank.shape, 0) % HALF).astype(F32)
    return jnp.where(hit, 1.0 if value is None else by_slot(value, HALF), 0.0).astype(BF)


def extra_rows(rank, value):
    rank = by_slot(rank, TILE)
    row = iota(rank.shape, 0)
    hit = rank == (2 * HALF + row % EXTRA).astype(F32)
    extra = jnp.where(hit, 1.0 if value is None else by_slot(value, TILE), 0.0)
    column = (row % TILE) // EXTRA
    return jnp.concatenate([jnp.where(column == c, extra, 0.0).astype(BF) for c in range(8)], axis=1)


def stack_columns(x_ref, side_ref):
    tokens, width = x_ref.shape
    groups = width // LANE // 8
    for c in range(8):
        for g in range(groups):
            at = (g * 8 + c) * LANE
            side_ref[c * tokens : (c + 1) * tokens, g * LANE : (g + 1) * LANE] = x_ref[:, at : at + LANE]


def start_pack(ids_ref, probs_ref, rank_ref, prob_ref):
    experts = rank_ref.shape[0]
    rank_ref[...] = expert_ranks(ids_ref[...], experts)
    prob_ref[...] = expert_probs(ids_ref[...], probs_ref[...].astype(F32), experts)


def pack_first_kernel(ids_ref, probs_ref, x_ref, cot_ref, out_ref, rank_ref, prob_ref, side_ref, cot_side_ref):
    step = pl.program_id(0)
    half = x_ref.shape[1] // LANE * HALF
    part = x_ref.shape[1] // LANE * FIRST

    @pl.when(step == 0)
    def _():
        start_pack(ids_ref, probs_ref, rank_ref, prob_ref)
        stack_columns(x_ref, side_ref)
        stack_columns(cot_ref, cot_side_ref)

    peers = pl.ds(pl.multiple_of(step * PEERS, PEERS), PEERS)
    rank, prob = rank_ref[peers, :], prob_ref[peers, :]
    store_half(out_ref, 0, dot(half_rows(rank, None, 0), x_ref[...]))
    store_extra(out_ref, half, dot(extra_rows(rank, None), side_ref[...]).astype(BF))
    store_half(out_ref, part, dot(half_rows(rank, prob, 0), cot_ref[...]))
    store_extra(out_ref, part + half, dot(extra_rows(rank, prob), cot_side_ref[...]).astype(BF))


def pack_second_kernel(ids_ref, probs_ref, x_ref, cot_ref, out_ref, rank_ref, prob_ref):
    step = pl.program_id(0)
    half = x_ref.shape[1] // LANE * HALF

    @pl.when(step == 0)
    def _():
        start_pack(ids_ref, probs_ref, rank_ref, prob_ref)

    peers = pl.ds(pl.multiple_of(step * PEERS, PEERS), PEERS)
    rank, prob = rank_ref[peers, :], prob_ref[peers, :]
    store_half(out_ref, 0, dot(half_rows(rank, None, HALF), x_ref[...]))
    store_half(out_ref, half, dot(half_rows(rank, prob, HALF), cot_ref[...]))


def pack(name, kernel, slots, sides, ids, probs, values, experts):
    tokens, width = values[0].shape
    rows = width // LANE * slots
    return pl.pallas_call(
        kernel,
        grid=(experts // PEERS,),
        out_shape=jax.ShapeDtypeStruct((experts, rows, LANE), BF),
        in_specs=[pl.BlockSpec(a.shape, lambda i: (0, 0)) for a in (ids, probs, *values)],
        out_specs=pl.BlockSpec((PEERS, rows, LANE), lambda i: (i, 0, 0)),
        scratch_shapes=[pltpu.VMEM((experts, tokens), F32)] * 2 + [pltpu.VMEM((8 * tokens, width // 8), BF)] * sides,
        compiler_params=pltpu.CompilerParams(vmem_limit_bytes=VMEM),
        cost_estimate=pl.CostEstimate(
            flops=4 * experts * slots * tokens * width, bytes_accessed=2 * experts * rows * LANE, transcendentals=0
        ),
        name=name,
    )(ids, probs, *values)


def project_kernel(extra, x_in, cot_in, gate_w, up_w, down_w, x_ref, cot_ref, gate_ref, up_ref, back_ref):
    peers = x_in.shape[0]
    tiles = x_ref.shape[1] // LANE
    for in_ref, rows_ref in ((x_in, x_ref), (cot_in, cot_ref)):
        unpack_half(in_ref, 0, rows_ref, 0, tiles)
        if extra:
            unpack_extra(in_ref, tiles * HALF, rows_ref, peers * HALF)
    gate_ref[...] = dot(x_ref[...], gate_w[...]).astype(BF)
    up_ref[...] = dot(x_ref[...], up_w[...]).astype(BF)
    back_ref[...] = dot(cot_ref[...], down_w[...]).astype(BF)


def project(name, got, weights):
    experts, both, _ = got.shape
    width, hidden = weights[0].shape
    part = both // 2
    slots = part * LANE // width
    total, rows = experts * slots, PEERS * slots
    return pl.pallas_call(
        functools.partial(project_kernel, slots == FIRST),
        grid=(experts // PEERS,),
        out_shape=[jax.ShapeDtypeStruct((total, width), BF)] * 2 + [jax.ShapeDtypeStruct((total, hidden), BF)] * 3,
        in_specs=[pl.BlockSpec((PEERS, part, LANE), lambda i, at=at: (i, at, 0)) for at in range(2)]
        + [pl.BlockSpec(w.shape, lambda i: (0, 0)) for w in weights],
        out_specs=[pl.BlockSpec((rows, width), lambda i: (i, 0))] * 2
        + [pl.BlockSpec((rows, hidden), lambda i: (i, 0))] * 3,
        compiler_params=pltpu.CompilerParams(vmem_limit_bytes=VMEM),
        cost_estimate=pl.CostEstimate(
            flops=6 * total * width * hidden,
            bytes_accessed=2 * (4 * total * width + 3 * (width + total) * hidden),
            transcendentals=0,
        ),
        name=name,
    )(got, got, *weights)


def slots_of(prob_grad, peers, extra):
    total = prob_grad.shape[0]
    main = peers * HALF
    row, lane = iota((total, LANE), 0), iota((total, LANE), 1)
    peer, of = iota((peers, total), 0), iota((peers, total), 1)
    slot, owner = row % HALF, of // HALF
    if extra:
        slot = jnp.where(row < main, slot, HALF + row % EXTRA)
        owner = jnp.where(of < main, owner, (of - main) // EXTRA)
    by_lane = jnp.where(lane == slot, prob_grad, 0.0).astype(BF)
    return dot(jnp.where(peer == owner, 1.0, 0.0).astype(BF), by_lane)


def pair_kernel(extra, gate, gate_far, up, up_far, back, back_far, gate_t, up_t, out_ref, act_ref, gg_ref, ug_ref):
    g = gate[...].astype(F32) + gate_far[...].astype(F32)
    u = up[...].astype(F32) + up_far[...].astype(F32)
    b = back[...].astype(F32) + back_far[...].astype(F32)
    sigmoid = jax.nn.sigmoid(g)
    silu = g * sigmoid
    act = silu * u
    act_ref[...] = act.astype(BF)
    gg_ref[...] = (b * u * sigmoid * (1.0 + g * (1.0 - sigmoid))).astype(BF)
    ug_ref[...] = (b * silu).astype(BF)
    prob_grad = jnp.sum(act * b, axis=1, keepdims=True)
    y = dot(gg_ref[...], gate_t[...]) + dot(ug_ref[...], up_t[...])
    half = y.shape[1] // LANE * HALF
    main = PEERS * HALF
    store_half(out_ref, 0, y[:main])
    if extra:
        order_extra(out_ref, half, y[main:].astype(BF))
    last = out_ref.shape[1] - TILE
    grads = by_slot(slots_of(prob_grad, PEERS, extra), TILE)
    out_ref[:, last:, :] = grads.astype(BF).reshape(PEERS, TILE, LANE)


def pair(name, gate, gate_far, up, up_far, back, back_far, gate_t, up_t, experts):
    total, hidden = gate.shape
    width = gate_t.shape[1]
    slots = total // experts
    rows = width // LANE * slots + TILE
    block = pl.BlockSpec((PEERS * slots, hidden), lambda i: (i, 0))
    whole = pl.BlockSpec(gate_t.shape, lambda i: (0, 0))
    return pl.pallas_call(
        functools.partial(pair_kernel, slots == FIRST),
        grid=(experts // PEERS,),
        out_shape=[jax.ShapeDtypeStruct((experts, rows, LANE), BF)]
        + [jax.ShapeDtypeStruct((total, hidden), BF)] * 3,
        in_specs=[block] * 6 + [whole] * 2,
        out_specs=[pl.BlockSpec((PEERS, rows, LANE), lambda i: (i, 0, 0))] + [block] * 3,
        compiler_params=pltpu.CompilerParams(vmem_limit_bytes=VMEM),
        cost_estimate=pl.CostEstimate(
            flops=4 * total * width * hidden,
            bytes_accessed=2 * (total * width + 9 * total * hidden + 2 * width * hidden),
            transcendentals=total * hidden,
        ),
        name=name,
    )(gate, gate_far, up, up_far, back, back_far, gate_t, up_t)


def combine_kernel(extra, ids_ref, in_ref, slots_ref, *refs):
    if extra:
        out_ref, probs_out_ref, rank_ref, rows_ref = refs
        total_ref = out_ref
    else:
        probs_ref, before_ref, probs_before_ref, out_ref, probs_out_ref, rank_ref, rows_ref, total_ref = refs
    step = pl.program_id(0)
    experts, tokens = rank_ref.shape
    peers, tiles = in_ref.shape[0], out_ref.shape[1] // LANE
    half = tiles * HALF

    @pl.when(step == 0)
    def _():
        rank_ref[...] = expert_ranks(ids_ref[...], experts)
        total_ref[...] = jnp.zeros_like(total_ref) if extra else before_ref[...]

    unpack_half(in_ref, 0, rows_ref, 0, tiles)
    rank = rank_ref[pl.ds(pl.multiple_of(step * peers, peers), peers), :]
    which = half_rows(rank, None, 0 if extra else HALF)
    if extra:
        unpack_extra(in_ref, half, rows_ref, peers * HALF)
        some = by_slot(rank, 8)
        some = jnp.where(some == (2 * HALF + iota(some.shape, 0) % 8).astype(F32), 1.0, 0.0).astype(BF)
        shape = (peers * EXTRA, peers * 8)
        keep = iota(shape, 1) == iota(shape, 0) // EXTRA * 8 + iota(shape, 0) % EXTRA
        which = jnp.concatenate([which, dot(jnp.where(keep, 1.0, 0.0).astype(BF), some).astype(BF)], axis=0)
    total_ref[...] += lax.dot_general(which, rows_ref[...], (((0,), (0,)), ((), ())), preferred_element_type=F32)

    @pl.when(step == pl.num_programs(0) - 1)
    def _():
        slots = slots_ref[:, 0, :].astype(F32)
        rank = rank_ref[...]
        found = jnp.zeros((experts, tokens), F32)
        for lane in range(FIRST if extra else HALF):
            slot = (lane if lane < HALF else lane + HALF) if extra else lane + HALF
            found = found + jnp.where(rank == float(slot), slots[:, lane : lane + 1], 0.0)
        ids = ids_ref[...]
        expert = iota((experts, tokens), 0)
        grads = [
            jnp.sum(jnp.where(ids[k : k + 1] == expert, found, 0.0), axis=0, keepdims=True)
            for k in range(ids.shape[0])
        ]
        grads = jnp.concatenate(grads, axis=0)
        if extra:
            probs_out_ref[...] = grads
        else:
            out_ref[...] = total_ref[...].astype(BF)
            probs_out_ref[...] = ((grads + probs_before_ref[...]) / probs_ref[...].astype(F32)).astype(BF)


def combine(name, ids, got, width, before=()):
    experts, rows, _ = got.shape
    top, tokens = ids.shape
    extra = not before
    slots = FIRST if extra else HALF
    whole = lambda shape: pl.BlockSpec(shape, lambda i: (0, 0))
    kind = F32 if extra else BF
    return pl.pallas_call(
        functools.partial(combine_kernel, extra),
        grid=(experts // PEERS,),
        out_shape=[jax.ShapeDtypeStruct((tokens, width), kind), jax.ShapeDtypeStruct((top, tokens), kind)],
        in_specs=[
            whole(ids.shape),
            pl.BlockSpec((PEERS, rows, LANE), lambda i: (i, 0, 0)),
            pl.BlockSpec((experts, TILE, LANE), lambda i: (0, rows // TILE - 1, 0)),
        ]
        + [whole(a.shape) for a in before],
        out_specs=[whole((tokens, width)), whole((top, tokens))],
        scratch_shapes=[pltpu.VMEM((experts, tokens), F32), pltpu.VMEM((PEERS * slots, width), BF)]
        + ([] if extra else [pltpu.VMEM((tokens, width), F32)]),
        compiler_params=pltpu.CompilerParams(vmem_limit_bytes=VMEM),
        cost_estimate=pl.CostEstimate(
            flops=2 * experts * slots * tokens * width, bytes_accessed=2 * experts * rows * LANE, transcendentals=0
        ),
        name=name,
    )(ids, got, got, *before)


def exchange(x):
    return lax.all_to_all(x, ("ctx", "tp"), split_axis=0, concat_axis=0, tiled=True)


def other_core(x):
    return lax.ppermute(x, "dp", [(0, 1), (1, 0)])


def contract_rows(left, right):
    return lax.dot_general(left, right, (((0,), (0,)), ((), ())), preferred_element_type=F32).astype(BF)


def per_device(tokens, cotangent, probs, expert_ids, gate_weight, up_weight, down_weight):
    experts = lax.axis_size("ctx") * lax.axis_size("tp")
    gate_mat, up_mat, down_mat = gate_weight[0], up_weight[0], down_weight[0]
    ids, weights = expert_ids.T, probs.T
    values = (tokens, cotangent)
    sent_a = pack("pack_a", pack_first_kernel, 2 * FIRST, 2, ids, weights, values, experts)
    got_a = exchange(sent_a)
    sent_b, gate_t, up_t, down_t = lax.optimization_barrier(
        (
            pack("pack_b", pack_second_kernel, 2 * HALF, 0, ids, weights, values, experts),
            gate_mat.T,
            up_mat.T,
            down_mat.T,
        )
    )
    got_b = exchange(sent_b)
    mats = (gate_mat, up_mat, down_t)

    def part(name, got):
        rows, cot_rows, gate, up, back = project("project_" + name, got, mats)
        far = other_core(gate), other_core(up), other_core(back)
        sent, *grads = pair("pair_" + name, gate, far[0], up, far[1], back, far[2], gate_t, up_t, experts)
        return sent, (rows, cot_rows, *grads)

    pairs_a, kept_a = part("a", got_a)
    got_b, pairs_a = lax.optimization_barrier((got_b, pairs_a))
    back_a = exchange(pairs_a)
    pairs_b, kept_b = part("b", got_b)
    back_b = exchange(pairs_b)
    rows, cot_rows, act, gate_grad, up_grad = (jnp.concatenate(ab) for ab in zip(kept_a, kept_b))
    grad_down = contract_rows(act, cot_rows)
    grad_gate = contract_rows(rows, gate_grad)
    grad_up = contract_rows(rows, up_grad)
    width = tokens.shape[1]
    before = combine("combine_a", ids, back_a, width)
    grad_tokens, grad_probs = combine("combine_b", ids, back_b, width, (weights, *before))
    return (grad_tokens, grad_probs.T, grad_gate[None], grad_up[None], grad_down[None])


def solution(mesh):
    return jax.shard_map(
        per_device,
        mesh=mesh,
        in_specs=(
            P(("ctx", "tp"), "dp"),
            P(("ctx", "tp"), "dp"),
            P(("ctx", "tp"), None),
            P(("ctx", "tp"), None),
            P(("ctx", "tp"), "dp", None),
            P(("ctx", "tp"), "dp", None),
            P(("ctx", "tp"), None, "dp"),
        ),
        out_specs=(
            P(("ctx", "tp"), "dp"),
            P(("ctx", "tp"), None),
            P(("ctx", "tp"), "dp", None),
            P(("ctx", "tp"), "dp", None),
            P(("ctx", "tp"), None, "dp"),
        ),
        check_vma=False,
    )
```

```python
import functools

import jax
import jax.numpy as jnp
from jax import lax
from jax.experimental import pallas as pl
from jax.experimental.pallas import tpu as pltpu
from jax.sharding import PartitionSpec as P

BF = jnp.bfloat16
F32 = jnp.float32
LANE = 128
HALF = 8
EXTRA = 2
CAP = 2 * HALF + EXTRA
FIRST = HALF + EXTRA
TILE = 16
GROUP = 16
PEERS = 32
SECOND_PEERS = 16
PACK_PEERS = 32
SUM_PEERS = 64
VMEM = 60 * 2**20


def iota(shape, dim):
    return lax.broadcasted_iota(jnp.int32, shape, dim)


def dot(a, b):
    return jnp.dot(a, b, preferred_element_type=F32)


def contract(left, right):
    return lax.dot_general(left, right, (((0,), (0,)), ((), ())), preferred_element_type=F32)


def expert_ranks(ids, experts):
    top, tokens = ids.shape
    expert = iota((experts, tokens), 0)
    hit = jnp.zeros((experts, tokens), F32)
    for k in range(top):
        hit = hit + jnp.where(ids[k : k + 1] == expert, 1.0, 0.0)
    earlier = jnp.where(iota((tokens, tokens), 0) < iota((tokens, tokens), 1), 1.0, 0.0)
    rank = dot(hit.astype(BF), earlier.astype(BF))
    return jnp.where(hit > 0.0, rank, -1.0)


def expert_probs(ids, probs, experts):
    top, tokens = ids.shape
    expert = iota((experts, tokens), 0)
    out = jnp.zeros((experts, tokens), F32)
    for k in range(top):
        out = out + jnp.where(ids[k : k + 1] == expert, probs[k : k + 1], 0.0)
    return out


def by_slot(a, slots):
    peers, tokens = a.shape
    return jnp.broadcast_to(a[:, None, :], (peers, slots, tokens)).reshape(peers * slots, tokens)


def extra_order(pack):
    shape = (GROUP * TILE, GROUP * TILE)
    row, col = iota(shape, 0), iota(shape, 1)
    step = GROUP * EXTRA
    if pack:
        source = (row % TILE) // EXTRA * step + row // TILE * EXTRA + row % EXTRA
    else:
        source = (row % step) // EXTRA * TILE + row // step * EXTRA + row % EXTRA
    return jnp.where(col == source, 1.0, 0.0).astype(BF)


def store_half(out_ref, start, values):
    for c in range(0, values.shape[1] // LANE, 2):
        pair = [values[:, k * LANE : (k + 1) * LANE].reshape(-1, HALF, LANE) for k in (c, c + 1)]
        at = start + c * HALF
        out_ref[:, at : at + TILE, :] = jnp.concatenate(pair, axis=1).astype(BF)


def store_extra(out_ref, start, values):
    for g in range(values.shape[1] // LANE):
        at = start + g * TILE
        out_ref[:, at : at + TILE, :] = values[:, g * LANE : (g + 1) * LANE].reshape(-1, TILE, LANE)


def order_extra(out_ref, start, values):
    groups = values.shape[1] // LANE // 8
    order = extra_order(True)
    step = GROUP * EXTRA
    parts = []
    for p in range(values.shape[0] // step):
        some = values[p * step : (p + 1) * step]
        columns = [
            jnp.concatenate([some[:, (g * 8 + c) * LANE : (g * 8 + c + 1) * LANE] for g in range(groups)], axis=1)
            for c in range(8)
        ]
        parts.append(dot(order, jnp.concatenate(columns, axis=0)).astype(BF))
    store_extra(out_ref, start, jnp.concatenate(parts, axis=0))


def unpack_half(in_ref, start, out_ref, first, count):
    rows = in_ref.shape[0] * HALF
    for c in range(0, count, 2):
        at = start + c * HALF
        pair = in_ref[:, at : at + TILE, :].astype(F32)
        for k in range(2):
            column = first + c + k
            out_ref[:rows, column * LANE : (column + 1) * LANE] = (
                pair[:, k * HALF : (k + 1) * HALF, :].reshape(rows, LANE).astype(BF)
            )


def unpack_extra(in_ref, start, out_ref, base):
    groups = out_ref.shape[1] // LANE // 8
    order = extra_order(False)
    step = GROUP * EXTRA
    for p in range(in_ref.shape[0] // GROUP):
        some = in_ref.at[p * GROUP : (p + 1) * GROUP]
        values = jnp.concatenate(
            [some[:, start + g * TILE : start + (g + 1) * TILE, :].reshape(-1, LANE) for g in range(groups)], axis=1
        )
        ordered = dot(order, values).astype(BF)
        for g in range(groups):
            for c in range(8):
                at = (g * 8 + c) * LANE
                out_ref[base + p * step : base + (p + 1) * step, at : at + LANE] = ordered[
                    c * step : (c + 1) * step, g * LANE : (g + 1) * LANE
                ]


def half_rows(rank, value, start):
    rank = by_slot(rank, HALF)
    hit = rank == (start + iota(rank.shape, 0) % HALF).astype(F32)
    return jnp.where(hit, 1.0 if value is None else by_slot(value, HALF), 0.0).astype(BF)


def extra_rows(rank, value):
    peers = rank.shape[0]
    rank = by_slot(rank, 8)
    hit = rank == (2 * HALF + iota(rank.shape, 0) % 8).astype(F32)
    eight = jnp.where(hit, 1.0 if value is None else by_slot(value, 8), 0.0).astype(BF)
    shape = (peers * EXTRA, peers * 8)
    keep = iota(shape, 1) == iota(shape, 0) // EXTRA * 8 + iota(shape, 0) % EXTRA
    return dot(jnp.where(keep, 1.0, 0.0).astype(BF), eight).astype(BF)


def wide_extra_rows(rank, value):
    rank = by_slot(rank, TILE)
    row = iota(rank.shape, 0)
    hit = rank == (2 * HALF + row % EXTRA).astype(F32)
    extra = jnp.where(hit, 1.0 if value is None else by_slot(value, TILE), 0.0)
    column = (row % TILE) // EXTRA
    return jnp.concatenate([jnp.where(column == c, extra, 0.0).astype(BF) for c in range(8)], axis=1)


def stack_columns(x_ref, side_ref):
    tokens, width = x_ref.shape
    groups = width // LANE // 8
    for c in range(8):
        for g in range(groups):
            at = (g * 8 + c) * LANE
            side_ref[c * tokens : (c + 1) * tokens, g * LANE : (g + 1) * LANE] = x_ref[:, at : at + LANE]


def start_pack(ids_ref, probs_ref, rank_ref, prob_ref):
    experts = rank_ref.shape[0]
    rank_ref[...] = expert_ranks(ids_ref[...], experts)
    prob_ref[...] = expert_probs(ids_ref[...], probs_ref[...].astype(F32), experts)


def pack_first_kernel(ids_ref, probs_ref, x_ref, cot_ref, out_ref, rank_ref, prob_ref, side_ref, cot_side_ref):
    step = pl.program_id(0)
    half = x_ref.shape[1] // LANE * HALF
    part = x_ref.shape[1] // LANE * FIRST
    count = out_ref.shape[0]

    @pl.when(step == 0)
    def _():
        start_pack(ids_ref, probs_ref, rank_ref, prob_ref)
        stack_columns(x_ref, side_ref)
        stack_columns(cot_ref, cot_side_ref)

    peers = pl.ds(pl.multiple_of(step * count, count), count)
    rank, prob = rank_ref[peers, :], prob_ref[peers, :]
    for start, value, ref, side in ((0, None, x_ref, side_ref), (part, prob, cot_ref, cot_side_ref)):
        store_half(out_ref, start, dot(half_rows(rank, value, 0), ref[...]))
        store_extra(out_ref, start + half, dot(wide_extra_rows(rank, value), side[...]).astype(BF))


def pack_second_kernel(ids_ref, probs_ref, x_ref, cot_ref, out_ref, rank_ref, prob_ref):
    step = pl.program_id(0)
    half = x_ref.shape[1] // LANE * HALF

    @pl.when(step == 0)
    def _():
        start_pack(ids_ref, probs_ref, rank_ref, prob_ref)

    count = out_ref.shape[0]
    peers = pl.ds(pl.multiple_of(step * count, count), count)
    rank, prob = rank_ref[peers, :], prob_ref[peers, :]
    store_half(out_ref, 0, dot(half_rows(rank, None, HALF), x_ref[...]))
    store_half(out_ref, half, dot(half_rows(rank, prob, HALF), cot_ref[...]))


def pack(name, kernel, slots, sides, ids, probs, values, experts):
    tokens, width = values[0].shape
    rows = width // LANE * slots
    return pl.pallas_call(
        kernel,
        grid=(experts // PACK_PEERS,),
        out_shape=jax.ShapeDtypeStruct((experts, rows, LANE), BF),
        in_specs=[pl.BlockSpec(a.shape, lambda i: (0, 0)) for a in (ids, probs, *values)],
        out_specs=pl.BlockSpec((PACK_PEERS, rows, LANE), lambda i: (i, 0, 0)),
        scratch_shapes=[pltpu.VMEM((experts, tokens), F32)] * 2 + [pltpu.VMEM((8 * tokens, width // 8), BF)] * sides,
        compiler_params=pltpu.CompilerParams(vmem_limit_bytes=VMEM),
        cost_estimate=pl.CostEstimate(
            flops=4 * experts * slots * tokens * width, bytes_accessed=2 * experts * rows * LANE, transcendentals=0
        ),
        name=name,
    )(ids, probs, *values)


def project_kernel(extra, x_in, cot_in, gate_w, up_w, down_w, *refs):
    x_ref, cot_ref, gate_ref, up_ref, back_ref = refs[-5:]
    peers = x_in.shape[0]
    tiles = x_ref.shape[1] // LANE
    for in_ref, rows_ref in ((x_in, x_ref), (cot_in, cot_ref)):
        unpack_half(in_ref, 0, rows_ref, 0, tiles)
        if extra:
            unpack_extra(in_ref, tiles * HALF, rows_ref, peers * HALF)
    gate_ref[...] = dot(x_ref[...], gate_w[...]).astype(BF)
    up_ref[...] = dot(x_ref[...], up_w[...]).astype(BF)
    back_ref[...] = dot(cot_ref[...], down_w[...]).astype(BF)


def project(name, got, weights, kept=()):
    experts, both, _ = got.shape
    width, hidden = weights[0].shape
    part = both // 2
    slots = part * LANE // width
    peers = SECOND_PEERS if kept else PEERS
    total, rows = experts * slots, peers * slots
    first = experts * FIRST // rows if kept else 0
    whole = experts * CAP
    return pl.pallas_call(
        functools.partial(project_kernel, not kept),
        grid=(experts // peers,),
        out_shape=[jax.ShapeDtypeStruct((whole, width), BF)] * 2 + [jax.ShapeDtypeStruct((total, hidden), BF)] * 3,
        in_specs=[pl.BlockSpec((peers, part, LANE), lambda i, at=at: (i, at, 0)) for at in range(2)]
        + [pl.BlockSpec(w.shape, lambda i: (0, 0)) for w in weights]
        + [pl.BlockSpec(memory_space=pl.ANY) for _ in kept],
        out_specs=[pl.BlockSpec((rows, width), lambda i: (first + i, 0))] * 2
        + [pl.BlockSpec((rows, hidden), lambda i: (i, 0))] * 3,
        input_output_aliases={5 + k: k for k in range(len(kept))},
        compiler_params=pltpu.CompilerParams(vmem_limit_bytes=VMEM),
        cost_estimate=pl.CostEstimate(
            flops=6 * total * width * hidden,
            bytes_accessed=2 * (4 * total * width + 3 * (width + total) * hidden),
            transcendentals=0,
        ),
        name=name,
    )(got, got, *weights, *kept)


def slots_of(prob_grad, peers, extra):
    total = prob_grad.shape[0]
    main = peers * HALF
    row, lane = iota((total, LANE), 0), iota((total, LANE), 1)
    peer, of = iota((peers, total), 0), iota((peers, total), 1)
    slot, owner = row % HALF, of // HALF
    if extra:
        slot = jnp.where(row < main, slot, 2 * HALF + row % EXTRA)
        owner = jnp.where(of < main, owner, (of - main) // EXTRA)
    else:
        slot = slot + HALF
    by_lane = jnp.where(lane == slot, prob_grad, 0.0).astype(BF)
    return dot(jnp.where(peer == owner, 1.0, 0.0).astype(BF), by_lane)


def pair_kernel(extra, *refs):
    if extra:
        *refs, out_ref, act_ref, gg_ref, ug_ref, slots_out_ref = refs
    else:
        *refs, slots_ref, _, _, _, out_ref, act_ref, gg_ref, ug_ref = refs
    gate, gate_far, up, up_far, back, back_far, gate_t, up_t = refs
    g = gate[...].astype(F32) + gate_far[...].astype(F32)
    u = up[...].astype(F32) + up_far[...].astype(F32)
    b = back[...].astype(F32) + back_far[...].astype(F32)
    sigmoid = jax.nn.sigmoid(g)
    silu = g * sigmoid
    act = silu * u
    act_ref[...] = act.astype(BF)
    gg_ref[...] = (b * u * sigmoid * (1.0 + g * (1.0 - sigmoid))).astype(BF)
    ug_ref[...] = (b * silu).astype(BF)
    prob_grad = jnp.sum(act * b, axis=1, keepdims=True)
    y = dot(gg_ref[...], gate_t[...]) + dot(ug_ref[...], up_t[...])
    half = y.shape[1] // LANE * HALF
    peers = out_ref.shape[0]
    main = peers * HALF
    store_half(out_ref, 0, y[:main])
    slots = slots_of(prob_grad, peers, extra)
    if extra:
        order_extra(out_ref, half, y[main:].astype(BF))
        slots_out_ref[...] = slots
    else:
        grads = by_slot(slots + slots_ref[...], TILE)
        out_ref[:, half:, :] = grads.astype(BF).reshape(peers, TILE, LANE)


def pair(name, gate, gate_far, up, up_far, back, back_far, gate_t, up_t, experts, slot_grads=None, kept=()):
    total, hidden = gate.shape
    width = gate_t.shape[1]
    slots = total // experts
    extra = not kept
    peers = PEERS if extra else SECOND_PEERS
    rows = width // LANE * slots + (0 if extra else TILE)
    first = 0 if extra else experts * FIRST // (peers * slots)
    block = pl.BlockSpec((peers * slots, hidden), lambda i: (i, 0))
    placed = pl.BlockSpec((peers * slots, hidden), lambda i: (first + i, 0))
    whole = pl.BlockSpec(gate_t.shape, lambda i: (0, 0))
    small = pl.BlockSpec((peers, LANE), lambda i: (i, 0))
    more = () if extra else (slot_grads, *kept)
    return pl.pallas_call(
        functools.partial(pair_kernel, extra),
        grid=(experts // peers,),
        out_shape=[jax.ShapeDtypeStruct((experts, rows, LANE), BF)]
        + [jax.ShapeDtypeStruct((experts * CAP, hidden), BF)] * 3
        + [jax.ShapeDtypeStruct((experts, LANE), F32)] * extra,
        in_specs=[block] * 6
        + [whole] * 2
        + ([] if extra else [small] + [pl.BlockSpec(memory_space=pl.ANY)] * len(kept)),
        out_specs=[pl.BlockSpec((peers, rows, LANE), lambda i: (i, 0, 0))] + [placed] * 3 + [small] * extra,
        input_output_aliases={9 + k: 1 + k for k in range(len(kept))},
        compiler_params=pltpu.CompilerParams(vmem_limit_bytes=VMEM),
        cost_estimate=pl.CostEstimate(
            flops=4 * total * width * hidden,
            bytes_accessed=2 * (total * width + 9 * total * hidden + 2 * width * hidden),
            transcendentals=total * hidden,
        ),
        name=name,
    )(gate, gate_far, up, up_far, back, back_far, gate_t, up_t, *more)


def combine_first_kernel(ids_ref, in_ref, total_ref, rank_ref, rows_ref):
    step = pl.program_id(0)
    experts = rank_ref.shape[0]
    peers, tiles = in_ref.shape[0], total_ref.shape[1] // LANE

    @pl.when(step == 0)
    def _():
        rank_ref[...] = expert_ranks(ids_ref[...], experts)
        total_ref[...] = jnp.zeros_like(total_ref)

    unpack_half(in_ref, 0, rows_ref, 0, tiles)
    unpack_extra(in_ref, tiles * HALF, rows_ref, peers * HALF)
    rank = rank_ref[pl.ds(pl.multiple_of(step * peers, peers), peers), :]
    which = jnp.concatenate([half_rows(rank, None, 0), extra_rows(rank, None)], axis=0)
    total_ref[...] += contract(which, rows_ref[...])


def combine_second_kernel(
    ids_ref, probs_ref, in_ref, slots_ref, before_ref, rank_ref, out_ref, probs_out_ref, rows_ref, total_ref
):
    step = pl.program_id(0)
    experts, tokens = rank_ref.shape
    peers, tiles = in_ref.shape[0], out_ref.shape[1] // LANE

    @pl.when(step == 0)
    def _():
        total_ref[...] = before_ref[...]
        slots = slots_ref[:, 0, :].astype(F32)
        rank = rank_ref[...]
        found = jnp.zeros((experts, tokens), F32)
        for s in range(CAP):
            found = found + jnp.where(rank == float(s), slots[:, s : s + 1], 0.0)
        ids = ids_ref[...]
        expert = iota((experts, tokens), 0)
        grads = [
            jnp.sum(jnp.where(ids[k : k + 1] == expert, found, 0.0), axis=0, keepdims=True)
            for k in range(ids.shape[0])
        ]
        probs_out_ref[...] = (jnp.concatenate(grads, axis=0) / probs_ref[...].astype(F32)).astype(BF)

    unpack_half(in_ref, 0, rows_ref, 0, tiles)
    rank = rank_ref[pl.ds(pl.multiple_of(step * peers, peers), peers), :]
    total_ref[...] += contract(half_rows(rank, None, HALF), rows_ref[...])

    @pl.when(step == pl.num_programs(0) - 1)
    def _():
        out_ref[...] = total_ref[...].astype(BF)


def combine_first(ids, got, width):
    experts, rows, _ = got.shape
    tokens = ids.shape[1]
    whole = lambda shape: pl.BlockSpec(shape, lambda i: (0, 0))
    return pl.pallas_call(
        combine_first_kernel,
        grid=(experts // PEERS,),
        out_shape=[jax.ShapeDtypeStruct((tokens, width), F32), jax.ShapeDtypeStruct((experts, tokens), F32)],
        in_specs=[whole(ids.shape), pl.BlockSpec((PEERS, rows, LANE), lambda i: (i, 0, 0))],
        out_specs=[whole((tokens, width)), whole((experts, tokens))],
        scratch_shapes=[pltpu.VMEM((PEERS * FIRST, width), BF)],
        compiler_params=pltpu.CompilerParams(vmem_limit_bytes=VMEM),
        cost_estimate=pl.CostEstimate(
            flops=2 * experts * FIRST * tokens * width, bytes_accessed=2 * experts * rows * LANE, transcendentals=0
        ),
        name="combine_a",
    )(ids, got)


def combine_second(ids, probs, got, before, rank):
    experts, rows, _ = got.shape
    tokens, width = before.shape
    whole = lambda a: pl.BlockSpec(a.shape, lambda i: (0, 0))
    return pl.pallas_call(
        combine_second_kernel,
        grid=(experts // SUM_PEERS,),
        out_shape=[jax.ShapeDtypeStruct(before.shape, BF), jax.ShapeDtypeStruct(ids.shape, BF)],
        in_specs=[
            whole(ids),
            whole(probs),
            pl.BlockSpec((SUM_PEERS, rows - TILE, LANE), lambda i: (i, 0, 0)),
            pl.BlockSpec((experts, TILE, LANE), lambda i: (0, rows // TILE - 1, 0)),
            whole(before),
            whole(rank),
        ],
        out_specs=[whole(before), whole(ids)],
        scratch_shapes=[pltpu.VMEM((SUM_PEERS * HALF, width), BF), pltpu.VMEM((tokens, width), F32)],
        compiler_params=pltpu.CompilerParams(vmem_limit_bytes=VMEM),
        cost_estimate=pl.CostEstimate(
            flops=2 * experts * HALF * tokens * width, bytes_accessed=2 * experts * rows * LANE, transcendentals=0
        ),
        name="combine_b",
    )(ids, probs, got, got, before, rank)


def exchange(x):
    return lax.all_to_all(x, ("ctx", "tp"), split_axis=0, concat_axis=0, tiled=True)


def other_core(x):
    return lax.ppermute(x, "dp", [(0, 1), (1, 0)])


def per_device(tokens, cotangent, probs, expert_ids, gate_weight, up_weight, down_weight):
    experts = lax.axis_size("ctx") * lax.axis_size("tp")
    gate_mat, up_mat, down_mat = gate_weight[0], up_weight[0], down_weight[0]
    ids, weights = expert_ids.T, probs.T
    values = (tokens, cotangent)
    sent_a = pack("pack_a", pack_first_kernel, 2 * FIRST, 2, ids, weights, values, experts)
    got_a = exchange(sent_a)
    sent_b, gate_t, up_t, down_t = lax.optimization_barrier(
        (
            pack("pack_b", pack_second_kernel, 2 * HALF, 0, ids, weights, values, experts),
            gate_mat.T,
            up_mat.T,
            down_mat.T,
        )
    )
    got_b = exchange(sent_b)
    mats = (gate_mat, up_mat, down_t)

    def part(name, got, slot_grads=None, kept=()):
        rows, cot_rows, gate, up, back = project("project_" + name, got, mats, kept[:2])
        far = other_core(gate), other_core(up), other_core(back)
        sent, act, gate_grad, up_grad, *slot_grads = pair(
            "pair_" + name, gate, far[0], up, far[1], back, far[2], gate_t, up_t, experts, slot_grads, kept[2:]
        )
        return sent, slot_grads, (rows, cot_rows, act, gate_grad, up_grad)

    pairs_a, (slot_grads,), kept = part("a", got_a)
    got_b, pairs_a = lax.optimization_barrier((got_b, pairs_a))
    back_a = exchange(pairs_a)
    pairs_b, _, (rows, cot_rows, act, gate_grad, up_grad) = part("b", got_b, slot_grads, kept)
    back_b = exchange(pairs_b)
    grad_down = contract(act, cot_rows).astype(BF)
    grad_gate = contract(rows, gate_grad).astype(BF)
    grad_up = contract(rows, up_grad).astype(BF)
    before, rank = combine_first(ids, back_a, tokens.shape[1])
    grad_tokens, grad_probs = combine_second(ids, weights, back_b, before, rank)
    return (grad_tokens, grad_probs.T, grad_gate[None], grad_up[None], grad_down[None])


def solution(mesh):
    return jax.shard_map(
        per_device,
        mesh=mesh,
        in_specs=(
            P(("ctx", "tp"), "dp"),
            P(("ctx", "tp"), "dp"),
            P(("ctx", "tp"), None),
            P(("ctx", "tp"), None),
            P(("ctx", "tp"), "dp", None),
            P(("ctx", "tp"), "dp", None),
            P(("ctx", "tp"), None, "dp"),
        ),
        out_specs=(
            P(("ctx", "tp"), "dp"),
            P(("ctx", "tp"), None),
            P(("ctx", "tp"), "dp", None),
            P(("ctx", "tp"), "dp", None),
            P(("ctx", "tp"), None, "dp"),
        ),
        check_vma=False,
    )
```

```python
import functools

import jax
import jax.numpy as jnp
from jax import lax
from jax.experimental import pallas as pl
from jax.experimental.pallas import tpu as pltpu
from jax.sharding import PartitionSpec as P

BF = jnp.bfloat16
F32 = jnp.float32
LANE = 128
HALF = 8
EXTRA = 2
CAP = 2 * HALF + EXTRA
FIRST = HALF + EXTRA
TILE = 16
GROUP = 16
PEERS = 32
SECOND_PEERS = 16
PACK_PEERS = 32
SUM_PEERS = 64
VMEM = 60 * 2**20
SUM_VMEM = 24 * 2**20


def iota(shape, dim):
    return lax.broadcasted_iota(jnp.int32, shape, dim)


def dot(a, b):
    return jnp.dot(a, b, preferred_element_type=F32)


def contract(left, right):
    return lax.dot_general(left, right, (((0,), (0,)), ((), ())), preferred_element_type=F32)


def expert_ranks(ids, experts):
    top, tokens = ids.shape
    expert = iota((experts, tokens), 0)
    hit = jnp.zeros((experts, tokens), F32)
    for k in range(top):
        hit = hit + jnp.where(ids[k : k + 1] == expert, 1.0, 0.0)
    earlier = jnp.where(iota((tokens, tokens), 0) < iota((tokens, tokens), 1), 1.0, 0.0)
    rank = dot(hit.astype(BF), earlier.astype(BF))
    return jnp.where(hit > 0.0, rank, -1.0)


def expert_probs(ids, probs, experts):
    top, tokens = ids.shape
    expert = iota((experts, tokens), 0)
    out = jnp.zeros((experts, tokens), F32)
    for k in range(top):
        out = out + jnp.where(ids[k : k + 1] == expert, probs[k : k + 1], 0.0)
    return out


def by_slot(a, slots):
    peers, tokens = a.shape
    return jnp.broadcast_to(a[:, None, :], (peers, slots, tokens)).reshape(peers * slots, tokens)


def extra_order(pack):
    shape = (GROUP * TILE, GROUP * TILE)
    row, col = iota(shape, 0), iota(shape, 1)
    step = GROUP * EXTRA
    if pack:
        source = (row % TILE) // EXTRA * step + row // TILE * EXTRA + row % EXTRA
    else:
        source = (row % step) // EXTRA * TILE + row // step * EXTRA + row % EXTRA
    return jnp.where(col == source, 1.0, 0.0).astype(BF)


def store_half(out_ref, start, values):
    for c in range(0, values.shape[1] // LANE, 2):
        pair = [values[:, k * LANE : (k + 1) * LANE].reshape(-1, HALF, LANE) for k in (c, c + 1)]
        at = start + c * HALF
        out_ref[:, at : at + TILE, :] = jnp.concatenate(pair, axis=1).astype(BF)


def store_extra(out_ref, start, values):
    for g in range(values.shape[1] // LANE):
        at = start + g * TILE
        out_ref[:, at : at + TILE, :] = values[:, g * LANE : (g + 1) * LANE].reshape(-1, TILE, LANE)


def order_extra(out_ref, start, values):
    groups = values.shape[1] // LANE // 8
    order = extra_order(True)
    step = GROUP * EXTRA
    parts = []
    for p in range(values.shape[0] // step):
        some = values[p * step : (p + 1) * step]
        columns = [
            jnp.concatenate([some[:, (g * 8 + c) * LANE : (g * 8 + c + 1) * LANE] for g in range(groups)], axis=1)
            for c in range(8)
        ]
        parts.append(dot(order, jnp.concatenate(columns, axis=0)).astype(BF))
    store_extra(out_ref, start, jnp.concatenate(parts, axis=0))


def unpack_half(in_ref, start, out_ref, first, count):
    rows = in_ref.shape[0] * HALF
    for c in range(0, count, 2):
        at = start + c * HALF
        pair = in_ref[:, at : at + TILE, :].astype(F32)
        for k in range(2):
            column = first + c + k
            out_ref[:rows, column * LANE : (column + 1) * LANE] = (
                pair[:, k * HALF : (k + 1) * HALF, :].reshape(rows, LANE).astype(BF)
            )


def unpack_extra(in_ref, start, out_ref, base):
    groups = out_ref.shape[1] // LANE // 8
    order = extra_order(False)
    step = GROUP * EXTRA
    for p in range(in_ref.shape[0] // GROUP):
        some = in_ref.at[p * GROUP : (p + 1) * GROUP]
        values = jnp.concatenate(
            [some[:, start + g * TILE : start + (g + 1) * TILE, :].reshape(-1, LANE) for g in range(groups)], axis=1
        )
        ordered = dot(order, values).astype(BF)
        for g in range(groups):
            for c in range(8):
                at = (g * 8 + c) * LANE
                out_ref[base + p * step : base + (p + 1) * step, at : at + LANE] = ordered[
                    c * step : (c + 1) * step, g * LANE : (g + 1) * LANE
                ]


def half_rows(rank, value, start):
    rank = by_slot(rank, HALF)
    hit = rank == (start + iota(rank.shape, 0) % HALF).astype(F32)
    return jnp.where(hit, 1.0 if value is None else by_slot(value, HALF), 0.0).astype(BF)


def extra_rows(rank, value):
    peers = rank.shape[0]
    rank = by_slot(rank, 8)
    hit = rank == (2 * HALF + iota(rank.shape, 0) % 8).astype(F32)
    eight = jnp.where(hit, 1.0 if value is None else by_slot(value, 8), 0.0).astype(BF)
    shape = (peers * EXTRA, peers * 8)
    keep = iota(shape, 1) == iota(shape, 0) // EXTRA * 8 + iota(shape, 0) % EXTRA
    return dot(jnp.where(keep, 1.0, 0.0).astype(BF), eight).astype(BF)


def wide_extra_rows(rank, value):
    rank = by_slot(rank, TILE)
    row = iota(rank.shape, 0)
    hit = rank == (2 * HALF + row % EXTRA).astype(F32)
    extra = jnp.where(hit, 1.0 if value is None else by_slot(value, TILE), 0.0)
    column = (row % TILE) // EXTRA
    return jnp.concatenate([jnp.where(column == c, extra, 0.0).astype(BF) for c in range(8)], axis=1)


def stack_columns(x_ref, side_ref):
    tokens, width = x_ref.shape
    groups = width // LANE // 8
    for c in range(8):
        for g in range(groups):
            at = (g * 8 + c) * LANE
            side_ref[c * tokens : (c + 1) * tokens, g * LANE : (g + 1) * LANE] = x_ref[:, at : at + LANE]


def start_pack(ids_ref, probs_ref, rank_ref, prob_ref):
    experts = rank_ref.shape[0]
    rank_ref[...] = expert_ranks(ids_ref[...], experts)
    prob_ref[...] = expert_probs(ids_ref[...], probs_ref[...].astype(F32), experts)


def pack_first_kernel(ids_ref, probs_ref, x_ref, cot_ref, out_ref, rank_ref, prob_ref, side_ref, cot_side_ref):
    step = pl.program_id(0)
    half = x_ref.shape[1] // LANE * HALF
    part = x_ref.shape[1] // LANE * FIRST
    count = out_ref.shape[0]

    @pl.when(step == 0)
    def _():
        start_pack(ids_ref, probs_ref, rank_ref, prob_ref)
        stack_columns(x_ref, side_ref)
        stack_columns(cot_ref, cot_side_ref)

    peers = pl.ds(pl.multiple_of(step * count, count), count)
    rank, prob = rank_ref[peers, :], prob_ref[peers, :]
    for start, value, ref, side in ((0, None, x_ref, side_ref), (part, prob, cot_ref, cot_side_ref)):
        store_half(out_ref, start, dot(half_rows(rank, value, 0), ref[...]))
        store_extra(out_ref, start + half, dot(wide_extra_rows(rank, value), side[...]).astype(BF))


def pack_second_kernel(ids_ref, probs_ref, x_ref, cot_ref, out_ref, rank_ref, prob_ref):
    step = pl.program_id(0)
    half = x_ref.shape[1] // LANE * HALF

    @pl.when(step == 0)
    def _():
        start_pack(ids_ref, probs_ref, rank_ref, prob_ref)

    count = out_ref.shape[0]
    peers = pl.ds(pl.multiple_of(step * count, count), count)
    rank, prob = rank_ref[peers, :], prob_ref[peers, :]
    store_half(out_ref, 0, dot(half_rows(rank, None, HALF), x_ref[...]))
    store_half(out_ref, half, dot(half_rows(rank, prob, HALF), cot_ref[...]))


def pack(name, kernel, slots, sides, ids, probs, values, experts):
    tokens, width = values[0].shape
    rows = width // LANE * slots
    return pl.pallas_call(
        kernel,
        grid=(experts // PACK_PEERS,),
        out_shape=jax.ShapeDtypeStruct((experts, rows, LANE), BF),
        in_specs=[pl.BlockSpec(a.shape, lambda i: (0, 0)) for a in (ids, probs, *values)],
        out_specs=pl.BlockSpec((PACK_PEERS, rows, LANE), lambda i: (i, 0, 0)),
        scratch_shapes=[pltpu.VMEM((experts, tokens), F32)] * 2 + [pltpu.VMEM((8 * tokens, width // 8), BF)] * sides,
        compiler_params=pltpu.CompilerParams(vmem_limit_bytes=VMEM),
        cost_estimate=pl.CostEstimate(
            flops=4 * experts * slots * tokens * width, bytes_accessed=2 * experts * rows * LANE, transcendentals=0
        ),
        name=name,
    )(ids, probs, *values)


def project_kernel(extra, x_in, cot_in, gate_w, up_w, down_w, *refs):
    x_ref, cot_ref, gate_ref, up_ref, back_ref = refs[-5:]
    peers = x_in.shape[0]
    tiles = x_ref.shape[1] // LANE
    for in_ref, rows_ref in ((x_in, x_ref), (cot_in, cot_ref)):
        unpack_half(in_ref, 0, rows_ref, 0, tiles)
        if extra:
            unpack_extra(in_ref, tiles * HALF, rows_ref, peers * HALF)
    gate_ref[...] = dot(x_ref[...], gate_w[...]).astype(BF)
    up_ref[...] = dot(x_ref[...], up_w[...]).astype(BF)
    back_ref[...] = dot(cot_ref[...], down_w[...]).astype(BF)


def project(name, got, weights, kept=()):
    experts, both, _ = got.shape
    width, hidden = weights[0].shape
    part = both // 2
    slots = part * LANE // width
    peers = SECOND_PEERS if kept else PEERS
    total, rows = experts * slots, peers * slots
    first = experts * FIRST // rows if kept else 0
    whole = experts * CAP
    return pl.pallas_call(
        functools.partial(project_kernel, not kept),
        grid=(experts // peers,),
        out_shape=[jax.ShapeDtypeStruct((whole, width), BF)] * 2 + [jax.ShapeDtypeStruct((total, hidden), BF)] * 3,
        in_specs=[pl.BlockSpec((peers, part, LANE), lambda i, at=at: (i, at, 0)) for at in range(2)]
        + [pl.BlockSpec(w.shape, lambda i: (0, 0)) for w in weights]
        + [pl.BlockSpec(memory_space=pl.ANY) for _ in kept],
        out_specs=[pl.BlockSpec((rows, width), lambda i: (first + i, 0))] * 2
        + [pl.BlockSpec((rows, hidden), lambda i: (i, 0))] * 3,
        input_output_aliases={5 + k: k for k in range(len(kept))},
        compiler_params=pltpu.CompilerParams(vmem_limit_bytes=VMEM),
        cost_estimate=pl.CostEstimate(
            flops=6 * total * width * hidden,
            bytes_accessed=2 * (4 * total * width + 3 * (width + total) * hidden),
            transcendentals=0,
        ),
        name=name,
    )(got, got, *weights, *kept)


def turn_kernel(core, count, *refs):
    ins, outs = refs[:count], refs[-5 * count : -4 * count]
    held, turned = refs[-4 * count : -3 * count], refs[-3 * count : -2 * count]
    in_sems, out_sems = refs[-2 * count : -count], refs[-count:]

    @pl.when(lax.axis_index("dp") == core)
    def _():
        loads = [pltpu.make_async_copy(a, b, sem) for a, b, sem in zip(ins, held, in_sems)]
        stores = [pltpu.make_async_copy(a, b, sem) for a, b, sem in zip(turned, outs, out_sems)]
        for load in loads:
            load.start()
        for load, store, a, b in zip(loads, stores, held, turned):
            load.wait()
            for at in range(0, a.shape[0], 256):
                b[:, at : at + 256] = a[at : at + 256, :].T
            store.start()
        for store in stores:
            store.wait()


def turn(name, core, mats, before=()):
    shapes = [m.shape for m in mats]
    anywhere = pl.BlockSpec(memory_space=pl.ANY)
    return pl.pallas_call(
        functools.partial(turn_kernel, core, len(mats)),
        out_shape=[jax.ShapeDtypeStruct(shape[::-1], BF) for shape in shapes],
        in_specs=[anywhere] * (len(mats) + len(before)),
        out_specs=[anywhere] * len(mats),
        input_output_aliases={len(mats) + k: k for k in range(len(before))},
        scratch_shapes=[pltpu.VMEM(shape, BF) for shape in shapes]
        + [pltpu.VMEM(shape[::-1], BF) for shape in shapes]
        + [pltpu.SemaphoreType.DMA] * (2 * len(mats)),
        compiler_params=pltpu.CompilerParams(vmem_limit_bytes=VMEM),
        cost_estimate=pl.CostEstimate(
            flops=0, bytes_accessed=sum(8 * a * b for a, b in shapes), transcendentals=0
        ),
        name=name,
    )(*mats, *before)


def slots_of(prob_grad, peers, extra):
    total = prob_grad.shape[0]
    main = peers * HALF
    row, lane = iota((total, LANE), 0), iota((total, LANE), 1)
    peer, of = iota((peers, total), 0), iota((peers, total), 1)
    slot, owner = row % HALF, of // HALF
    if extra:
        slot = jnp.where(row < main, slot, 2 * HALF + row % EXTRA)
        owner = jnp.where(of < main, owner, (of - main) // EXTRA)
    else:
        slot = slot + HALF
    by_lane = jnp.where(lane == slot, prob_grad, 0.0).astype(BF)
    return dot(jnp.where(peer == owner, 1.0, 0.0).astype(BF), by_lane)


def pair_kernel(extra, *refs):
    if extra:
        *refs, out_ref, act_ref, gg_ref, ug_ref, slots_out_ref = refs
    else:
        *refs, slots_ref, _, _, _, out_ref, act_ref, gg_ref, ug_ref = refs
    gate, gate_far, up, up_far, back, back_far, gate_t, up_t = refs
    g = gate[...].astype(F32) + gate_far[...].astype(F32)
    u = up[...].astype(F32) + up_far[...].astype(F32)
    b = back[...].astype(F32) + back_far[...].astype(F32)
    sigmoid = jax.nn.sigmoid(g)
    silu = g * sigmoid
    act = silu * u
    act_ref[...] = act.astype(BF)
    gg_ref[...] = (b * u * sigmoid * (1.0 + g * (1.0 - sigmoid))).astype(BF)
    ug_ref[...] = (b * silu).astype(BF)
    prob_grad = jnp.sum(act * b, axis=1, keepdims=True)
    y = dot(gg_ref[...], gate_t[...]) + dot(ug_ref[...], up_t[...])
    half = y.shape[1] // LANE * HALF
    peers = out_ref.shape[0]
    main = peers * HALF
    store_half(out_ref, 0, y[:main])
    slots = slots_of(prob_grad, peers, extra)
    if extra:
        order_extra(out_ref, half, y[main:].astype(BF))
        slots_out_ref[...] = slots
    else:
        grads = by_slot(slots + slots_ref[...], TILE)
        out_ref[:, half:, :] = grads.astype(BF).reshape(peers, TILE, LANE)


def pair(name, gate, gate_far, up, up_far, back, back_far, gate_t, up_t, experts, slot_grads=None, kept=()):
    total, hidden = gate.shape
    width = gate_t.shape[1]
    slots = total // experts
    extra = not kept
    peers = PEERS if extra else SECOND_PEERS
    rows = width // LANE * slots + (0 if extra else TILE)
    first = 0 if extra else experts * FIRST // (peers * slots)
    block = pl.BlockSpec((peers * slots, hidden), lambda i: (i, 0))
    placed = pl.BlockSpec((peers * slots, hidden), lambda i: (first + i, 0))
    whole = pl.BlockSpec(gate_t.shape, lambda i: (0, 0))
    small = pl.BlockSpec((peers, LANE), lambda i: (i, 0))
    more = () if extra else (slot_grads, *kept)
    return pl.pallas_call(
        functools.partial(pair_kernel, extra),
        grid=(experts // peers,),
        out_shape=[jax.ShapeDtypeStruct((experts, rows, LANE), BF)]
        + [jax.ShapeDtypeStruct((experts * CAP, hidden), BF)] * 3
        + [jax.ShapeDtypeStruct((experts, LANE), F32)] * extra,
        in_specs=[block] * 6
        + [whole] * 2
        + ([] if extra else [small] + [pl.BlockSpec(memory_space=pl.ANY)] * len(kept)),
        out_specs=[pl.BlockSpec((peers, rows, LANE), lambda i: (i, 0, 0))] + [placed] * 3 + [small] * extra,
        input_output_aliases={9 + k: 1 + k for k in range(len(kept))},
        compiler_params=pltpu.CompilerParams(vmem_limit_bytes=VMEM),
        cost_estimate=pl.CostEstimate(
            flops=4 * total * width * hidden,
            bytes_accessed=2 * (total * width + 9 * total * hidden + 2 * width * hidden),
            transcendentals=total * hidden,
        ),
        name=name,
    )(gate, gate_far, up, up_far, back, back_far, gate_t, up_t, *more)


def combine_first_kernel(ids_ref, in_ref, total_ref, rank_ref, rows_ref):
    step = pl.program_id(0)
    experts = rank_ref.shape[0]
    peers, tiles = in_ref.shape[0], total_ref.shape[1] // LANE

    @pl.when(step == 0)
    def _():
        rank_ref[...] = expert_ranks(ids_ref[...], experts)
        total_ref[...] = jnp.zeros_like(total_ref)

    unpack_half(in_ref, 0, rows_ref, 0, tiles)
    unpack_extra(in_ref, tiles * HALF, rows_ref, peers * HALF)
    rank = rank_ref[pl.ds(pl.multiple_of(step * peers, peers), peers), :]
    which = jnp.concatenate([half_rows(rank, None, 0), extra_rows(rank, None)], axis=0)
    total_ref[...] += contract(which, rows_ref[...])


def combine_second_kernel(
    ids_ref, probs_ref, in_ref, slots_ref, before_ref, rank_ref, out_ref, probs_out_ref, rows_ref, total_ref
):
    step = pl.program_id(0)
    experts, tokens = rank_ref.shape
    peers, tiles = in_ref.shape[0], out_ref.shape[1] // LANE

    @pl.when(step == 0)
    def _():
        total_ref[...] = before_ref[...]
        slots = slots_ref[:, 0, :].astype(F32)
        rank = rank_ref[...]
        found = jnp.zeros((experts, tokens), F32)
        for s in range(CAP):
            found = found + jnp.where(rank == float(s), slots[:, s : s + 1], 0.0)
        ids = ids_ref[...]
        expert = iota((experts, tokens), 0)
        grads = [
            jnp.sum(jnp.where(ids[k : k + 1] == expert, found, 0.0), axis=0, keepdims=True)
            for k in range(ids.shape[0])
        ]
        probs_out_ref[...] = (jnp.concatenate(grads, axis=0) / probs_ref[...].astype(F32)).astype(BF)

    unpack_half(in_ref, 0, rows_ref, 0, tiles)
    rank = rank_ref[pl.ds(pl.multiple_of(step * peers, peers), peers), :]
    total_ref[...] += contract(half_rows(rank, None, HALF), rows_ref[...])

    @pl.when(step == pl.num_programs(0) - 1)
    def _():
        out_ref[...] = total_ref[...].astype(BF)


def combine_first(ids, got, width):
    experts, rows, _ = got.shape
    tokens = ids.shape[1]
    whole = lambda shape: pl.BlockSpec(shape, lambda i: (0, 0))
    return pl.pallas_call(
        combine_first_kernel,
        grid=(experts // PEERS,),
        out_shape=[jax.ShapeDtypeStruct((tokens, width), F32), jax.ShapeDtypeStruct((experts, tokens), F32)],
        in_specs=[whole(ids.shape), pl.BlockSpec((PEERS, rows, LANE), lambda i: (i, 0, 0))],
        out_specs=[whole((tokens, width)), whole((experts, tokens))],
        scratch_shapes=[pltpu.VMEM((PEERS * FIRST, width), BF)],
        compiler_params=pltpu.CompilerParams(vmem_limit_bytes=SUM_VMEM),
        cost_estimate=pl.CostEstimate(
            flops=2 * experts * FIRST * tokens * width, bytes_accessed=2 * experts * rows * LANE, transcendentals=0
        ),
        name="combine_a",
    )(ids, got)


def combine_second(ids, probs, got, before, rank):
    experts, rows, _ = got.shape
    tokens, width = before.shape
    whole = lambda a: pl.BlockSpec(a.shape, lambda i: (0, 0))
    return pl.pallas_call(
        combine_second_kernel,
        grid=(experts // SUM_PEERS,),
        out_shape=[jax.ShapeDtypeStruct(before.shape, BF), jax.ShapeDtypeStruct(ids.shape, BF)],
        in_specs=[
            whole(ids),
            whole(probs),
            pl.BlockSpec((SUM_PEERS, rows - TILE, LANE), lambda i: (i, 0, 0)),
            pl.BlockSpec((experts, TILE, LANE), lambda i: (0, rows // TILE - 1, 0)),
            whole(before),
            whole(rank),
        ],
        out_specs=[whole(before), whole(ids)],
        scratch_shapes=[pltpu.VMEM((SUM_PEERS * HALF, width), BF), pltpu.VMEM((tokens, width), F32)],
        compiler_params=pltpu.CompilerParams(vmem_limit_bytes=SUM_VMEM),
        cost_estimate=pl.CostEstimate(
            flops=2 * experts * HALF * tokens * width, bytes_accessed=2 * experts * rows * LANE, transcendentals=0
        ),
        name="combine_b",
    )(ids, probs, got, got, before, rank)


def exchange(x):
    return lax.all_to_all(x, ("ctx", "tp"), split_axis=0, concat_axis=0, tiled=True)


def other_core(x):
    return lax.ppermute(x, "dp", [(0, 1), (1, 0)])


def per_device(tokens, cotangent, probs, expert_ids, gate_weight, up_weight, down_weight):
    experts = lax.axis_size("ctx") * lax.axis_size("tp")
    gate_mat, up_mat, down_mat = gate_weight[0], up_weight[0], down_weight[0]
    ids, weights = expert_ids.T, probs.T
    values = (tokens, cotangent)
    mats = (gate_mat, up_mat, down_mat)
    sent_a, *turned = lax.optimization_barrier(
        (
            pack("pack_a", pack_first_kernel, 2 * FIRST, 2, ids, weights, values, experts),
            *turn("turn_first", 1, mats),
        )
    )
    got_a = exchange(sent_a)
    sent_b, gate_t, up_t, down_t = lax.optimization_barrier(
        (
            pack("pack_b", pack_second_kernel, 2 * HALF, 0, ids, weights, values, experts),
            *turn("turn_second", 0, mats, turned),
        )
    )
    got_b = exchange(sent_b)
    mats = (gate_mat, up_mat, down_t)

    def part(name, got, slot_grads=None, kept=()):
        rows, cot_rows, gate, up, back = project("project_" + name, got, mats, kept[:2])
        far = other_core(gate), other_core(up), other_core(back)
        sent, act, gate_grad, up_grad, *slot_grads = pair(
            "pair_" + name, gate, far[0], up, far[1], back, far[2], gate_t, up_t, experts, slot_grads, kept[2:]
        )
        return sent, slot_grads, (rows, cot_rows, act, gate_grad, up_grad)

    pairs_a, (slot_grads,), kept = part("a", got_a)
    got_b, pairs_a = lax.optimization_barrier((got_b, pairs_a))
    back_a = exchange(pairs_a)
    pairs_b, _, (rows, cot_rows, act, gate_grad, up_grad) = part("b", got_b, slot_grads, kept)
    back_b = exchange(pairs_b)
    grad_down = contract(act, cot_rows).astype(BF)
    grad_gate = contract(rows, gate_grad).astype(BF)
    grad_up = contract(rows, up_grad).astype(BF)
    before, rank = combine_first(ids, back_a, tokens.shape[1])
    grad_tokens, grad_probs = combine_second(ids, weights, back_b, before, rank)
    return (grad_tokens, grad_probs.T, grad_gate[None], grad_up[None], grad_down[None])


def solution(mesh):
    return jax.shard_map(
        per_device,
        mesh=mesh,
        in_specs=(
            P(("ctx", "tp"), "dp"),
            P(("ctx", "tp"), "dp"),
            P(("ctx", "tp"), None),
            P(("ctx", "tp"), None),
            P(("ctx", "tp"), "dp", None),
            P(("ctx", "tp"), "dp", None),
            P(("ctx", "tp"), None, "dp"),
        ),
        out_specs=(
            P(("ctx", "tp"), "dp"),
            P(("ctx", "tp"), None),
            P(("ctx", "tp"), "dp", None),
            P(("ctx", "tp"), "dp", None),
            P(("ctx", "tp"), None, "dp"),
        ),
        check_vma=False,
    )
```

```python
import functools

import jax
import jax.numpy as jnp
from jax import lax
from jax.experimental import pallas as pl
from jax.experimental.pallas import tpu as pltpu
from jax.sharding import PartitionSpec as P

BF = jnp.bfloat16
F32 = jnp.float32
LANE = 128
HALF = 8
EXTRA = 2
CAP = 2 * HALF + EXTRA
FIRST = HALF + EXTRA
TILE = 16
GROUP = 16
PEERS = 32
SECOND_PEERS = 16
PACK_PEERS = 32
SUM_PEERS = 64
VMEM = 62 * 2**20
SUM_VMEM = 24 * 2**20


def iota(shape, dim):
    return lax.broadcasted_iota(jnp.int32, shape, dim)


def dot(a, b):
    return jnp.dot(a, b, preferred_element_type=F32)


def contract(left, right):
    return lax.dot_general(left, right, (((0,), (0,)), ((), ())), preferred_element_type=F32)


def expert_ranks(ids, experts):
    top, tokens = ids.shape
    expert = iota((experts, tokens), 0)
    hit = jnp.zeros((experts, tokens), F32)
    for k in range(top):
        hit = hit + jnp.where(ids[k : k + 1] == expert, 1.0, 0.0)
    earlier = jnp.where(iota((tokens, tokens), 0) < iota((tokens, tokens), 1), 1.0, 0.0)
    rank = dot(hit.astype(BF), earlier.astype(BF))
    return jnp.where(hit > 0.0, rank, -1.0)


def expert_probs(ids, probs, experts):
    top, tokens = ids.shape
    expert = iota((experts, tokens), 0)
    out = jnp.zeros((experts, tokens), F32)
    for k in range(top):
        out = out + jnp.where(ids[k : k + 1] == expert, probs[k : k + 1], 0.0)
    return out


def by_slot(a, slots):
    peers, tokens = a.shape
    return jnp.broadcast_to(a[:, None, :], (peers, slots, tokens)).reshape(peers * slots, tokens)


def extra_order(pack):
    shape = (GROUP * TILE, GROUP * TILE)
    row, col = iota(shape, 0), iota(shape, 1)
    step = GROUP * EXTRA
    if pack:
        source = (row % TILE) // EXTRA * step + row // TILE * EXTRA + row % EXTRA
    else:
        source = (row % step) // EXTRA * TILE + row // step * EXTRA + row % EXTRA
    return jnp.where(col == source, 1.0, 0.0).astype(BF)


def store_half(out_ref, start, values):
    for c in range(0, values.shape[1] // LANE, 2):
        pair = [values[:, k * LANE : (k + 1) * LANE].reshape(-1, HALF, LANE) for k in (c, c + 1)]
        at = start + c * HALF
        out_ref[:, at : at + TILE, :] = jnp.concatenate(pair, axis=1).astype(BF)


def store_extra(out_ref, start, values):
    for g in range(values.shape[1] // LANE):
        at = start + g * TILE
        out_ref[:, at : at + TILE, :] = values[:, g * LANE : (g + 1) * LANE].reshape(-1, TILE, LANE)


def order_extra(out_ref, start, values):
    groups = values.shape[1] // LANE // 8
    order = extra_order(True)
    step = GROUP * EXTRA
    parts = []
    for p in range(values.shape[0] // step):
        some = values[p * step : (p + 1) * step]
        columns = [
            jnp.concatenate([some[:, (g * 8 + c) * LANE : (g * 8 + c + 1) * LANE] for g in range(groups)], axis=1)
            for c in range(8)
        ]
        parts.append(dot(order, jnp.concatenate(columns, axis=0)).astype(BF))
    store_extra(out_ref, start, jnp.concatenate(parts, axis=0))


def unpack_half(in_ref, start, out_ref, first, count):
    rows = in_ref.shape[0] * HALF
    for c in range(0, count, 2):
        at = start + c * HALF
        pair = in_ref[:, at : at + TILE, :].astype(F32)
        for k in range(2):
            column = first + c + k
            out_ref[:rows, column * LANE : (column + 1) * LANE] = (
                pair[:, k * HALF : (k + 1) * HALF, :].reshape(rows, LANE).astype(BF)
            )


def unpack_extra(in_ref, start, out_ref, base):
    groups = out_ref.shape[1] // LANE // 8
    order = extra_order(False)
    step = GROUP * EXTRA
    for p in range(in_ref.shape[0] // GROUP):
        some = in_ref.at[p * GROUP : (p + 1) * GROUP]
        values = jnp.concatenate(
            [some[:, start + g * TILE : start + (g + 1) * TILE, :].reshape(-1, LANE) for g in range(groups)], axis=1
        )
        ordered = dot(order, values).astype(BF)
        for g in range(groups):
            for c in range(8):
                at = (g * 8 + c) * LANE
                out_ref[base + p * step : base + (p + 1) * step, at : at + LANE] = ordered[
                    c * step : (c + 1) * step, g * LANE : (g + 1) * LANE
                ]


def half_rows(rank, value, start):
    rank = by_slot(rank, HALF)
    hit = rank == (start + iota(rank.shape, 0) % HALF).astype(F32)
    return jnp.where(hit, 1.0 if value is None else by_slot(value, HALF), 0.0).astype(BF)


def extra_rows(rank, value):
    peers = rank.shape[0]
    rank = by_slot(rank, 8)
    hit = rank == (2 * HALF + iota(rank.shape, 0) % 8).astype(F32)
    eight = jnp.where(hit, 1.0 if value is None else by_slot(value, 8), 0.0).astype(BF)
    shape = (peers * EXTRA, peers * 8)
    keep = iota(shape, 1) == iota(shape, 0) // EXTRA * 8 + iota(shape, 0) % EXTRA
    return dot(jnp.where(keep, 1.0, 0.0).astype(BF), eight).astype(BF)


def wide_extra_rows(rank, value):
    rank = by_slot(rank, TILE)
    row = iota(rank.shape, 0)
    hit = rank == (2 * HALF + row % EXTRA).astype(F32)
    extra = jnp.where(hit, 1.0 if value is None else by_slot(value, TILE), 0.0)
    column = (row % TILE) // EXTRA
    return jnp.concatenate([jnp.where(column == c, extra, 0.0).astype(BF) for c in range(8)], axis=1)


def stack_columns(x_ref, side_ref):
    tokens, width = x_ref.shape
    groups = width // LANE // 8
    for c in range(8):
        for g in range(groups):
            at = (g * 8 + c) * LANE
            side_ref[c * tokens : (c + 1) * tokens, g * LANE : (g + 1) * LANE] = x_ref[:, at : at + LANE]


def start_pack(ids_ref, probs_ref, rank_ref, prob_ref):
    experts = rank_ref.shape[0]
    rank_ref[...] = expert_ranks(ids_ref[...], experts)
    prob_ref[...] = expert_probs(ids_ref[...], probs_ref[...].astype(F32), experts)


def pack_first_kernel(ids_ref, probs_ref, x_ref, cot_ref, out_ref, rank_ref, prob_ref, side_ref, cot_side_ref):
    step = pl.program_id(0)
    half = x_ref.shape[1] // LANE * HALF
    part = x_ref.shape[1] // LANE * FIRST
    count = out_ref.shape[0]

    @pl.when(step == 0)
    def _():
        start_pack(ids_ref, probs_ref, rank_ref, prob_ref)
        stack_columns(x_ref, side_ref)
        stack_columns(cot_ref, cot_side_ref)

    peers = pl.ds(pl.multiple_of(step * count, count), count)
    rank, prob = rank_ref[peers, :], prob_ref[peers, :]
    for start, value, ref, side in ((0, None, x_ref, side_ref), (part, prob, cot_ref, cot_side_ref)):
        store_half(out_ref, start, dot(half_rows(rank, value, 0), ref[...]))
        store_extra(out_ref, start + half, dot(wide_extra_rows(rank, value), side[...]).astype(BF))


def pack(name, kernel, slots, sides, ids, probs, values, experts):
    tokens, width = values[0].shape
    rows = width // LANE * slots
    return pl.pallas_call(
        kernel,
        grid=(experts // PACK_PEERS,),
        out_shape=jax.ShapeDtypeStruct((experts, rows, LANE), BF),
        in_specs=[pl.BlockSpec(a.shape, lambda i: (0, 0)) for a in (ids, probs, *values)],
        out_specs=pl.BlockSpec((PACK_PEERS, rows, LANE), lambda i: (i, 0, 0)),
        scratch_shapes=[pltpu.VMEM((experts, tokens), F32)] * 2 + [pltpu.VMEM((8 * tokens, width // 8), BF)] * sides,
        compiler_params=pltpu.CompilerParams(vmem_limit_bytes=VMEM),
        cost_estimate=pl.CostEstimate(
            flops=4 * experts * slots * tokens * width, bytes_accessed=2 * experts * rows * LANE, transcendentals=0
        ),
        name=name,
    )(ids, probs, *values)


def ahead_kernel(core, count, ids_ref, probs_ref, *refs):
    mats, (x_ref, cot_ref), refs = refs[:count], refs[count : count + 2], refs[-(4 * count + 9) :]
    outs, out_ref, refs = refs[:count], refs[count], refs[count + 1 :]
    held, turned, refs = refs[:count], refs[count : 2 * count], refs[2 * count :]
    x, cot, packed, rank_ref, prob_ref = refs[:5]
    mat_sems, x_sem, cot_sem, pack_sems = refs[5 : 5 + count], refs[5 + count], refs[6 + count], refs[7 + count]
    experts = out_ref.shape[0]

    @pl.when(lax.axis_index("dp") == core)
    def _():
        values = [pltpu.make_async_copy(x_ref, x, x_sem), pltpu.make_async_copy(cot_ref, cot, cot_sem)]
        for copy in values:
            copy.start()
        for mat, a, b, out, sem in zip(mats, held, turned, outs, mat_sems):
            load = pltpu.make_async_copy(mat, a, sem)
            load.start()
            load.wait()
            for at in range(0, a.shape[0], 256):
                b[:, at : at + 256] = a[at : at + 256, :].T
            store = pltpu.make_async_copy(b, out, sem)
            store.start()
            store.wait()
        for copy in values:
            copy.wait()
        start_pack(ids_ref, probs_ref, rank_ref, prob_ref)
        half = x.shape[1] // LANE * HALF
        stores = []
        for n in range(experts // PACK_PEERS):
            peers = pl.ds(n * PACK_PEERS, PACK_PEERS)
            rank, prob = rank_ref[peers, :], prob_ref[peers, :]
            slot = packed.at[n]
            store_half(slot, 0, dot(half_rows(rank, None, HALF), x[...]))
            store_half(slot, half, dot(half_rows(rank, prob, HALF), cot[...]))
            stores.append(pltpu.make_async_copy(slot, out_ref.at[peers], pack_sems.at[n]))
            stores[-1].start()
        for store in stores:
            store.wait()


def ahead(name, core, ids, probs, mats, values, experts, before=()):
    tokens, width = values[0].shape
    rows = width // LANE * 2 * HALF
    steps = experts // PACK_PEERS
    shapes = [m.shape for m in mats]
    outs = [shape[::-1] for shape in shapes] + [(experts, rows, LANE)]
    anywhere = pl.BlockSpec(memory_space=pl.ANY)
    given = (*mats, *values, *before)
    return pl.pallas_call(
        functools.partial(ahead_kernel, core, len(mats)),
        out_shape=[jax.ShapeDtypeStruct(shape, BF) for shape in outs],
        in_specs=[pl.BlockSpec(memory_space=pltpu.VMEM)] * 2 + [anywhere] * len(given),
        out_specs=[anywhere] * len(outs),
        input_output_aliases={2 + len(given) - len(before) + k: k for k in range(len(before))},
        scratch_shapes=[pltpu.VMEM(shape, BF) for shape in shapes]
        + [pltpu.VMEM(shape[::-1], BF) for shape in shapes]
        + [pltpu.VMEM((tokens, width), BF)] * 2
        + [pltpu.VMEM((steps, PACK_PEERS, rows, LANE), BF)]
        + [pltpu.VMEM((experts, tokens), F32)] * 2
        + [pltpu.SemaphoreType.DMA] * (len(mats) + 2)
        + [pltpu.SemaphoreType.DMA((steps,))],
        compiler_params=pltpu.CompilerParams(vmem_limit_bytes=VMEM),
        cost_estimate=pl.CostEstimate(
            flops=4 * experts * HALF * tokens * width,
            bytes_accessed=sum(8 * a * b for a, b in shapes) + 2 * experts * rows * LANE,
            transcendentals=0,
        ),
        name=name,
    )(ids, probs, *given)


def project_kernel(extra, x_in, cot_in, gate_w, up_w, down_w, *refs):
    x_ref, cot_ref, gate_ref, up_ref, back_ref = refs[-5:]
    peers = x_in.shape[0]
    tiles = x_ref.shape[1] // LANE
    for in_ref, rows_ref in ((x_in, x_ref), (cot_in, cot_ref)):
        unpack_half(in_ref, 0, rows_ref, 0, tiles)
        if extra:
            unpack_extra(in_ref, tiles * HALF, rows_ref, peers * HALF)
    gate_ref[...] = dot(x_ref[...], gate_w[...]).astype(BF)
    up_ref[...] = dot(x_ref[...], up_w[...]).astype(BF)
    back_ref[...] = dot(cot_ref[...], down_w[...]).astype(BF)


def project(name, got, weights, kept=()):
    experts, both, _ = got.shape
    width, hidden = weights[0].shape
    part = both // 2
    slots = part * LANE // width
    peers = SECOND_PEERS if kept else PEERS
    total, rows = experts * slots, peers * slots
    first = experts * FIRST // rows if kept else 0
    whole = experts * CAP
    return pl.pallas_call(
        functools.partial(project_kernel, not kept),
        grid=(experts // peers,),
        out_shape=[jax.ShapeDtypeStruct((whole, width), BF)] * 2 + [jax.ShapeDtypeStruct((total, hidden), BF)] * 3,
        in_specs=[pl.BlockSpec((peers, part, LANE), lambda i, at=at: (i, at, 0)) for at in range(2)]
        + [pl.BlockSpec(w.shape, lambda i: (0, 0)) for w in weights]
        + [pl.BlockSpec(memory_space=pl.ANY) for _ in kept],
        out_specs=[pl.BlockSpec((rows, width), lambda i: (first + i, 0))] * 2
        + [pl.BlockSpec((rows, hidden), lambda i: (i, 0))] * 3,
        input_output_aliases={5 + k: k for k in range(len(kept))},
        compiler_params=pltpu.CompilerParams(vmem_limit_bytes=VMEM),
        cost_estimate=pl.CostEstimate(
            flops=6 * total * width * hidden,
            bytes_accessed=2 * (4 * total * width + 3 * (width + total) * hidden),
            transcendentals=0,
        ),
        name=name,
    )(got, got, *weights, *kept)


def slots_of(prob_grad, peers, extra):
    total = prob_grad.shape[0]
    main = peers * HALF
    row, lane = iota((total, LANE), 0), iota((total, LANE), 1)
    peer, of = iota((peers, total), 0), iota((peers, total), 1)
    slot, owner = row % HALF, of // HALF
    if extra:
        slot = jnp.where(row < main, slot, 2 * HALF + row % EXTRA)
        owner = jnp.where(of < main, owner, (of - main) // EXTRA)
    else:
        slot = slot + HALF
    by_lane = jnp.where(lane == slot, prob_grad, 0.0).astype(BF)
    return dot(jnp.where(peer == owner, 1.0, 0.0).astype(BF), by_lane)


def pair_kernel(extra, *refs):
    if extra:
        *refs, out_ref, act_ref, gg_ref, ug_ref, slots_out_ref = refs
    else:
        *refs, slots_ref, _, _, _, out_ref, act_ref, gg_ref, ug_ref = refs
    gate, gate_far, up, up_far, back, back_far, gate_t, up_t = refs
    g = gate[...].astype(F32) + gate_far[...].astype(F32)
    u = up[...].astype(F32) + up_far[...].astype(F32)
    b = back[...].astype(F32) + back_far[...].astype(F32)
    sigmoid = jax.nn.sigmoid(g)
    silu = g * sigmoid
    act = silu * u
    act_ref[...] = act.astype(BF)
    gg_ref[...] = (b * u * sigmoid * (1.0 + g * (1.0 - sigmoid))).astype(BF)
    ug_ref[...] = (b * silu).astype(BF)
    prob_grad = jnp.sum(act * b, axis=1, keepdims=True)
    y = dot(gg_ref[...], gate_t[...]) + dot(ug_ref[...], up_t[...])
    half = y.shape[1] // LANE * HALF
    peers = out_ref.shape[0]
    main = peers * HALF
    store_half(out_ref, 0, y[:main])
    slots = slots_of(prob_grad, peers, extra)
    if extra:
        order_extra(out_ref, half, y[main:].astype(BF))
        slots_out_ref[...] = slots
    else:
        grads = by_slot(slots + slots_ref[...], TILE)
        out_ref[:, half:, :] = grads.astype(BF).reshape(peers, TILE, LANE)


def pair(name, gate, gate_far, up, up_far, back, back_far, gate_t, up_t, experts, slot_grads=None, kept=()):
    total, hidden = gate.shape
    width = gate_t.shape[1]
    slots = total // experts
    extra = not kept
    peers = PEERS if extra else SECOND_PEERS
    rows = width // LANE * slots + (0 if extra else TILE)
    first = 0 if extra else experts * FIRST // (peers * slots)
    block = pl.BlockSpec((peers * slots, hidden), lambda i: (i, 0))
    placed = pl.BlockSpec((peers * slots, hidden), lambda i: (first + i, 0))
    whole = pl.BlockSpec(gate_t.shape, lambda i: (0, 0))
    small = pl.BlockSpec((peers, LANE), lambda i: (i, 0))
    more = () if extra else (slot_grads, *kept)
    return pl.pallas_call(
        functools.partial(pair_kernel, extra),
        grid=(experts // peers,),
        out_shape=[jax.ShapeDtypeStruct((experts, rows, LANE), BF)]
        + [jax.ShapeDtypeStruct((experts * CAP, hidden), BF)] * 3
        + [jax.ShapeDtypeStruct((experts, LANE), F32)] * extra,
        in_specs=[block] * 6
        + [whole] * 2
        + ([] if extra else [small] + [pl.BlockSpec(memory_space=pl.ANY)] * len(kept)),
        out_specs=[pl.BlockSpec((peers, rows, LANE), lambda i: (i, 0, 0))] + [placed] * 3 + [small] * extra,
        input_output_aliases={9 + k: 1 + k for k in range(len(kept))},
        compiler_params=pltpu.CompilerParams(vmem_limit_bytes=VMEM),
        cost_estimate=pl.CostEstimate(
            flops=4 * total * width * hidden,
            bytes_accessed=2 * (total * width + 9 * total * hidden + 2 * width * hidden),
            transcendentals=total * hidden,
        ),
        name=name,
    )(gate, gate_far, up, up_far, back, back_far, gate_t, up_t, *more)


def combine_first_kernel(ids_ref, in_ref, total_ref, rank_ref, rows_ref):
    step = pl.program_id(0)
    experts = rank_ref.shape[0]
    peers, tiles = in_ref.shape[0], total_ref.shape[1] // LANE

    @pl.when(step == 0)
    def _():
        rank_ref[...] = expert_ranks(ids_ref[...], experts)
        total_ref[...] = jnp.zeros_like(total_ref)

    unpack_half(in_ref, 0, rows_ref, 0, tiles)
    unpack_extra(in_ref, tiles * HALF, rows_ref, peers * HALF)
    rank = rank_ref[pl.ds(pl.multiple_of(step * peers, peers), peers), :]
    which = jnp.concatenate([half_rows(rank, None, 0), extra_rows(rank, None)], axis=0)
    total_ref[...] += contract(which, rows_ref[...])


def combine_second_kernel(
    ids_ref, probs_ref, in_ref, slots_ref, before_ref, rank_ref, out_ref, probs_out_ref, rows_ref, total_ref
):
    step = pl.program_id(0)
    experts, tokens = rank_ref.shape
    peers, tiles = in_ref.shape[0], out_ref.shape[1] // LANE

    @pl.when(step == 0)
    def _():
        total_ref[...] = before_ref[...]
        slots = slots_ref[:, 0, :].astype(F32)
        rank = rank_ref[...]
        found = jnp.zeros((experts, tokens), F32)
        for s in range(CAP):
            found = found + jnp.where(rank == float(s), slots[:, s : s + 1], 0.0)
        ids = ids_ref[...]
        expert = iota((experts, tokens), 0)
        grads = [
            jnp.sum(jnp.where(ids[k : k + 1] == expert, found, 0.0), axis=0, keepdims=True)
            for k in range(ids.shape[0])
        ]
        probs_out_ref[...] = (jnp.concatenate(grads, axis=0) / probs_ref[...].astype(F32)).astype(BF)

    unpack_half(in_ref, 0, rows_ref, 0, tiles)
    rank = rank_ref[pl.ds(pl.multiple_of(step * peers, peers), peers), :]
    total_ref[...] += contract(half_rows(rank, None, HALF), rows_ref[...])

    @pl.when(step == pl.num_programs(0) - 1)
    def _():
        out_ref[...] = total_ref[...].astype(BF)


def combine_first(ids, got, width):
    experts, rows, _ = got.shape
    tokens = ids.shape[1]
    whole = lambda shape: pl.BlockSpec(shape, lambda i: (0, 0))
    return pl.pallas_call(
        combine_first_kernel,
        grid=(experts // PEERS,),
        out_shape=[jax.ShapeDtypeStruct((tokens, width), F32), jax.ShapeDtypeStruct((experts, tokens), F32)],
        in_specs=[whole(ids.shape), pl.BlockSpec((PEERS, rows, LANE), lambda i: (i, 0, 0))],
        out_specs=[whole((tokens, width)), whole((experts, tokens))],
        scratch_shapes=[pltpu.VMEM((PEERS * FIRST, width), BF)],
        compiler_params=pltpu.CompilerParams(vmem_limit_bytes=SUM_VMEM),
        cost_estimate=pl.CostEstimate(
            flops=2 * experts * FIRST * tokens * width, bytes_accessed=2 * experts * rows * LANE, transcendentals=0
        ),
        name="combine_a",
    )(ids, got)


def combine_second(ids, probs, got, before, rank):
    experts, rows, _ = got.shape
    tokens, width = before.shape
    whole = lambda a: pl.BlockSpec(a.shape, lambda i: (0, 0))
    return pl.pallas_call(
        combine_second_kernel,
        grid=(experts // SUM_PEERS,),
        out_shape=[jax.ShapeDtypeStruct(before.shape, BF), jax.ShapeDtypeStruct(ids.shape, BF)],
        in_specs=[
            whole(ids),
            whole(probs),
            pl.BlockSpec((SUM_PEERS, rows - TILE, LANE), lambda i: (i, 0, 0)),
            pl.BlockSpec((experts, TILE, LANE), lambda i: (0, rows // TILE - 1, 0)),
            whole(before),
            whole(rank),
        ],
        out_specs=[whole(before), whole(ids)],
        scratch_shapes=[pltpu.VMEM((SUM_PEERS * HALF, width), BF), pltpu.VMEM((tokens, width), F32)],
        compiler_params=pltpu.CompilerParams(vmem_limit_bytes=SUM_VMEM),
        cost_estimate=pl.CostEstimate(
            flops=2 * experts * HALF * tokens * width, bytes_accessed=2 * experts * rows * LANE, transcendentals=0
        ),
        name="combine_b",
    )(ids, probs, got, got, before, rank)


def exchange(x):
    return lax.all_to_all(x, ("ctx", "tp"), split_axis=0, concat_axis=0, tiled=True)


def other_core(x):
    return lax.ppermute(x, "dp", [(0, 1), (1, 0)])


def per_device(tokens, cotangent, probs, expert_ids, gate_weight, up_weight, down_weight):
    experts = lax.axis_size("ctx") * lax.axis_size("tp")
    gate_mat, up_mat, down_mat = gate_weight[0], up_weight[0], down_weight[0]
    ids, weights = expert_ids.T, probs.T
    values = (tokens, cotangent)
    mats = (gate_mat, up_mat, down_mat)
    sent_a, *done = lax.optimization_barrier(
        (
            pack("pack_a", pack_first_kernel, 2 * FIRST, 2, ids, weights, values, experts),
            *ahead("ahead_1", 1, ids, weights, mats, values, experts),
        )
    )
    got_a = exchange(sent_a)
    gate_t, up_t, down_t, sent_b = ahead("ahead_0", 0, ids, weights, mats, values, experts, done)
    sent_b, gate_t, up_t, down_t = lax.optimization_barrier((sent_b, gate_t, up_t, down_t))
    got_b = exchange(sent_b)
    mats = (gate_mat, up_mat, down_t)

    def part(name, got, slot_grads=None, kept=()):
        rows, cot_rows, gate, up, back = project("project_" + name, got, mats, kept[:2])
        far = other_core(gate), other_core(up), other_core(back)
        sent, act, gate_grad, up_grad, *slot_grads = pair(
            "pair_" + name, gate, far[0], up, far[1], back, far[2], gate_t, up_t, experts, slot_grads, kept[2:]
        )
        return sent, slot_grads, (rows, cot_rows, act, gate_grad, up_grad)

    pairs_a, (slot_grads,), kept = part("a", got_a)
    got_b, pairs_a = lax.optimization_barrier((got_b, pairs_a))
    back_a = exchange(pairs_a)
    pairs_b, _, (rows, cot_rows, act, gate_grad, up_grad) = part("b", got_b, slot_grads, kept)
    back_b = exchange(pairs_b)
    grad_down = contract(act, cot_rows).astype(BF)
    grad_gate = contract(rows, gate_grad).astype(BF)
    grad_up = contract(rows, up_grad).astype(BF)
    before, rank = combine_first(ids, back_a, tokens.shape[1])
    grad_tokens, grad_probs = combine_second(ids, weights, back_b, before, rank)
    return (grad_tokens, grad_probs.T, grad_gate[None], grad_up[None], grad_down[None])


def solution(mesh):
    return jax.shard_map(
        per_device,
        mesh=mesh,
        in_specs=(
            P(("ctx", "tp"), "dp"),
            P(("ctx", "tp"), "dp"),
            P(("ctx", "tp"), None),
            P(("ctx", "tp"), None),
            P(("ctx", "tp"), "dp", None),
            P(("ctx", "tp"), "dp", None),
            P(("ctx", "tp"), None, "dp"),
        ),
        out_specs=(
            P(("ctx", "tp"), "dp"),
            P(("ctx", "tp"), None),
            P(("ctx", "tp"), "dp", None),
            P(("ctx", "tp"), "dp", None),
            P(("ctx", "tp"), None, "dp"),
        ),
        check_vma=False,
    )
```

```python
import functools

import jax
import jax.numpy as jnp
from jax import lax
from jax.experimental import pallas as pl
from jax.experimental.pallas import tpu as pltpu
from jax.sharding import PartitionSpec as P

BF = jnp.bfloat16
F32 = jnp.float32
LANE = 128
HALF = 8
EXTRA = 2
CAP = 2 * HALF + EXTRA
FIRST = HALF + EXTRA
TILE = 16
GROUP = 16
PEERS = 32
SECOND_PEERS = 16
PACK_PEERS = 32
SUM_PEERS = 64
VMEM = 62 * 2**20
SUM_VMEM = 24 * 2**20


def iota(shape, dim):
    return lax.broadcasted_iota(jnp.int32, shape, dim)


def dot(a, b):
    return jnp.dot(a, b, preferred_element_type=F32)


def contract(left, right):
    return lax.dot_general(left, right, (((0,), (0,)), ((), ())), preferred_element_type=F32)


def expert_ranks(ids, experts):
    top, tokens = ids.shape
    expert = iota((experts, tokens), 0)
    hit = jnp.zeros((experts, tokens), F32)
    for k in range(top):
        hit = hit + jnp.where(ids[k : k + 1] == expert, 1.0, 0.0)
    earlier = jnp.where(iota((tokens, tokens), 0) < iota((tokens, tokens), 1), 1.0, 0.0)
    rank = dot(hit.astype(BF), earlier.astype(BF))
    return jnp.where(hit > 0.0, rank, -1.0)


def expert_probs(ids, probs, experts):
    top, tokens = ids.shape
    expert = iota((experts, tokens), 0)
    out = jnp.zeros((experts, tokens), F32)
    for k in range(top):
        out = out + jnp.where(ids[k : k + 1] == expert, probs[k : k + 1], 0.0)
    return out


def by_slot(a, slots):
    peers, tokens = a.shape
    return jnp.broadcast_to(a[:, None, :], (peers, slots, tokens)).reshape(peers * slots, tokens)


def extra_order(pack):
    shape = (GROUP * TILE, GROUP * TILE)
    row, col = iota(shape, 0), iota(shape, 1)
    step = GROUP * EXTRA
    if pack:
        source = (row % TILE) // EXTRA * step + row // TILE * EXTRA + row % EXTRA
    else:
        source = (row % step) // EXTRA * TILE + row // step * EXTRA + row % EXTRA
    return jnp.where(col == source, 1.0, 0.0).astype(BF)


def store_half(out_ref, start, values):
    for c in range(0, values.shape[1] // LANE, 2):
        pair = [values[:, k * LANE : (k + 1) * LANE].reshape(-1, HALF, LANE) for k in (c, c + 1)]
        at = start + c * HALF
        out_ref[:, at : at + TILE, :] = jnp.concatenate(pair, axis=1).astype(BF)


def store_extra(out_ref, start, values):
    for g in range(values.shape[1] // LANE):
        at = start + g * TILE
        out_ref[:, at : at + TILE, :] = values[:, g * LANE : (g + 1) * LANE].reshape(-1, TILE, LANE)


def order_extra(out_ref, start, values):
    groups = values.shape[1] // LANE // 8
    order = extra_order(True)
    step = GROUP * EXTRA
    parts = []
    for p in range(values.shape[0] // step):
        some = values[p * step : (p + 1) * step]
        columns = [
            jnp.concatenate([some[:, (g * 8 + c) * LANE : (g * 8 + c + 1) * LANE] for g in range(groups)], axis=1)
            for c in range(8)
        ]
        parts.append(dot(order, jnp.concatenate(columns, axis=0)).astype(BF))
    store_extra(out_ref, start, jnp.concatenate(parts, axis=0))


def unpack_half(in_ref, start, out_ref, first, count):
    rows = in_ref.shape[0] * HALF
    for c in range(0, count, 2):
        at = start + c * HALF
        pair = in_ref[:, at : at + TILE, :].astype(F32)
        for k in range(2):
            column = first + c + k
            out_ref[:rows, column * LANE : (column + 1) * LANE] = (
                pair[:, k * HALF : (k + 1) * HALF, :].reshape(rows, LANE).astype(BF)
            )


def unpack_extra(in_ref, start, out_ref, base):
    groups = out_ref.shape[1] // LANE // 8
    order = extra_order(False)
    step = GROUP * EXTRA
    for p in range(in_ref.shape[0] // GROUP):
        some = in_ref.at[p * GROUP : (p + 1) * GROUP]
        values = jnp.concatenate(
            [some[:, start + g * TILE : start + (g + 1) * TILE, :].reshape(-1, LANE) for g in range(groups)], axis=1
        )
        ordered = dot(order, values).astype(BF)
        for g in range(groups):
            for c in range(8):
                at = (g * 8 + c) * LANE
                out_ref[base + p * step : base + (p + 1) * step, at : at + LANE] = ordered[
                    c * step : (c + 1) * step, g * LANE : (g + 1) * LANE
                ]


def half_rows(rank, value, start):
    rank = by_slot(rank, HALF)
    hit = rank == (start + iota(rank.shape, 0) % HALF).astype(F32)
    return jnp.where(hit, 1.0 if value is None else by_slot(value, HALF), 0.0).astype(BF)


def extra_rows(rank, value):
    peers = rank.shape[0]
    rank = by_slot(rank, 8)
    hit = rank == (2 * HALF + iota(rank.shape, 0) % 8).astype(F32)
    eight = jnp.where(hit, 1.0 if value is None else by_slot(value, 8), 0.0).astype(BF)
    shape = (peers * EXTRA, peers * 8)
    keep = iota(shape, 1) == iota(shape, 0) // EXTRA * 8 + iota(shape, 0) % EXTRA
    return dot(jnp.where(keep, 1.0, 0.0).astype(BF), eight).astype(BF)


def wide_extra_rows(rank, value):
    rank = by_slot(rank, TILE)
    row = iota(rank.shape, 0)
    hit = rank == (2 * HALF + row % EXTRA).astype(F32)
    extra = jnp.where(hit, 1.0 if value is None else by_slot(value, TILE), 0.0)
    column = (row % TILE) // EXTRA
    return jnp.concatenate([jnp.where(column == c, extra, 0.0).astype(BF) for c in range(8)], axis=1)


def stack_columns(x_ref, side_ref):
    tokens, width = x_ref.shape
    groups = width // LANE // 8
    for c in range(8):
        for g in range(groups):
            at = (g * 8 + c) * LANE
            side_ref[c * tokens : (c + 1) * tokens, g * LANE : (g + 1) * LANE] = x_ref[:, at : at + LANE]


def pack_kernel(
    ids_ref, probs_ref, x_ref, cot_ref, out_a_ref, out_b_ref, rank_ref, prob_ref, side_ref, cot_side_ref
):
    step = pl.program_id(0)
    half = x_ref.shape[1] // LANE * HALF
    part = x_ref.shape[1] // LANE * FIRST
    count = out_a_ref.shape[0]

    @pl.when(step == 0)
    def _():
        rank_ref[...] = expert_ranks(ids_ref[...], rank_ref.shape[0])
        prob_ref[...] = expert_probs(ids_ref[...], probs_ref[...].astype(F32), rank_ref.shape[0])
        stack_columns(x_ref, side_ref)
        stack_columns(cot_ref, cot_side_ref)

    peers = pl.ds(pl.multiple_of(step * count, count), count)
    rank, prob = rank_ref[peers, :], prob_ref[peers, :]
    for n, value, ref, side in ((0, None, x_ref, side_ref), (1, prob, cot_ref, cot_side_ref)):
        store_half(out_a_ref, n * part, dot(half_rows(rank, value, 0), ref[...]))
        store_extra(out_a_ref, n * part + half, dot(wide_extra_rows(rank, value), side[...]).astype(BF))
        store_half(out_b_ref, n * half, dot(half_rows(rank, value, HALF), ref[...]))


def pack(ids, probs, x, cot, experts):
    tokens, width = x.shape
    rows = [width // LANE * 2 * slots for slots in (FIRST, HALF)]
    return pl.pallas_call(
        pack_kernel,
        grid=(experts // PACK_PEERS,),
        out_shape=[jax.ShapeDtypeStruct((experts, n, LANE), BF) for n in rows],
        in_specs=[pl.BlockSpec(a.shape, lambda i: (0, 0)) for a in (ids, probs, x, cot)],
        out_specs=[pl.BlockSpec((PACK_PEERS, n, LANE), lambda i: (i, 0, 0)) for n in rows],
        scratch_shapes=[pltpu.VMEM((experts, tokens), F32)] * 2 + [pltpu.VMEM((8 * tokens, width // 8), BF)] * 2,
        compiler_params=pltpu.CompilerParams(vmem_limit_bytes=VMEM),
        cost_estimate=pl.CostEstimate(
            flops=4 * experts * CAP * tokens * width,
            bytes_accessed=2 * experts * sum(rows) * LANE,
            transcendentals=0,
        ),
        name="pack",
    )(ids, probs, x, cot)


def turn_kernel(core, count, *refs):
    ins, outs = refs[:count], refs[-4 * count : -3 * count]
    held, turned, sems = refs[-3 * count : -2 * count], refs[-2 * count : -count], refs[-count:]

    @pl.when(lax.axis_index("dp") == core)
    def _():
        for mat, a, b, out, sem in zip(ins, held, turned, outs, sems):
            load = pltpu.make_async_copy(mat, a, sem)
            load.start()
            load.wait()
            for at in range(0, a.shape[0], 256):
                b[:, at : at + 256] = a[at : at + 256, :].T
            store = pltpu.make_async_copy(b, out, sem)
            store.start()
            store.wait()


def turn(name, core, mats, before=()):
    shapes = [m.shape for m in mats]
    anywhere = pl.BlockSpec(memory_space=pl.ANY)
    return pl.pallas_call(
        functools.partial(turn_kernel, core, len(mats)),
        out_shape=[jax.ShapeDtypeStruct(shape[::-1], BF) for shape in shapes],
        in_specs=[anywhere] * (len(mats) + len(before)),
        out_specs=[anywhere] * len(mats),
        input_output_aliases={len(mats) + k: k for k in range(len(before))},
        scratch_shapes=[pltpu.VMEM(shape, BF) for shape in shapes]
        + [pltpu.VMEM(shape[::-1], BF) for shape in shapes]
        + [pltpu.SemaphoreType.DMA] * len(mats),
        compiler_params=pltpu.CompilerParams(vmem_limit_bytes=VMEM),
        cost_estimate=pl.CostEstimate(flops=0, bytes_accessed=sum(4 * a * b for a, b in shapes), transcendentals=0),
        name=name,
    )(*mats, *before)


def project_kernel(extra, x_in, cot_in, gate_w, up_w, down_w, *refs):
    x_ref, cot_ref, gate_ref, up_ref, back_ref = refs[-5:]
    peers = x_in.shape[0]
    tiles = x_ref.shape[1] // LANE
    for in_ref, rows_ref in ((x_in, x_ref), (cot_in, cot_ref)):
        unpack_half(in_ref, 0, rows_ref, 0, tiles)
        if extra:
            unpack_extra(in_ref, tiles * HALF, rows_ref, peers * HALF)
    gate_ref[...] = dot(x_ref[...], gate_w[...]).astype(BF)
    up_ref[...] = dot(x_ref[...], up_w[...]).astype(BF)
    back_ref[...] = dot(cot_ref[...], down_w[...]).astype(BF)


def project(name, got, weights, kept=()):
    experts, both, _ = got.shape
    width, hidden = weights[0].shape
    part = both // 2
    slots = part * LANE // width
    peers = SECOND_PEERS if kept else PEERS
    total, rows = experts * slots, peers * slots
    first = experts * FIRST // rows if kept else 0
    whole = experts * CAP
    return pl.pallas_call(
        functools.partial(project_kernel, not kept),
        grid=(experts // peers,),
        out_shape=[jax.ShapeDtypeStruct((whole, width), BF)] * 2 + [jax.ShapeDtypeStruct((total, hidden), BF)] * 3,
        in_specs=[pl.BlockSpec((peers, part, LANE), lambda i, at=at: (i, at, 0)) for at in range(2)]
        + [pl.BlockSpec(w.shape, lambda i: (0, 0)) for w in weights]
        + [pl.BlockSpec(memory_space=pl.ANY) for _ in kept],
        out_specs=[pl.BlockSpec((rows, width), lambda i: (first + i, 0))] * 2
        + [pl.BlockSpec((rows, hidden), lambda i: (i, 0))] * 3,
        input_output_aliases={5 + k: k for k in range(len(kept))},
        compiler_params=pltpu.CompilerParams(vmem_limit_bytes=VMEM),
        cost_estimate=pl.CostEstimate(
            flops=6 * total * width * hidden,
            bytes_accessed=2 * (4 * total * width + 3 * (width + total) * hidden),
            transcendentals=0,
        ),
        name=name,
    )(got, got, *weights, *kept)


def slots_of(prob_grad, peers, extra):
    total = prob_grad.shape[0]
    main = peers * HALF
    row, lane = iota((total, LANE), 0), iota((total, LANE), 1)
    peer, of = iota((peers, total), 0), iota((peers, total), 1)
    slot, owner = row % HALF, of // HALF
    if extra:
        slot = jnp.where(row < main, slot, 2 * HALF + row % EXTRA)
        owner = jnp.where(of < main, owner, (of - main) // EXTRA)
    else:
        slot = slot + HALF
    by_lane = jnp.where(lane == slot, prob_grad, 0.0).astype(BF)
    return dot(jnp.where(peer == owner, 1.0, 0.0).astype(BF), by_lane)


def pair_kernel(extra, *refs):
    if extra:
        *refs, out_ref, act_ref, gg_ref, ug_ref, slots_out_ref = refs
    else:
        *refs, slots_ref, _, _, _, out_ref, act_ref, gg_ref, ug_ref = refs
    gate, gate_far, up, up_far, back, back_far, gate_t, up_t = refs
    g = gate[...].astype(F32) + gate_far[...].astype(F32)
    u = up[...].astype(F32) + up_far[...].astype(F32)
    b = back[...].astype(F32) + back_far[...].astype(F32)
    sigmoid = jax.nn.sigmoid(g)
    silu = g * sigmoid
    act = silu * u
    act_ref[...] = act.astype(BF)
    gg_ref[...] = (b * u * sigmoid * (1.0 + g * (1.0 - sigmoid))).astype(BF)
    ug_ref[...] = (b * silu).astype(BF)
    prob_grad = jnp.sum(act * b, axis=1, keepdims=True)
    y = dot(gg_ref[...], gate_t[...]) + dot(ug_ref[...], up_t[...])
    half = y.shape[1] // LANE * HALF
    peers = out_ref.shape[0]
    main = peers * HALF
    store_half(out_ref, 0, y[:main])
    slots = slots_of(prob_grad, peers, extra)
    if extra:
        order_extra(out_ref, half, y[main:].astype(BF))
        slots_out_ref[...] = slots
    else:
        grads = by_slot(slots + slots_ref[...], TILE)
        out_ref[:, half:, :] = grads.astype(BF).reshape(peers, TILE, LANE)


def pair(name, gate, gate_far, up, up_far, back, back_far, gate_t, up_t, experts, slot_grads=None, kept=()):
    total, hidden = gate.shape
    width = gate_t.shape[1]
    slots = total // experts
    extra = not kept
    peers = PEERS if extra else SECOND_PEERS
    rows = width // LANE * slots + (0 if extra else TILE)
    first = 0 if extra else experts * FIRST // (peers * slots)
    block = pl.BlockSpec((peers * slots, hidden), lambda i: (i, 0))
    placed = pl.BlockSpec((peers * slots, hidden), lambda i: (first + i, 0))
    whole = pl.BlockSpec(gate_t.shape, lambda i: (0, 0))
    small = pl.BlockSpec((peers, LANE), lambda i: (i, 0))
    more = () if extra else (slot_grads, *kept)
    return pl.pallas_call(
        functools.partial(pair_kernel, extra),
        grid=(experts // peers,),
        out_shape=[jax.ShapeDtypeStruct((experts, rows, LANE), BF)]
        + [jax.ShapeDtypeStruct((experts * CAP, hidden), BF)] * 3
        + [jax.ShapeDtypeStruct((experts, LANE), F32)] * extra,
        in_specs=[block] * 6
        + [whole] * 2
        + ([] if extra else [small] + [pl.BlockSpec(memory_space=pl.ANY)] * len(kept)),
        out_specs=[pl.BlockSpec((peers, rows, LANE), lambda i: (i, 0, 0))] + [placed] * 3 + [small] * extra,
        input_output_aliases={9 + k: 1 + k for k in range(len(kept))},
        compiler_params=pltpu.CompilerParams(vmem_limit_bytes=VMEM),
        cost_estimate=pl.CostEstimate(
            flops=4 * total * width * hidden,
            bytes_accessed=2 * (total * width + 9 * total * hidden + 2 * width * hidden),
            transcendentals=total * hidden,
        ),
        name=name,
    )(gate, gate_far, up, up_far, back, back_far, gate_t, up_t, *more)


def combine_first_kernel(ids_ref, in_ref, total_ref, rank_ref, rows_ref):
    step = pl.program_id(0)
    experts = rank_ref.shape[0]
    peers, tiles = in_ref.shape[0], total_ref.shape[1] // LANE

    @pl.when(step == 0)
    def _():
        rank_ref[...] = expert_ranks(ids_ref[...], experts)
        total_ref[...] = jnp.zeros_like(total_ref)

    unpack_half(in_ref, 0, rows_ref, 0, tiles)
    unpack_extra(in_ref, tiles * HALF, rows_ref, peers * HALF)
    rank = rank_ref[pl.ds(pl.multiple_of(step * peers, peers), peers), :]
    which = jnp.concatenate([half_rows(rank, None, 0), extra_rows(rank, None)], axis=0)
    total_ref[...] += contract(which, rows_ref[...])


def combine_second_kernel(
    ids_ref, probs_ref, in_ref, slots_ref, before_ref, rank_ref, out_ref, probs_out_ref, rows_ref, total_ref
):
    step = pl.program_id(0)
    experts, tokens = rank_ref.shape
    peers, tiles = in_ref.shape[0], out_ref.shape[1] // LANE

    @pl.when(step == 0)
    def _():
        total_ref[...] = before_ref[...]
        slots = slots_ref[:, 0, :].astype(F32)
        rank = rank_ref[...]
        found = jnp.zeros((experts, tokens), F32)
        for s in range(CAP):
            found = found + jnp.where(rank == float(s), slots[:, s : s + 1], 0.0)
        ids = ids_ref[...]
        expert = iota((experts, tokens), 0)
        grads = [
            jnp.sum(jnp.where(ids[k : k + 1] == expert, found, 0.0), axis=0, keepdims=True)
            for k in range(ids.shape[0])
        ]
        probs_out_ref[...] = (jnp.concatenate(grads, axis=0) / probs_ref[...].astype(F32)).astype(BF)

    unpack_half(in_ref, 0, rows_ref, 0, tiles)
    rank = rank_ref[pl.ds(pl.multiple_of(step * peers, peers), peers), :]
    total_ref[...] += contract(half_rows(rank, None, HALF), rows_ref[...])

    @pl.when(step == pl.num_programs(0) - 1)
    def _():
        out_ref[...] = total_ref[...].astype(BF)


def combine_first(ids, got, width):
    experts, rows, _ = got.shape
    tokens = ids.shape[1]
    whole = lambda shape: pl.BlockSpec(shape, lambda i: (0, 0))
    return pl.pallas_call(
        combine_first_kernel,
        grid=(experts // PEERS,),
        out_shape=[jax.ShapeDtypeStruct((tokens, width), F32), jax.ShapeDtypeStruct((experts, tokens), F32)],
        in_specs=[whole(ids.shape), pl.BlockSpec((PEERS, rows, LANE), lambda i: (i, 0, 0))],
        out_specs=[whole((tokens, width)), whole((experts, tokens))],
        scratch_shapes=[pltpu.VMEM((PEERS * FIRST, width), BF)],
        compiler_params=pltpu.CompilerParams(vmem_limit_bytes=SUM_VMEM),
        cost_estimate=pl.CostEstimate(
            flops=2 * experts * FIRST * tokens * width, bytes_accessed=2 * experts * rows * LANE, transcendentals=0
        ),
        name="combine_a",
    )(ids, got)


def combine_second(ids, probs, got, before, rank):
    experts, rows, _ = got.shape
    tokens, width = before.shape
    whole = lambda a: pl.BlockSpec(a.shape, lambda i: (0, 0))
    return pl.pallas_call(
        combine_second_kernel,
        grid=(experts // SUM_PEERS,),
        out_shape=[jax.ShapeDtypeStruct(before.shape, BF), jax.ShapeDtypeStruct(ids.shape, BF)],
        in_specs=[
            whole(ids),
            whole(probs),
            pl.BlockSpec((SUM_PEERS, rows - TILE, LANE), lambda i: (i, 0, 0)),
            pl.BlockSpec((experts, TILE, LANE), lambda i: (0, rows // TILE - 1, 0)),
            whole(before),
            whole(rank),
        ],
        out_specs=[whole(before), whole(ids)],
        scratch_shapes=[pltpu.VMEM((SUM_PEERS * HALF, width), BF), pltpu.VMEM((tokens, width), F32)],
        compiler_params=pltpu.CompilerParams(vmem_limit_bytes=SUM_VMEM),
        cost_estimate=pl.CostEstimate(
            flops=2 * experts * HALF * tokens * width, bytes_accessed=2 * experts * rows * LANE, transcendentals=0
        ),
        name="combine_b",
    )(ids, probs, got, got, before, rank)


def exchange(x):
    return lax.all_to_all(x, ("ctx", "tp"), split_axis=0, concat_axis=0, tiled=True)


def other_core(x):
    return lax.ppermute(x, "dp", [(0, 1), (1, 0)])


def per_device(tokens, cotangent, probs, expert_ids, gate_weight, up_weight, down_weight):
    experts = lax.axis_size("ctx") * lax.axis_size("tp")
    gate_mat, up_mat, down_mat = gate_weight[0], up_weight[0], down_weight[0]
    ids, weights = expert_ids.T, probs.T
    mats = (gate_mat, up_mat, down_mat)
    sent_a, sent_b, *turned = lax.optimization_barrier(
        (*pack(ids, weights, tokens, cotangent, experts), *turn("turn_1", 1, mats))
    )
    got_a, sent_b, turned, mats = lax.optimization_barrier((exchange(sent_a), sent_b, turned, mats))
    got_b = exchange(sent_b)
    gate_t, up_t, down_t = turn("turn_0", 0, mats, turned)
    mats = (gate_mat, up_mat, down_t)

    def part(name, got, slot_grads=None, kept=()):
        rows, cot_rows, gate, up, back = project("project_" + name, got, mats, kept[:2])
        far = other_core(gate), other_core(up), other_core(back)
        sent, act, gate_grad, up_grad, *slot_grads = pair(
            "pair_" + name, gate, far[0], up, far[1], back, far[2], gate_t, up_t, experts, slot_grads, kept[2:]
        )
        return sent, slot_grads, (rows, cot_rows, act, gate_grad, up_grad)

    pairs_a, (slot_grads,), kept = part("a", got_a)
    got_b, pairs_a = lax.optimization_barrier((got_b, pairs_a))
    back_a = exchange(pairs_a)
    pairs_b, _, (rows, cot_rows, act, gate_grad, up_grad) = part("b", got_b, slot_grads, kept)
    back_b = exchange(pairs_b)
    grad_down = contract(act, cot_rows).astype(BF)
    grad_gate = contract(rows, gate_grad).astype(BF)
    grad_up = contract(rows, up_grad).astype(BF)
    before, rank = combine_first(ids, back_a, tokens.shape[1])
    grad_tokens, grad_probs = combine_second(ids, weights, back_b, before, rank)
    return (grad_tokens, grad_probs.T, grad_gate[None], grad_up[None], grad_down[None])


def solution(mesh):
    return jax.shard_map(
        per_device,
        mesh=mesh,
        in_specs=(
            P(("ctx", "tp"), "dp"),
            P(("ctx", "tp"), "dp"),
            P(("ctx", "tp"), None),
            P(("ctx", "tp"), None),
            P(("ctx", "tp"), "dp", None),
            P(("ctx", "tp"), "dp", None),
            P(("ctx", "tp"), None, "dp"),
        ),
        out_specs=(
            P(("ctx", "tp"), "dp"),
            P(("ctx", "tp"), None),
            P(("ctx", "tp"), "dp", None),
            P(("ctx", "tp"), "dp", None),
            P(("ctx", "tp"), None, "dp"),
        ),
        check_vma=False,
    )
```

```python
import functools

import jax
import jax.numpy as jnp
from jax import lax
from jax.experimental import pallas as pl
from jax.experimental.pallas import tpu as pltpu
from jax.sharding import PartitionSpec as P

BF = jnp.bfloat16
F32 = jnp.float32
LANE = 128
HALF = 8
EXTRA = 2
CAP = 2 * HALF + EXTRA
FIRST = HALF + EXTRA
TILE = 16
GROUP = 16
PEERS = 32
SECOND_PEERS = 16
PACK_PEERS = 32
SUM_PEERS = 64
VMEM = 62 * 2**20
SUM_VMEM = 24 * 2**20


def iota(shape, dim):
    return lax.broadcasted_iota(jnp.int32, shape, dim)


def dot(a, b):
    return jnp.dot(a, b, preferred_element_type=F32)


def contract(left, right):
    return lax.dot_general(left, right, (((0,), (0,)), ((), ())), preferred_element_type=F32)


def expert_ranks(ids, experts):
    top, tokens = ids.shape
    expert = iota((experts, tokens), 0)
    hit = jnp.zeros((experts, tokens), F32)
    for k in range(top):
        hit = hit + jnp.where(ids[k : k + 1] == expert, 1.0, 0.0)
    earlier = jnp.where(iota((tokens, tokens), 0) < iota((tokens, tokens), 1), 1.0, 0.0)
    rank = dot(hit.astype(BF), earlier.astype(BF))
    return jnp.where(hit > 0.0, rank, -1.0)


def expert_probs(ids, probs, experts):
    top, tokens = ids.shape
    expert = iota((experts, tokens), 0)
    out = jnp.zeros((experts, tokens), F32)
    for k in range(top):
        out = out + jnp.where(ids[k : k + 1] == expert, probs[k : k + 1], 0.0)
    return out


def by_slot(a, slots):
    peers, tokens = a.shape
    return jnp.broadcast_to(a[:, None, :], (peers, slots, tokens)).reshape(peers * slots, tokens)


def extra_order(pack):
    shape = (GROUP * TILE, GROUP * TILE)
    row, col = iota(shape, 0), iota(shape, 1)
    step = GROUP * EXTRA
    if pack:
        source = (row % TILE) // EXTRA * step + row // TILE * EXTRA + row % EXTRA
    else:
        source = (row % step) // EXTRA * TILE + row // step * EXTRA + row % EXTRA
    return jnp.where(col == source, 1.0, 0.0).astype(BF)


def store_half(out_ref, start, values):
    for c in range(0, values.shape[1] // LANE, 2):
        pair = [values[:, k * LANE : (k + 1) * LANE].reshape(-1, HALF, LANE) for k in (c, c + 1)]
        at = start + c * HALF
        out_ref[:, at : at + TILE, :] = jnp.concatenate(pair, axis=1).astype(BF)


def store_extra(out_ref, start, values):
    for g in range(values.shape[1] // LANE):
        at = start + g * TILE
        out_ref[:, at : at + TILE, :] = values[:, g * LANE : (g + 1) * LANE].reshape(-1, TILE, LANE)


def order_extra(out_ref, start, values):
    groups = values.shape[1] // LANE // 8
    order = extra_order(True)
    step = GROUP * EXTRA
    parts = []
    for p in range(values.shape[0] // step):
        some = values[p * step : (p + 1) * step]
        columns = [
            jnp.concatenate([some[:, (g * 8 + c) * LANE : (g * 8 + c + 1) * LANE] for g in range(groups)], axis=1)
            for c in range(8)
        ]
        parts.append(dot(order, jnp.concatenate(columns, axis=0)).astype(BF))
    store_extra(out_ref, start, jnp.concatenate(parts, axis=0))


def unpack_half(in_ref, start, out_ref, first, count):
    rows = in_ref.shape[0] * HALF
    for c in range(0, count, 2):
        at = start + c * HALF
        pair = in_ref[:, at : at + TILE, :].astype(F32)
        for k in range(2):
            column = first + c + k
            out_ref[:rows, column * LANE : (column + 1) * LANE] = (
                pair[:, k * HALF : (k + 1) * HALF, :].reshape(rows, LANE).astype(BF)
            )


def unpack_extra(in_ref, start, out_ref, base):
    groups = out_ref.shape[1] // LANE // 8
    order = extra_order(False)
    step = GROUP * EXTRA
    for p in range(in_ref.shape[0] // GROUP):
        some = in_ref.at[p * GROUP : (p + 1) * GROUP]
        values = jnp.concatenate(
            [some[:, start + g * TILE : start + (g + 1) * TILE, :].reshape(-1, LANE) for g in range(groups)], axis=1
        )
        ordered = dot(order, values).astype(BF)
        for g in range(groups):
            for c in range(8):
                at = (g * 8 + c) * LANE
                out_ref[base + p * step : base + (p + 1) * step, at : at + LANE] = ordered[
                    c * step : (c + 1) * step, g * LANE : (g + 1) * LANE
                ]


def half_rows(rank, value, start):
    rank = by_slot(rank, HALF)
    hit = rank == (start + iota(rank.shape, 0) % HALF).astype(F32)
    return jnp.where(hit, 1.0 if value is None else by_slot(value, HALF), 0.0).astype(BF)


def extra_rows(rank, value):
    peers = rank.shape[0]
    rank = by_slot(rank, 8)
    hit = rank == (2 * HALF + iota(rank.shape, 0) % 8).astype(F32)
    eight = jnp.where(hit, 1.0 if value is None else by_slot(value, 8), 0.0).astype(BF)
    shape = (peers * EXTRA, peers * 8)
    keep = iota(shape, 1) == iota(shape, 0) // EXTRA * 8 + iota(shape, 0) % EXTRA
    return dot(jnp.where(keep, 1.0, 0.0).astype(BF), eight).astype(BF)


def wide_extra_rows(rank, value):
    rank = by_slot(rank, TILE)
    row = iota(rank.shape, 0)
    hit = rank == (2 * HALF + row % EXTRA).astype(F32)
    extra = jnp.where(hit, 1.0 if value is None else by_slot(value, TILE), 0.0)
    column = (row % TILE) // EXTRA
    return jnp.concatenate([jnp.where(column == c, extra, 0.0).astype(BF) for c in range(8)], axis=1)


def stack_columns(x_ref, side_ref):
    tokens, width = x_ref.shape
    groups = width // LANE // 8
    for c in range(8):
        for g in range(groups):
            at = (g * 8 + c) * LANE
            side_ref[c * tokens : (c + 1) * tokens, g * LANE : (g + 1) * LANE] = x_ref[:, at : at + LANE]


def start_pack(ids_ref, probs_ref, rank_ref, prob_ref):
    experts = rank_ref.shape[0]
    rank_ref[...] = expert_ranks(ids_ref[...], experts)
    prob_ref[...] = expert_probs(ids_ref[...], probs_ref[...].astype(F32), experts)


def pack_first_kernel(ids_ref, probs_ref, x_ref, cot_ref, out_ref, rank_ref, prob_ref, side_ref, cot_side_ref):
    step = pl.program_id(0)
    half = x_ref.shape[1] // LANE * HALF
    part = x_ref.shape[1] // LANE * FIRST
    count = out_ref.shape[0]

    @pl.when(step == 0)
    def _():
        start_pack(ids_ref, probs_ref, rank_ref, prob_ref)
        stack_columns(x_ref, side_ref)
        stack_columns(cot_ref, cot_side_ref)

    peers = pl.ds(pl.multiple_of(step * count, count), count)
    rank, prob = rank_ref[peers, :], prob_ref[peers, :]
    for start, value, ref, side in ((0, None, x_ref, side_ref), (part, prob, cot_ref, cot_side_ref)):
        store_half(out_ref, start, dot(half_rows(rank, value, 0), ref[...]))
        store_extra(out_ref, start + half, dot(wide_extra_rows(rank, value), side[...]).astype(BF))


def pack(name, kernel, slots, sides, ids, probs, values, experts):
    tokens, width = values[0].shape
    rows = width // LANE * slots
    return pl.pallas_call(
        kernel,
        grid=(experts // PACK_PEERS,),
        out_shape=jax.ShapeDtypeStruct((experts, rows, LANE), BF),
        in_specs=[pl.BlockSpec(a.shape, lambda i: (0, 0)) for a in (ids, probs, *values)],
        out_specs=pl.BlockSpec((PACK_PEERS, rows, LANE), lambda i: (i, 0, 0)),
        scratch_shapes=[pltpu.VMEM((experts, tokens), F32)] * 2 + [pltpu.VMEM((8 * tokens, width // 8), BF)] * sides,
        compiler_params=pltpu.CompilerParams(vmem_limit_bytes=VMEM),
        cost_estimate=pl.CostEstimate(
            flops=4 * experts * slots * tokens * width, bytes_accessed=2 * experts * rows * LANE, transcendentals=0
        ),
        name=name,
    )(ids, probs, *values)


def ahead_kernel(core, count, ids_ref, probs_ref, *refs):
    mats, (x_ref, cot_ref), refs = refs[:count], refs[count : count + 2], refs[-(4 * count + 9) :]
    outs, out_ref, refs = refs[:count], refs[count], refs[count + 1 :]
    held, turned, refs = refs[:count], refs[count : 2 * count], refs[2 * count :]
    x, cot, packed, rank_ref, prob_ref = refs[:5]
    mat_sems, x_sem, cot_sem, pack_sems = refs[5 : 5 + count], refs[5 + count], refs[6 + count], refs[7 + count]
    experts = out_ref.shape[0]

    @pl.when(lax.axis_index("dp") == core)
    def _():
        values = [pltpu.make_async_copy(x_ref, x, x_sem), pltpu.make_async_copy(cot_ref, cot, cot_sem)]
        for copy in values:
            copy.start()
        for mat, a, b, out, sem in zip(mats, held, turned, outs, mat_sems):
            load = pltpu.make_async_copy(mat, a, sem)
            load.start()
            load.wait()
            for at in range(0, a.shape[0], 256):
                b[:, at : at + 256] = a[at : at + 256, :].T
            store = pltpu.make_async_copy(b, out, sem)
            store.start()
            store.wait()
        for copy in values:
            copy.wait()
        start_pack(ids_ref, probs_ref, rank_ref, prob_ref)
        half = x.shape[1] // LANE * HALF
        stores = []
        for n in range(experts // PACK_PEERS):
            peers = pl.ds(n * PACK_PEERS, PACK_PEERS)
            rank, prob = rank_ref[peers, :], prob_ref[peers, :]
            slot = packed.at[n]
            store_half(slot, 0, dot(half_rows(rank, None, HALF), x[...]))
            store_half(slot, half, dot(half_rows(rank, prob, HALF), cot[...]))
            stores.append(pltpu.make_async_copy(slot, out_ref.at[peers], pack_sems.at[n]))
            stores[-1].start()
        for store in stores:
            store.wait()


def ahead(name, core, ids, probs, mats, values, experts, before=()):
    tokens, width = values[0].shape
    rows = width // LANE * 2 * HALF
    steps = experts // PACK_PEERS
    shapes = [m.shape for m in mats]
    outs = [shape[::-1] for shape in shapes] + [(experts, rows, LANE)]
    anywhere = pl.BlockSpec(memory_space=pl.ANY)
    given = (*mats, *values, *before)
    return pl.pallas_call(
        functools.partial(ahead_kernel, core, len(mats)),
        out_shape=[jax.ShapeDtypeStruct(shape, BF) for shape in outs],
        in_specs=[pl.BlockSpec(memory_space=pltpu.VMEM)] * 2 + [anywhere] * len(given),
        out_specs=[anywhere] * len(outs),
        input_output_aliases={2 + len(given) - len(before) + k: k for k in range(len(before))},
        scratch_shapes=[pltpu.VMEM(shape, BF) for shape in shapes]
        + [pltpu.VMEM(shape[::-1], BF) for shape in shapes]
        + [pltpu.VMEM((tokens, width), BF)] * 2
        + [pltpu.VMEM((steps, PACK_PEERS, rows, LANE), BF)]
        + [pltpu.VMEM((experts, tokens), F32)] * 2
        + [pltpu.SemaphoreType.DMA] * (len(mats) + 2)
        + [pltpu.SemaphoreType.DMA((steps,))],
        compiler_params=pltpu.CompilerParams(vmem_limit_bytes=VMEM),
        cost_estimate=pl.CostEstimate(
            flops=4 * experts * HALF * tokens * width,
            bytes_accessed=sum(8 * a * b for a, b in shapes) + 2 * experts * rows * LANE,
            transcendentals=0,
        ),
        name=name,
    )(ids, probs, *given)


def turn_kernel(core, count, *refs):
    ins, outs = refs[:count], refs[-4 * count : -3 * count]
    held, turned, sems = refs[-3 * count : -2 * count], refs[-2 * count : -count], refs[-count:]

    @pl.when(lax.axis_index("dp") == core)
    def _():
        for mat, a, b, out, sem in zip(ins, held, turned, outs, sems):
            load = pltpu.make_async_copy(mat, a, sem)
            load.start()
            load.wait()
            for at in range(0, a.shape[0], 256):
                b[:, at : at + 256] = a[at : at + 256, :].T
            store = pltpu.make_async_copy(b, out, sem)
            store.start()
            store.wait()


def turn(name, core, mats, before=()):
    shapes = [m.shape for m in mats]
    anywhere = pl.BlockSpec(memory_space=pl.ANY)
    return pl.pallas_call(
        functools.partial(turn_kernel, core, len(mats)),
        out_shape=[jax.ShapeDtypeStruct(shape[::-1], BF) for shape in shapes],
        in_specs=[anywhere] * (len(mats) + len(before)),
        out_specs=[anywhere] * len(mats),
        input_output_aliases={len(mats) + k: k for k in range(len(before))},
        scratch_shapes=[pltpu.VMEM(shape, BF) for shape in shapes]
        + [pltpu.VMEM(shape[::-1], BF) for shape in shapes]
        + [pltpu.SemaphoreType.DMA] * len(mats),
        compiler_params=pltpu.CompilerParams(vmem_limit_bytes=VMEM),
        cost_estimate=pl.CostEstimate(flops=0, bytes_accessed=sum(4 * a * b for a, b in shapes), transcendentals=0),
        name=name,
    )(*mats, *before)


def project_kernel(extra, x_in, cot_in, gate_w, up_w, down_w, *refs):
    x_ref, cot_ref, gate_ref, up_ref, back_ref = refs[-5:]
    peers = x_in.shape[0]
    tiles = x_ref.shape[1] // LANE
    for in_ref, rows_ref in ((x_in, x_ref), (cot_in, cot_ref)):
        unpack_half(in_ref, 0, rows_ref, 0, tiles)
        if extra:
            unpack_extra(in_ref, tiles * HALF, rows_ref, peers * HALF)
    gate_ref[...] = dot(x_ref[...], gate_w[...]).astype(BF)
    up_ref[...] = dot(x_ref[...], up_w[...]).astype(BF)
    back_ref[...] = dot(cot_ref[...], down_w[...]).astype(BF)


def project(name, got, weights, kept=()):
    experts, both, _ = got.shape
    width, hidden = weights[0].shape
    part = both // 2
    slots = part * LANE // width
    peers = SECOND_PEERS if kept else PEERS
    total, rows = experts * slots, peers * slots
    first = experts * FIRST // rows if kept else 0
    whole = experts * CAP
    return pl.pallas_call(
        functools.partial(project_kernel, not kept),
        grid=(experts // peers,),
        out_shape=[jax.ShapeDtypeStruct((whole, width), BF)] * 2 + [jax.ShapeDtypeStruct((total, hidden), BF)] * 3,
        in_specs=[pl.BlockSpec((peers, part, LANE), lambda i, at=at: (i, at, 0)) for at in range(2)]
        + [pl.BlockSpec(w.shape, lambda i: (0, 0)) for w in weights]
        + [pl.BlockSpec(memory_space=pl.ANY) for _ in kept],
        out_specs=[pl.BlockSpec((rows, width), lambda i: (first + i, 0))] * 2
        + [pl.BlockSpec((rows, hidden), lambda i: (i, 0))] * 3,
        input_output_aliases={5 + k: k for k in range(len(kept))},
        compiler_params=pltpu.CompilerParams(vmem_limit_bytes=VMEM),
        cost_estimate=pl.CostEstimate(
            flops=6 * total * width * hidden,
            bytes_accessed=2 * (4 * total * width + 3 * (width + total) * hidden),
            transcendentals=0,
        ),
        name=name,
    )(got, got, *weights, *kept)


def slots_of(prob_grad, peers, extra):
    total = prob_grad.shape[0]
    main = peers * HALF
    row, lane = iota((total, LANE), 0), iota((total, LANE), 1)
    peer, of = iota((peers, total), 0), iota((peers, total), 1)
    slot, owner = row % HALF, of // HALF
    if extra:
        slot = jnp.where(row < main, slot, 2 * HALF + row % EXTRA)
        owner = jnp.where(of < main, owner, (of - main) // EXTRA)
    else:
        slot = slot + HALF
    by_lane = jnp.where(lane == slot, prob_grad, 0.0).astype(BF)
    return dot(jnp.where(peer == owner, 1.0, 0.0).astype(BF), by_lane)


def pair_kernel(extra, *refs):
    if extra:
        *refs, out_ref, act_ref, gg_ref, ug_ref, slots_out_ref = refs
    else:
        *refs, slots_ref, _, _, _, out_ref, act_ref, gg_ref, ug_ref = refs
    gate, gate_far, up, up_far, back, back_far, gate_t, up_t = refs
    g = gate[...].astype(F32) + gate_far[...].astype(F32)
    u = up[...].astype(F32) + up_far[...].astype(F32)
    b = back[...].astype(F32) + back_far[...].astype(F32)
    sigmoid = jax.nn.sigmoid(g)
    silu = g * sigmoid
    act = silu * u
    act_ref[...] = act.astype(BF)
    gg_ref[...] = (b * u * sigmoid * (1.0 + g * (1.0 - sigmoid))).astype(BF)
    ug_ref[...] = (b * silu).astype(BF)
    prob_grad = jnp.sum(act * b, axis=1, keepdims=True)
    y = dot(gg_ref[...], gate_t[...]) + dot(ug_ref[...], up_t[...])
    half = y.shape[1] // LANE * HALF
    peers = out_ref.shape[0]
    main = peers * HALF
    store_half(out_ref, 0, y[:main])
    slots = slots_of(prob_grad, peers, extra)
    if extra:
        order_extra(out_ref, half, y[main:].astype(BF))
        slots_out_ref[...] = slots
    else:
        grads = by_slot(slots + slots_ref[...], TILE)
        out_ref[:, half:, :] = grads.astype(BF).reshape(peers, TILE, LANE)


def pair(name, gate, gate_far, up, up_far, back, back_far, gate_t, up_t, experts, slot_grads=None, kept=()):
    total, hidden = gate.shape
    width = gate_t.shape[1]
    slots = total // experts
    extra = not kept
    peers = PEERS if extra else SECOND_PEERS
    rows = width // LANE * slots + (0 if extra else TILE)
    first = 0 if extra else experts * FIRST // (peers * slots)
    block = pl.BlockSpec((peers * slots, hidden), lambda i: (i, 0))
    placed = pl.BlockSpec((peers * slots, hidden), lambda i: (first + i, 0))
    whole = pl.BlockSpec(gate_t.shape, lambda i: (0, 0))
    small = pl.BlockSpec((peers, LANE), lambda i: (i, 0))
    more = () if extra else (slot_grads, *kept)
    return pl.pallas_call(
        functools.partial(pair_kernel, extra),
        grid=(experts // peers,),
        out_shape=[jax.ShapeDtypeStruct((experts, rows, LANE), BF)]
        + [jax.ShapeDtypeStruct((experts * CAP, hidden), BF)] * 3
        + [jax.ShapeDtypeStruct((experts, LANE), F32)] * extra,
        in_specs=[block] * 6
        + [whole] * 2
        + ([] if extra else [small] + [pl.BlockSpec(memory_space=pl.ANY)] * len(kept)),
        out_specs=[pl.BlockSpec((peers, rows, LANE), lambda i: (i, 0, 0))] + [placed] * 3 + [small] * extra,
        input_output_aliases={9 + k: 1 + k for k in range(len(kept))},
        compiler_params=pltpu.CompilerParams(vmem_limit_bytes=VMEM),
        cost_estimate=pl.CostEstimate(
            flops=4 * total * width * hidden,
            bytes_accessed=2 * (total * width + 9 * total * hidden + 2 * width * hidden),
            transcendentals=total * hidden,
        ),
        name=name,
    )(gate, gate_far, up, up_far, back, back_far, gate_t, up_t, *more)


def combine_first_kernel(ids_ref, in_ref, total_ref, rank_ref, rows_ref):
    step = pl.program_id(0)
    experts = rank_ref.shape[0]
    peers, tiles = in_ref.shape[0], total_ref.shape[1] // LANE

    @pl.when(step == 0)
    def _():
        rank_ref[...] = expert_ranks(ids_ref[...], experts)
        total_ref[...] = jnp.zeros_like(total_ref)

    unpack_half(in_ref, 0, rows_ref, 0, tiles)
    unpack_extra(in_ref, tiles * HALF, rows_ref, peers * HALF)
    rank = rank_ref[pl.ds(pl.multiple_of(step * peers, peers), peers), :]
    which = jnp.concatenate([half_rows(rank, None, 0), extra_rows(rank, None)], axis=0)
    total_ref[...] += contract(which, rows_ref[...])


def combine_second_kernel(
    ids_ref, probs_ref, in_ref, slots_ref, before_ref, rank_ref, out_ref, probs_out_ref, rows_ref, total_ref
):
    step = pl.program_id(0)
    experts, tokens = rank_ref.shape
    peers, tiles = in_ref.shape[0], out_ref.shape[1] // LANE

    @pl.when(step == 0)
    def _():
        total_ref[...] = before_ref[...]
        slots = slots_ref[:, 0, :].astype(F32)
        rank = rank_ref[...]
        found = jnp.zeros((experts, tokens), F32)
        for s in range(CAP):
            found = found + jnp.where(rank == float(s), slots[:, s : s + 1], 0.0)
        ids = ids_ref[...]
        expert = iota((experts, tokens), 0)
        grads = [
            jnp.sum(jnp.where(ids[k : k + 1] == expert, found, 0.0), axis=0, keepdims=True)
            for k in range(ids.shape[0])
        ]
        probs_out_ref[...] = (jnp.concatenate(grads, axis=0) / probs_ref[...].astype(F32)).astype(BF)

    unpack_half(in_ref, 0, rows_ref, 0, tiles)
    rank = rank_ref[pl.ds(pl.multiple_of(step * peers, peers), peers), :]
    total_ref[...] += contract(half_rows(rank, None, HALF), rows_ref[...])

    @pl.when(step == pl.num_programs(0) - 1)
    def _():
        out_ref[...] = total_ref[...].astype(BF)


def combine_first(ids, got, width):
    experts, rows, _ = got.shape
    tokens = ids.shape[1]
    whole = lambda shape: pl.BlockSpec(shape, lambda i: (0, 0))
    return pl.pallas_call(
        combine_first_kernel,
        grid=(experts // PEERS,),
        out_shape=[jax.ShapeDtypeStruct((tokens, width), F32), jax.ShapeDtypeStruct((experts, tokens), F32)],
        in_specs=[whole(ids.shape), pl.BlockSpec((PEERS, rows, LANE), lambda i: (i, 0, 0))],
        out_specs=[whole((tokens, width)), whole((experts, tokens))],
        scratch_shapes=[pltpu.VMEM((PEERS * FIRST, width), BF)],
        compiler_params=pltpu.CompilerParams(vmem_limit_bytes=SUM_VMEM),
        cost_estimate=pl.CostEstimate(
            flops=2 * experts * FIRST * tokens * width, bytes_accessed=2 * experts * rows * LANE, transcendentals=0
        ),
        name="combine_a",
    )(ids, got)


def combine_second(ids, probs, got, before, rank):
    experts, rows, _ = got.shape
    tokens, width = before.shape
    whole = lambda a: pl.BlockSpec(a.shape, lambda i: (0, 0))
    return pl.pallas_call(
        combine_second_kernel,
        grid=(experts // SUM_PEERS,),
        out_shape=[jax.ShapeDtypeStruct(before.shape, BF), jax.ShapeDtypeStruct(ids.shape, BF)],
        in_specs=[
            whole(ids),
            whole(probs),
            pl.BlockSpec((SUM_PEERS, rows - TILE, LANE), lambda i: (i, 0, 0)),
            pl.BlockSpec((experts, TILE, LANE), lambda i: (0, rows // TILE - 1, 0)),
            whole(before),
            whole(rank),
        ],
        out_specs=[whole(before), whole(ids)],
        scratch_shapes=[pltpu.VMEM((SUM_PEERS * HALF, width), BF), pltpu.VMEM((tokens, width), F32)],
        compiler_params=pltpu.CompilerParams(vmem_limit_bytes=SUM_VMEM),
        cost_estimate=pl.CostEstimate(
            flops=2 * experts * HALF * tokens * width, bytes_accessed=2 * experts * rows * LANE, transcendentals=0
        ),
        name="combine_b",
    )(ids, probs, got, got, before, rank)


def exchange(x):
    return lax.all_to_all(x, ("ctx", "tp"), split_axis=0, concat_axis=0, tiled=True)


def other_core(x):
    return lax.ppermute(x, "dp", [(0, 1), (1, 0)])


def per_device(tokens, cotangent, probs, expert_ids, gate_weight, up_weight, down_weight):
    experts = lax.axis_size("ctx") * lax.axis_size("tp")
    gate_mat, up_mat, down_mat = gate_weight[0], up_weight[0], down_weight[0]
    ids, weights = expert_ids.T, probs.T
    mats, values = (gate_mat, up_mat, down_mat), (tokens, cotangent)
    sent_a, *turned, sent_b = lax.optimization_barrier(
        (
            pack("pack_a", pack_first_kernel, 2 * FIRST, 2, ids, weights, values, experts),
            *ahead("ahead_1", 1, ids, weights, mats, values, experts),
        )
    )
    got_a, sent_b, turned, mats, values = lax.optimization_barrier((exchange(sent_a), sent_b, turned, mats, values))
    (sent_b,) = ahead("pack_b_0", 0, ids, weights, (), values, experts, (sent_b,))
    sent_b, turned, mats = lax.optimization_barrier((sent_b, turned, mats))
    got_b = exchange(sent_b)
    gate_t, up_t, down_t = turn("turn_0", 0, mats, turned)
    mats = (gate_mat, up_mat, down_t)

    def part(name, got, slot_grads=None, kept=()):
        rows, cot_rows, gate, up, back = project("project_" + name, got, mats, kept[:2])
        far = other_core(gate), other_core(up), other_core(back)
        sent, act, gate_grad, up_grad, *slot_grads = pair(
            "pair_" + name, gate, far[0], up, far[1], back, far[2], gate_t, up_t, experts, slot_grads, kept[2:]
        )
        return sent, slot_grads, (rows, cot_rows, act, gate_grad, up_grad)

    pairs_a, (slot_grads,), kept = part("a", got_a)
    got_b, pairs_a = lax.optimization_barrier((got_b, pairs_a))
    back_a = exchange(pairs_a)
    pairs_b, _, (rows, cot_rows, act, gate_grad, up_grad) = part("b", got_b, slot_grads, kept)
    back_b = exchange(pairs_b)
    grad_down = contract(act, cot_rows).astype(BF)
    grad_gate = contract(rows, gate_grad).astype(BF)
    grad_up = contract(rows, up_grad).astype(BF)
    before, rank = combine_first(ids, back_a, tokens.shape[1])
    grad_tokens, grad_probs = combine_second(ids, weights, back_b, before, rank)
    return (grad_tokens, grad_probs.T, grad_gate[None], grad_up[None], grad_down[None])


def solution(mesh):
    return jax.shard_map(
        per_device,
        mesh=mesh,
        in_specs=(
            P(("ctx", "tp"), "dp"),
            P(("ctx", "tp"), "dp"),
            P(("ctx", "tp"), None),
            P(("ctx", "tp"), None),
            P(("ctx", "tp"), "dp", None),
            P(("ctx", "tp"), "dp", None),
            P(("ctx", "tp"), None, "dp"),
        ),
        out_specs=(
            P(("ctx", "tp"), "dp"),
            P(("ctx", "tp"), None),
            P(("ctx", "tp"), "dp", None),
            P(("ctx", "tp"), "dp", None),
            P(("ctx", "tp"), None, "dp"),
        ),
        check_vma=False,
    )
```

```python
import functools

import jax
import jax.numpy as jnp
from jax import lax
from jax.experimental import pallas as pl
from jax.experimental.pallas import tpu as pltpu
from jax.sharding import PartitionSpec as P

BF = jnp.bfloat16
F32 = jnp.float32
LANE = 128
HALF = 8
EXTRA = 2
CAP = 2 * HALF + EXTRA
FIRST = HALF + EXTRA
TILE = 16
GROUP = 16
PEERS = 32
SECOND_PEERS = 16
PACK_PEERS = 32
SUM_PEERS = 64
VMEM = 62 * 2**20
SUM_VMEM = 24 * 2**20


def iota(shape, dim):
    return lax.broadcasted_iota(jnp.int32, shape, dim)


def dot(a, b):
    return jnp.dot(a, b, preferred_element_type=F32)


def contract(left, right):
    return lax.dot_general(left, right, (((0,), (0,)), ((), ())), preferred_element_type=F32)


def expert_ranks(ids, experts):
    top, tokens = ids.shape
    expert = iota((experts, tokens), 0)
    hit = jnp.zeros((experts, tokens), F32)
    for k in range(top):
        hit = hit + jnp.where(ids[k : k + 1] == expert, 1.0, 0.0)
    earlier = jnp.where(iota((tokens, tokens), 0) < iota((tokens, tokens), 1), 1.0, 0.0)
    rank = dot(hit.astype(BF), earlier.astype(BF))
    return jnp.where(hit > 0.0, rank, -1.0)


def expert_probs(ids, probs, experts):
    top, tokens = ids.shape
    expert = iota((experts, tokens), 0)
    out = jnp.zeros((experts, tokens), F32)
    for k in range(top):
        out = out + jnp.where(ids[k : k + 1] == expert, probs[k : k + 1], 0.0)
    return out


def by_slot(a, slots):
    peers, tokens = a.shape
    return jnp.broadcast_to(a[:, None, :], (peers, slots, tokens)).reshape(peers * slots, tokens)


def extra_order(pack):
    shape = (GROUP * TILE, GROUP * TILE)
    row, col = iota(shape, 0), iota(shape, 1)
    step = GROUP * EXTRA
    if pack:
        source = (row % TILE) // EXTRA * step + row // TILE * EXTRA + row % EXTRA
    else:
        source = (row % step) // EXTRA * TILE + row // step * EXTRA + row % EXTRA
    return jnp.where(col == source, 1.0, 0.0).astype(BF)


def store_half(out_ref, start, values):
    for c in range(0, values.shape[1] // LANE, 2):
        pair = [values[:, k * LANE : (k + 1) * LANE].reshape(-1, HALF, LANE) for k in (c, c + 1)]
        at = start + c * HALF
        out_ref[:, at : at + TILE, :] = jnp.concatenate(pair, axis=1).astype(BF)


def store_extra(out_ref, start, values):
    for g in range(values.shape[1] // LANE):
        at = start + g * TILE
        out_ref[:, at : at + TILE, :] = values[:, g * LANE : (g + 1) * LANE].reshape(-1, TILE, LANE)


def order_extra(out_ref, start, values):
    groups = values.shape[1] // LANE // 8
    order = extra_order(True)
    step = GROUP * EXTRA
    parts = []
    for p in range(values.shape[0] // step):
        some = values[p * step : (p + 1) * step]
        columns = [
            jnp.concatenate([some[:, (g * 8 + c) * LANE : (g * 8 + c + 1) * LANE] for g in range(groups)], axis=1)
            for c in range(8)
        ]
        parts.append(dot(order, jnp.concatenate(columns, axis=0)).astype(BF))
    store_extra(out_ref, start, jnp.concatenate(parts, axis=0))


def unpack_half(in_ref, start, out_ref, first, count):
    rows = in_ref.shape[0] * HALF
    for c in range(0, count, 2):
        at = start + c * HALF
        pair = in_ref[:, at : at + TILE, :].astype(F32)
        for k in range(2):
            column = first + c + k
            out_ref[:rows, column * LANE : (column + 1) * LANE] = (
                pair[:, k * HALF : (k + 1) * HALF, :].reshape(rows, LANE).astype(BF)
            )


def unpack_extra(in_ref, start, out_ref, base):
    groups = out_ref.shape[1] // LANE // 8
    order = extra_order(False)
    step = GROUP * EXTRA
    for p in range(in_ref.shape[0] // GROUP):
        some = in_ref.at[p * GROUP : (p + 1) * GROUP]
        values = jnp.concatenate(
            [some[:, start + g * TILE : start + (g + 1) * TILE, :].reshape(-1, LANE) for g in range(groups)], axis=1
        )
        ordered = dot(order, values).astype(BF)
        for g in range(groups):
            for c in range(8):
                at = (g * 8 + c) * LANE
                out_ref[base + p * step : base + (p + 1) * step, at : at + LANE] = ordered[
                    c * step : (c + 1) * step, g * LANE : (g + 1) * LANE
                ]


def half_rows(rank, value, start):
    rank = by_slot(rank, HALF)
    hit = rank == (start + iota(rank.shape, 0) % HALF).astype(F32)
    return jnp.where(hit, 1.0 if value is None else by_slot(value, HALF), 0.0).astype(BF)


def extra_rows(rank, value):
    peers = rank.shape[0]
    rank = by_slot(rank, 8)
    hit = rank == (2 * HALF + iota(rank.shape, 0) % 8).astype(F32)
    eight = jnp.where(hit, 1.0 if value is None else by_slot(value, 8), 0.0).astype(BF)
    shape = (peers * EXTRA, peers * 8)
    keep = iota(shape, 1) == iota(shape, 0) // EXTRA * 8 + iota(shape, 0) % EXTRA
    return dot(jnp.where(keep, 1.0, 0.0).astype(BF), eight).astype(BF)


def wide_extra_rows(rank, value):
    rank = by_slot(rank, TILE)
    row = iota(rank.shape, 0)
    hit = rank == (2 * HALF + row % EXTRA).astype(F32)
    extra = jnp.where(hit, 1.0 if value is None else by_slot(value, TILE), 0.0)
    column = (row % TILE) // EXTRA
    return jnp.concatenate([jnp.where(column == c, extra, 0.0).astype(BF) for c in range(8)], axis=1)


def stack_columns(x_ref, side_ref):
    tokens, width = x_ref.shape
    groups = width // LANE // 8
    for c in range(8):
        for g in range(groups):
            at = (g * 8 + c) * LANE
            side_ref[c * tokens : (c + 1) * tokens, g * LANE : (g + 1) * LANE] = x_ref[:, at : at + LANE]


def pack_kernel(
    ids_ref, probs_ref, x_ref, cot_ref, out_a_ref, out_b_ref, rank_ref, prob_ref, side_ref, cot_side_ref
):
    step = pl.program_id(0)
    half = x_ref.shape[1] // LANE * HALF
    part = x_ref.shape[1] // LANE * FIRST
    count = out_a_ref.shape[0]

    @pl.when(step == 0)
    def _():
        rank_ref[...] = expert_ranks(ids_ref[...], rank_ref.shape[0])
        prob_ref[...] = expert_probs(ids_ref[...], probs_ref[...].astype(F32), rank_ref.shape[0])
        stack_columns(x_ref, side_ref)
        stack_columns(cot_ref, cot_side_ref)

    peers = pl.ds(pl.multiple_of(step * count, count), count)
    rank, prob = rank_ref[peers, :], prob_ref[peers, :]
    for n, value, ref, side in ((0, None, x_ref, side_ref), (1, prob, cot_ref, cot_side_ref)):
        store_half(out_a_ref, n * part, dot(half_rows(rank, value, 0), ref[...]))
        store_extra(out_a_ref, n * part + half, dot(wide_extra_rows(rank, value), side[...]).astype(BF))
        store_half(out_b_ref, n * half, dot(half_rows(rank, value, HALF), ref[...]))


def pack(ids, probs, x, cot, experts):
    tokens, width = x.shape
    rows = [width // LANE * 2 * slots for slots in (FIRST, HALF)]
    return pl.pallas_call(
        pack_kernel,
        grid=(experts // PACK_PEERS,),
        out_shape=[jax.ShapeDtypeStruct((experts, n, LANE), BF) for n in rows],
        in_specs=[pl.BlockSpec(a.shape, lambda i: (0, 0)) for a in (ids, probs, x, cot)],
        out_specs=[pl.BlockSpec((PACK_PEERS, n, LANE), lambda i: (i, 0, 0)) for n in rows],
        scratch_shapes=[pltpu.VMEM((experts, tokens), F32)] * 2 + [pltpu.VMEM((8 * tokens, width // 8), BF)] * 2,
        compiler_params=pltpu.CompilerParams(vmem_limit_bytes=VMEM),
        cost_estimate=pl.CostEstimate(
            flops=4 * experts * CAP * tokens * width,
            bytes_accessed=2 * experts * sum(rows) * LANE,
            transcendentals=0,
        ),
        name="pack",
    )(ids, probs, x, cot)


def turn_kernel(core, count, *refs):
    ins, outs = refs[:count], refs[-5 * count : -4 * count]
    held, turned = refs[-4 * count : -3 * count], refs[-3 * count : -2 * count]
    in_sems, out_sems = refs[-2 * count : -count], refs[-count:]

    def move(mat, a, b, out, in_sem, out_sem, start, size):
        rows = pl.ds(start, size)
        load = pltpu.make_async_copy(mat.at[rows], a.at[rows], in_sem)
        store = pltpu.make_async_copy(b.at[:, rows], out.at[:, rows], out_sem)
        return load, store

    def flip(a, b, start, size):
        for at in range(start, start + size, 128):
            b[:, at : at + 128] = a[at : at + 128, :].T

    @pl.when(lax.axis_index("dp") == core)
    def _():
        given = list(zip(ins, held, turned, outs, in_sems, out_sems))
        if core:
            for refs in given:
                size = refs[0].shape[0] // 2
                for start in (0, size):
                    load, store = move(*refs, start, size)
                    load.start()
                    load.wait()
                    flip(refs[1], refs[2], start, size)
                    store.start()
                    store.wait()
        else:
            moves = [move(*refs, 0, refs[0].shape[0]) for refs in given]
            for load, _ in moves:
                load.start()
            for refs, (load, store) in zip(given, moves):
                load.wait()
                flip(refs[1], refs[2], 0, refs[0].shape[0])
                store.start()
            for _, store in moves:
                store.wait()


def turn(name, core, mats, before=()):
    shapes = [m.shape for m in mats]
    anywhere = pl.BlockSpec(memory_space=pl.ANY)
    return pl.pallas_call(
        functools.partial(turn_kernel, core, len(mats)),
        out_shape=[jax.ShapeDtypeStruct(shape[::-1], BF) for shape in shapes],
        in_specs=[anywhere] * (len(mats) + len(before)),
        out_specs=[anywhere] * len(mats),
        input_output_aliases={len(mats) + k: k for k in range(len(before))},
        scratch_shapes=[pltpu.VMEM(shape, BF) for shape in shapes]
        + [pltpu.VMEM(shape[::-1], BF) for shape in shapes]
        + [pltpu.SemaphoreType.DMA] * (2 * len(mats)),
        compiler_params=pltpu.CompilerParams(vmem_limit_bytes=VMEM),
        cost_estimate=pl.CostEstimate(flops=0, bytes_accessed=sum(4 * a * b for a, b in shapes), transcendentals=0),
        name=name,
    )(*mats, *before)


def project_kernel(extra, x_in, cot_in, gate_w, up_w, down_w, *refs):
    x_ref, cot_ref, gate_ref, up_ref, back_ref = refs[-5:]
    peers = x_in.shape[0]
    tiles = x_ref.shape[1] // LANE
    for in_ref, rows_ref in ((x_in, x_ref), (cot_in, cot_ref)):
        unpack_half(in_ref, 0, rows_ref, 0, tiles)
        if extra:
            unpack_extra(in_ref, tiles * HALF, rows_ref, peers * HALF)
    gate_ref[...] = dot(x_ref[...], gate_w[...]).astype(BF)
    up_ref[...] = dot(x_ref[...], up_w[...]).astype(BF)
    back_ref[...] = dot(cot_ref[...], down_w[...]).astype(BF)


def project(name, got, weights, kept=()):
    experts, both, _ = got.shape
    width, hidden = weights[0].shape
    part = both // 2
    slots = part * LANE // width
    peers = SECOND_PEERS if kept else PEERS
    total, rows = experts * slots, peers * slots
    first = experts * FIRST // rows if kept else 0
    whole = experts * CAP
    return pl.pallas_call(
        functools.partial(project_kernel, not kept),
        grid=(experts // peers,),
        out_shape=[jax.ShapeDtypeStruct((whole, width), BF)] * 2 + [jax.ShapeDtypeStruct((total, hidden), BF)] * 3,
        in_specs=[pl.BlockSpec((peers, part, LANE), lambda i, at=at: (i, at, 0)) for at in range(2)]
        + [pl.BlockSpec(w.shape, lambda i: (0, 0)) for w in weights]
        + [pl.BlockSpec(memory_space=pl.ANY) for _ in kept],
        out_specs=[pl.BlockSpec((rows, width), lambda i: (first + i, 0))] * 2
        + [pl.BlockSpec((rows, hidden), lambda i: (i, 0))] * 3,
        input_output_aliases={5 + k: k for k in range(len(kept))},
        compiler_params=pltpu.CompilerParams(vmem_limit_bytes=VMEM),
        cost_estimate=pl.CostEstimate(
            flops=6 * total * width * hidden,
            bytes_accessed=2 * (4 * total * width + 3 * (width + total) * hidden),
            transcendentals=0,
        ),
        name=name,
    )(got, got, *weights, *kept)


def slots_of(prob_grad, peers, extra):
    total = prob_grad.shape[0]
    main = peers * HALF
    row, lane = iota((total, LANE), 0), iota((total, LANE), 1)
    peer, of = iota((peers, total), 0), iota((peers, total), 1)
    slot, owner = row % HALF, of // HALF
    if extra:
        slot = jnp.where(row < main, slot, 2 * HALF + row % EXTRA)
        owner = jnp.where(of < main, owner, (of - main) // EXTRA)
    else:
        slot = slot + HALF
    by_lane = jnp.where(lane == slot, prob_grad, 0.0).astype(BF)
    return dot(jnp.where(peer == owner, 1.0, 0.0).astype(BF), by_lane)


def pair_kernel(extra, *refs):
    if extra:
        *refs, out_ref, act_ref, gg_ref, ug_ref, slots_out_ref = refs
    else:
        *refs, slots_ref, _, _, _, out_ref, act_ref, gg_ref, ug_ref = refs
    gate, gate_far, up, up_far, back, back_far, gate_t, up_t = refs
    g = gate[...].astype(F32) + gate_far[...].astype(F32)
    u = up[...].astype(F32) + up_far[...].astype(F32)
    b = back[...].astype(F32) + back_far[...].astype(F32)
    sigmoid = jax.nn.sigmoid(g)
    silu = g * sigmoid
    act = silu * u
    act_ref[...] = act.astype(BF)
    gg_ref[...] = (b * u * sigmoid * (1.0 + g * (1.0 - sigmoid))).astype(BF)
    ug_ref[...] = (b * silu).astype(BF)
    prob_grad = jnp.sum(act * b, axis=1, keepdims=True)
    y = dot(gg_ref[...], gate_t[...]) + dot(ug_ref[...], up_t[...])
    half = y.shape[1] // LANE * HALF
    peers = out_ref.shape[0]
    main = peers * HALF
    store_half(out_ref, 0, y[:main])
    slots = slots_of(prob_grad, peers, extra)
    if extra:
        order_extra(out_ref, half, y[main:].astype(BF))
        slots_out_ref[...] = slots
    else:
        grads = by_slot(slots + slots_ref[...], TILE)
        out_ref[:, half:, :] = grads.astype(BF).reshape(peers, TILE, LANE)


def pair(name, gate, gate_far, up, up_far, back, back_far, gate_t, up_t, experts, slot_grads=None, kept=()):
    total, hidden = gate.shape
    width = gate_t.shape[1]
    slots = total // experts
    extra = not kept
    peers = PEERS if extra else SECOND_PEERS
    rows = width // LANE * slots + (0 if extra else TILE)
    first = 0 if extra else experts * FIRST // (peers * slots)
    block = pl.BlockSpec((peers * slots, hidden), lambda i: (i, 0))
    placed = pl.BlockSpec((peers * slots, hidden), lambda i: (first + i, 0))
    whole = pl.BlockSpec(gate_t.shape, lambda i: (0, 0))
    small = pl.BlockSpec((peers, LANE), lambda i: (i, 0))
    more = () if extra else (slot_grads, *kept)
    return pl.pallas_call(
        functools.partial(pair_kernel, extra),
        grid=(experts // peers,),
        out_shape=[jax.ShapeDtypeStruct((experts, rows, LANE), BF)]
        + [jax.ShapeDtypeStruct((experts * CAP, hidden), BF)] * 3
        + [jax.ShapeDtypeStruct((experts, LANE), F32)] * extra,
        in_specs=[block] * 6
        + [whole] * 2
        + ([] if extra else [small] + [pl.BlockSpec(memory_space=pl.ANY)] * len(kept)),
        out_specs=[pl.BlockSpec((peers, rows, LANE), lambda i: (i, 0, 0))] + [placed] * 3 + [small] * extra,
        input_output_aliases={9 + k: 1 + k for k in range(len(kept))},
        compiler_params=pltpu.CompilerParams(vmem_limit_bytes=VMEM),
        cost_estimate=pl.CostEstimate(
            flops=4 * total * width * hidden,
            bytes_accessed=2 * (total * width + 9 * total * hidden + 2 * width * hidden),
            transcendentals=total * hidden,
        ),
        name=name,
    )(gate, gate_far, up, up_far, back, back_far, gate_t, up_t, *more)


def combine_first_kernel(ids_ref, in_ref, total_ref, rank_ref, rows_ref):
    step = pl.program_id(0)
    experts = rank_ref.shape[0]
    peers, tiles = in_ref.shape[0], total_ref.shape[1] // LANE

    @pl.when(step == 0)
    def _():
        rank_ref[...] = expert_ranks(ids_ref[...], experts)
        total_ref[...] = jnp.zeros_like(total_ref)

    unpack_half(in_ref, 0, rows_ref, 0, tiles)
    unpack_extra(in_ref, tiles * HALF, rows_ref, peers * HALF)
    rank = rank_ref[pl.ds(pl.multiple_of(step * peers, peers), peers), :]
    which = jnp.concatenate([half_rows(rank, None, 0), extra_rows(rank, None)], axis=0)
    total_ref[...] += contract(which, rows_ref[...])


def combine_second_kernel(
    ids_ref, probs_ref, in_ref, slots_ref, before_ref, rank_ref, out_ref, probs_out_ref, rows_ref, total_ref
):
    step = pl.program_id(0)
    experts, tokens = rank_ref.shape
    peers, tiles = in_ref.shape[0], out_ref.shape[1] // LANE

    @pl.when(step == 0)
    def _():
        total_ref[...] = before_ref[...]
        slots = slots_ref[:, 0, :].astype(F32)
        rank = rank_ref[...]
        found = jnp.zeros((experts, tokens), F32)
        for s in range(CAP):
            found = found + jnp.where(rank == float(s), slots[:, s : s + 1], 0.0)
        ids = ids_ref[...]
        expert = iota((experts, tokens), 0)
        grads = [
            jnp.sum(jnp.where(ids[k : k + 1] == expert, found, 0.0), axis=0, keepdims=True)
            for k in range(ids.shape[0])
        ]
        probs_out_ref[...] = (jnp.concatenate(grads, axis=0) / probs_ref[...].astype(F32)).astype(BF)

    unpack_half(in_ref, 0, rows_ref, 0, tiles)
    rank = rank_ref[pl.ds(pl.multiple_of(step * peers, peers), peers), :]
    total_ref[...] += contract(half_rows(rank, None, HALF), rows_ref[...])

    @pl.when(step == pl.num_programs(0) - 1)
    def _():
        out_ref[...] = total_ref[...].astype(BF)


def combine_first(ids, got, width):
    experts, rows, _ = got.shape
    tokens = ids.shape[1]
    whole = lambda shape: pl.BlockSpec(shape, lambda i: (0, 0))
    return pl.pallas_call(
        combine_first_kernel,
        grid=(experts // PEERS,),
        out_shape=[jax.ShapeDtypeStruct((tokens, width), F32), jax.ShapeDtypeStruct((experts, tokens), F32)],
        in_specs=[whole(ids.shape), pl.BlockSpec((PEERS, rows, LANE), lambda i: (i, 0, 0))],
        out_specs=[whole((tokens, width)), whole((experts, tokens))],
        scratch_shapes=[pltpu.VMEM((PEERS * FIRST, width), BF)],
        compiler_params=pltpu.CompilerParams(vmem_limit_bytes=SUM_VMEM),
        cost_estimate=pl.CostEstimate(
            flops=2 * experts * FIRST * tokens * width, bytes_accessed=2 * experts * rows * LANE, transcendentals=0
        ),
        name="combine_a",
    )(ids, got)


def combine_second(ids, probs, got, before, rank):
    experts, rows, _ = got.shape
    tokens, width = before.shape
    whole = lambda a: pl.BlockSpec(a.shape, lambda i: (0, 0))
    return pl.pallas_call(
        combine_second_kernel,
        grid=(experts // SUM_PEERS,),
        out_shape=[jax.ShapeDtypeStruct(before.shape, BF), jax.ShapeDtypeStruct(ids.shape, BF)],
        in_specs=[
            whole(ids),
            whole(probs),
            pl.BlockSpec((SUM_PEERS, rows - TILE, LANE), lambda i: (i, 0, 0)),
            pl.BlockSpec((experts, TILE, LANE), lambda i: (0, rows // TILE - 1, 0)),
            whole(before),
            whole(rank),
        ],
        out_specs=[whole(before), whole(ids)],
        scratch_shapes=[pltpu.VMEM((SUM_PEERS * HALF, width), BF), pltpu.VMEM((tokens, width), F32)],
        compiler_params=pltpu.CompilerParams(vmem_limit_bytes=SUM_VMEM),
        cost_estimate=pl.CostEstimate(
            flops=2 * experts * HALF * tokens * width, bytes_accessed=2 * experts * rows * LANE, transcendentals=0
        ),
        name="combine_b",
    )(ids, probs, got, got, before, rank)


def exchange(x):
    return lax.all_to_all(x, ("ctx", "tp"), split_axis=0, concat_axis=0, tiled=True)


def other_core(x):
    return lax.ppermute(x, "dp", [(0, 1), (1, 0)])


def per_device(tokens, cotangent, probs, expert_ids, gate_weight, up_weight, down_weight):
    experts = lax.axis_size("ctx") * lax.axis_size("tp")
    gate_mat, up_mat, down_mat = gate_weight[0], up_weight[0], down_weight[0]
    ids, weights = expert_ids.T, probs.T
    mats = (gate_mat, up_mat, down_mat)
    sent_a, sent_b, *turned = lax.optimization_barrier(
        (*pack(ids, weights, tokens, cotangent, experts), *turn("turn_1", 1, mats))
    )
    got_a, sent_b, turned, mats = lax.optimization_barrier((exchange(sent_a), sent_b, turned, mats))
    got_b = exchange(sent_b)
    gate_t, up_t, down_t = turn("turn_0", 0, mats, turned)
    mats = (gate_mat, up_mat, down_t)

    def part(name, got, slot_grads=None, kept=()):
        rows, cot_rows, gate, up, back = project("project_" + name, got, mats, kept[:2])
        far = other_core(gate), other_core(up), other_core(back)
        sent, act, gate_grad, up_grad, *slot_grads = pair(
            "pair_" + name, gate, far[0], up, far[1], back, far[2], gate_t, up_t, experts, slot_grads, kept[2:]
        )
        return sent, slot_grads, (rows, cot_rows, act, gate_grad, up_grad)

    pairs_a, (slot_grads,), kept = part("a", got_a)
    got_b, pairs_a = lax.optimization_barrier((got_b, pairs_a))
    back_a = exchange(pairs_a)
    pairs_b, _, (rows, cot_rows, act, gate_grad, up_grad) = part("b", got_b, slot_grads, kept)
    back_b = exchange(pairs_b)
    grad_down = contract(act, cot_rows).astype(BF)
    grad_gate = contract(rows, gate_grad).astype(BF)
    grad_up = contract(rows, up_grad).astype(BF)
    before, rank = combine_first(ids, back_a, tokens.shape[1])
    grad_tokens, grad_probs = combine_second(ids, weights, back_b, before, rank)
    return (grad_tokens, grad_probs.T, grad_gate[None], grad_up[None], grad_down[None])


def solution(mesh):
    return jax.shard_map(
        per_device,
        mesh=mesh,
        in_specs=(
            P(("ctx", "tp"), "dp"),
            P(("ctx", "tp"), "dp"),
            P(("ctx", "tp"), None),
            P(("ctx", "tp"), None),
            P(("ctx", "tp"), "dp", None),
            P(("ctx", "tp"), "dp", None),
            P(("ctx", "tp"), None, "dp"),
        ),
        out_specs=(
            P(("ctx", "tp"), "dp"),
            P(("ctx", "tp"), None),
            P(("ctx", "tp"), "dp", None),
            P(("ctx", "tp"), "dp", None),
            P(("ctx", "tp"), None, "dp"),
        ),
        check_vma=False,
    )
```

```python
import functools

import jax
import jax.numpy as jnp
from jax import lax
from jax.experimental import pallas as pl
from jax.experimental.pallas import tpu as pltpu
from jax.sharding import PartitionSpec as P

BF = jnp.bfloat16
F32 = jnp.float32
LANE = 128
HALF = 8
EXTRA = 2
CAP = 2 * HALF + EXTRA
FIRST = HALF + EXTRA
TILE = 16
GROUP = 16
PEERS = 32
SECOND_PEERS = 16
PACK_PEERS = 32
SUM_PEERS = 64
VMEM = 62 * 2**20
SUM_VMEM = 24 * 2**20


def iota(shape, dim):
    return lax.broadcasted_iota(jnp.int32, shape, dim)


def dot(a, b):
    return jnp.dot(a, b, preferred_element_type=F32)


def contract(left, right):
    return lax.dot_general(left, right, (((0,), (0,)), ((), ())), preferred_element_type=F32)


def expert_ranks(ids, experts):
    top, tokens = ids.shape
    expert = iota((experts, tokens), 0)
    hit = jnp.zeros((experts, tokens), F32)
    for k in range(top):
        hit = hit + jnp.where(ids[k : k + 1] == expert, 1.0, 0.0)
    earlier = jnp.where(iota((tokens, tokens), 0) < iota((tokens, tokens), 1), 1.0, 0.0)
    rank = dot(hit.astype(BF), earlier.astype(BF))
    return jnp.where(hit > 0.0, rank, -1.0)


def expert_probs(ids, probs, experts):
    top, tokens = ids.shape
    expert = iota((experts, tokens), 0)
    out = jnp.zeros((experts, tokens), F32)
    for k in range(top):
        out = out + jnp.where(ids[k : k + 1] == expert, probs[k : k + 1], 0.0)
    return out


def by_slot(a, slots):
    peers, tokens = a.shape
    return jnp.broadcast_to(a[:, None, :], (peers, slots, tokens)).reshape(peers * slots, tokens)


def extra_order(pack):
    shape = (GROUP * TILE, GROUP * TILE)
    row, col = iota(shape, 0), iota(shape, 1)
    step = GROUP * EXTRA
    if pack:
        source = (row % TILE) // EXTRA * step + row // TILE * EXTRA + row % EXTRA
    else:
        source = (row % step) // EXTRA * TILE + row // step * EXTRA + row % EXTRA
    return jnp.where(col == source, 1.0, 0.0).astype(BF)


def store_half(out_ref, start, values):
    for c in range(0, values.shape[1] // LANE, 2):
        pair = [values[:, k * LANE : (k + 1) * LANE].reshape(-1, HALF, LANE) for k in (c, c + 1)]
        at = start + c * HALF
        out_ref[:, at : at + TILE, :] = jnp.concatenate(pair, axis=1).astype(BF)


def store_extra(out_ref, start, values):
    for g in range(values.shape[1] // LANE):
        at = start + g * TILE
        out_ref[:, at : at + TILE, :] = values[:, g * LANE : (g + 1) * LANE].reshape(-1, TILE, LANE)


def order_extra(out_ref, start, values):
    groups = values.shape[1] // LANE // 8
    order = extra_order(True)
    step = GROUP * EXTRA
    parts = []
    for p in range(values.shape[0] // step):
        some = values[p * step : (p + 1) * step]
        columns = [
            jnp.concatenate([some[:, (g * 8 + c) * LANE : (g * 8 + c + 1) * LANE] for g in range(groups)], axis=1)
            for c in range(8)
        ]
        parts.append(dot(order, jnp.concatenate(columns, axis=0)).astype(BF))
    store_extra(out_ref, start, jnp.concatenate(parts, axis=0))


def unpack_half(in_ref, start, out_ref, first, count):
    rows = in_ref.shape[0] * HALF
    for c in range(0, count, 2):
        at = start + c * HALF
        pair = in_ref[:, at : at + TILE, :].astype(F32)
        for k in range(2):
            column = first + c + k
            out_ref[:rows, column * LANE : (column + 1) * LANE] = (
                pair[:, k * HALF : (k + 1) * HALF, :].reshape(rows, LANE).astype(BF)
            )


def unpack_extra(in_ref, start, out_ref, base):
    groups = out_ref.shape[1] // LANE // 8
    order = extra_order(False)
    step = GROUP * EXTRA
    for p in range(in_ref.shape[0] // GROUP):
        some = in_ref.at[p * GROUP : (p + 1) * GROUP]
        values = jnp.concatenate(
            [some[:, start + g * TILE : start + (g + 1) * TILE, :].reshape(-1, LANE) for g in range(groups)], axis=1
        )
        ordered = dot(order, values).astype(BF)
        for g in range(groups):
            for c in range(8):
                at = (g * 8 + c) * LANE
                out_ref[base + p * step : base + (p + 1) * step, at : at + LANE] = ordered[
                    c * step : (c + 1) * step, g * LANE : (g + 1) * LANE
                ]


def half_rows(rank, value, start):
    rank = by_slot(rank, HALF)
    hit = rank == (start + iota(rank.shape, 0) % HALF).astype(F32)
    return jnp.where(hit, 1.0 if value is None else by_slot(value, HALF), 0.0).astype(BF)


def extra_rows(rank, value):
    peers = rank.shape[0]
    rank = by_slot(rank, 8)
    hit = rank == (2 * HALF + iota(rank.shape, 0) % 8).astype(F32)
    eight = jnp.where(hit, 1.0 if value is None else by_slot(value, 8), 0.0).astype(BF)
    shape = (peers * EXTRA, peers * 8)
    keep = iota(shape, 1) == iota(shape, 0) // EXTRA * 8 + iota(shape, 0) % EXTRA
    return dot(jnp.where(keep, 1.0, 0.0).astype(BF), eight).astype(BF)


def wide_extra_rows(rank, value):
    rank = by_slot(rank, TILE)
    row = iota(rank.shape, 0)
    hit = rank == (2 * HALF + row % EXTRA).astype(F32)
    extra = jnp.where(hit, 1.0 if value is None else by_slot(value, TILE), 0.0)
    column = (row % TILE) // EXTRA
    return jnp.concatenate([jnp.where(column == c, extra, 0.0).astype(BF) for c in range(8)], axis=1)


def stack_columns(x_ref, side_ref):
    tokens, width = x_ref.shape
    groups = width // LANE // 8
    for c in range(8):
        for g in range(groups):
            at = (g * 8 + c) * LANE
            side_ref[c * tokens : (c + 1) * tokens, g * LANE : (g + 1) * LANE] = x_ref[:, at : at + LANE]


def pack_kernel(
    ids_ref, probs_ref, x_ref, cot_ref, out_a_ref, out_b_ref, rank_ref, prob_ref, side_ref, cot_side_ref
):
    step = pl.program_id(0)
    half = x_ref.shape[1] // LANE * HALF
    part = x_ref.shape[1] // LANE * FIRST
    count = out_a_ref.shape[0]

    @pl.when(step == 0)
    def _():
        rank_ref[...] = expert_ranks(ids_ref[...], rank_ref.shape[0])
        prob_ref[...] = expert_probs(ids_ref[...], probs_ref[...].astype(F32), rank_ref.shape[0])
        stack_columns(x_ref, side_ref)
        stack_columns(cot_ref, cot_side_ref)

    peers = pl.ds(pl.multiple_of(step * count, count), count)
    rank, prob = rank_ref[peers, :], prob_ref[peers, :]
    for n, value, ref, side in ((0, None, x_ref, side_ref), (1, prob, cot_ref, cot_side_ref)):
        store_half(out_a_ref, n * part, dot(half_rows(rank, value, 0), ref[...]))
        store_extra(out_a_ref, n * part + half, dot(wide_extra_rows(rank, value), side[...]).astype(BF))
        store_half(out_b_ref, n * half, dot(half_rows(rank, value, HALF), ref[...]))


def pack(ids, probs, x, cot, experts):
    tokens, width = x.shape
    rows = [width // LANE * 2 * slots for slots in (FIRST, HALF)]
    return pl.pallas_call(
        pack_kernel,
        grid=(experts // PACK_PEERS,),
        out_shape=[jax.ShapeDtypeStruct((experts, n, LANE), BF) for n in rows],
        in_specs=[pl.BlockSpec(a.shape, lambda i: (0, 0)) for a in (ids, probs, x, cot)],
        out_specs=[pl.BlockSpec((PACK_PEERS, n, LANE), lambda i: (i, 0, 0)) for n in rows],
        scratch_shapes=[pltpu.VMEM((experts, tokens), F32)] * 2 + [pltpu.VMEM((8 * tokens, width // 8), BF)] * 2,
        compiler_params=pltpu.CompilerParams(vmem_limit_bytes=VMEM),
        cost_estimate=pl.CostEstimate(
            flops=4 * experts * CAP * tokens * width,
            bytes_accessed=2 * experts * sum(rows) * LANE,
            transcendentals=0,
        ),
        name="pack",
    )(ids, probs, x, cot)


def turn_kernel(core, count, *refs):
    ins, outs = refs[:count], refs[-5 * count : -4 * count]
    held, turned = refs[-4 * count : -3 * count], refs[-3 * count : -2 * count]
    in_sems, out_sems = refs[-2 * count : -count], refs[-count:]

    def move(mat, a, b, out, in_sem, out_sem, start, size):
        rows = pl.ds(start, size)
        load = pltpu.make_async_copy(mat.at[rows], a.at[rows], in_sem)
        store = pltpu.make_async_copy(b.at[:, rows], out.at[:, rows], out_sem)
        return load, store

    def flip(a, b, start, size):
        for at in range(start, start + size, 128):
            b[:, at : at + 128] = a[at : at + 128, :].T

    @pl.when(lax.axis_index("dp") == core)
    def _():
        given = list(zip(ins, held, turned, outs, in_sems, out_sems))
        if core:
            for refs in given:
                rows = refs[0].shape[0]
                size = min(rows, 1024)
                for start in range(0, rows, size):
                    load, store = move(*refs, start, size)
                    load.start()
                    load.wait()
                    flip(refs[1], refs[2], start, size)
                    store.start()
                    store.wait()
        else:
            moves = [move(*refs, 0, refs[0].shape[0]) for refs in given]
            for load, _ in moves:
                load.start()
            for refs, (load, store) in zip(given, moves):
                load.wait()
                flip(refs[1], refs[2], 0, refs[0].shape[0])
                store.start()
            for _, store in moves:
                store.wait()


def turn(name, core, mats, before=()):
    shapes = [m.shape for m in mats]
    anywhere = pl.BlockSpec(memory_space=pl.ANY)
    return pl.pallas_call(
        functools.partial(turn_kernel, core, len(mats)),
        out_shape=[jax.ShapeDtypeStruct(shape[::-1], BF) for shape in shapes],
        in_specs=[anywhere] * (len(mats) + len(before)),
        out_specs=[anywhere] * len(mats),
        input_output_aliases={len(mats) + k: k for k in range(len(before))},
        scratch_shapes=[pltpu.VMEM(shape, BF) for shape in shapes]
        + [pltpu.VMEM(shape[::-1], BF) for shape in shapes]
        + [pltpu.SemaphoreType.DMA] * (2 * len(mats)),
        compiler_params=pltpu.CompilerParams(vmem_limit_bytes=VMEM),
        cost_estimate=pl.CostEstimate(flops=0, bytes_accessed=sum(4 * a * b for a, b in shapes), transcendentals=0),
        name=name,
    )(*mats, *before)


def project_kernel(count, extra, in_ref, *refs):
    weights, rows_ref, outs = refs[:count], refs[-1 - count], refs[-count:]
    tiles = rows_ref.shape[1] // LANE
    unpack_half(in_ref, 0, rows_ref, 0, tiles)
    if extra:
        unpack_extra(in_ref, tiles * HALF, rows_ref, in_ref.shape[0] * HALF)
    for weight, out in zip(weights, outs):
        out[...] = dot(rows_ref[...], weight[...]).astype(BF)


def project(name, got, at, weights, kept=()):
    experts, both, _ = got.shape
    width, hidden = weights[0].shape
    part = both // 2
    slots = part * LANE // width
    peers = SECOND_PEERS if kept else PEERS
    total, rows = experts * slots, peers * slots
    first = experts * FIRST // rows if kept else 0
    count = len(weights)
    return pl.pallas_call(
        functools.partial(project_kernel, count, not kept),
        grid=(experts // peers,),
        out_shape=[jax.ShapeDtypeStruct((experts * CAP, width), BF)]
        + [jax.ShapeDtypeStruct((total, hidden), BF)] * count,
        in_specs=[pl.BlockSpec((peers, part, LANE), lambda i: (i, at, 0))]
        + [pl.BlockSpec(w.shape, lambda i: (0, 0)) for w in weights]
        + [pl.BlockSpec(memory_space=pl.ANY) for _ in kept],
        out_specs=[pl.BlockSpec((rows, width), lambda i: (first + i, 0))]
        + [pl.BlockSpec((rows, hidden), lambda i: (i, 0))] * count,
        input_output_aliases={1 + count: 0} if kept else {},
        compiler_params=pltpu.CompilerParams(vmem_limit_bytes=VMEM),
        cost_estimate=pl.CostEstimate(
            flops=2 * count * total * width * hidden,
            bytes_accessed=2 * (2 * total * width + count * (width + total) * hidden),
            transcendentals=0,
        ),
        name=name,
    )(got, *weights, *kept)


def slots_of(prob_grad, peers, extra):
    total = prob_grad.shape[0]
    main = peers * HALF
    row, lane = iota((total, LANE), 0), iota((total, LANE), 1)
    peer, of = iota((peers, total), 0), iota((peers, total), 1)
    slot, owner = row % HALF, of // HALF
    if extra:
        slot = jnp.where(row < main, slot, 2 * HALF + row % EXTRA)
        owner = jnp.where(of < main, owner, (of - main) // EXTRA)
    else:
        slot = slot + HALF
    by_lane = jnp.where(lane == slot, prob_grad, 0.0).astype(BF)
    return dot(jnp.where(peer == owner, 1.0, 0.0).astype(BF), by_lane)


def pair_kernel(extra, *refs):
    if extra:
        *refs, out_ref, act_ref, gg_ref, ug_ref, slots_out_ref = refs
    else:
        *refs, slots_ref, _, _, _, out_ref, act_ref, gg_ref, ug_ref = refs
    gate, gate_far, up, up_far, back, back_far, gate_t, up_t = refs
    g = gate[...].astype(F32) + gate_far[...].astype(F32)
    u = up[...].astype(F32) + up_far[...].astype(F32)
    b = back[...].astype(F32) + back_far[...].astype(F32)
    sigmoid = jax.nn.sigmoid(g)
    silu = g * sigmoid
    act = silu * u
    act_ref[...] = act.astype(BF)
    gg_ref[...] = (b * u * sigmoid * (1.0 + g * (1.0 - sigmoid))).astype(BF)
    ug_ref[...] = (b * silu).astype(BF)
    prob_grad = jnp.sum(act * b, axis=1, keepdims=True)
    y = dot(gg_ref[...], gate_t[...]) + dot(ug_ref[...], up_t[...])
    half = y.shape[1] // LANE * HALF
    peers = out_ref.shape[0]
    main = peers * HALF
    store_half(out_ref, 0, y[:main])
    slots = slots_of(prob_grad, peers, extra)
    if extra:
        order_extra(out_ref, half, y[main:].astype(BF))
        slots_out_ref[...] = slots
    else:
        grads = by_slot(slots + slots_ref[...], TILE)
        out_ref[:, half:, :] = grads.astype(BF).reshape(peers, TILE, LANE)


def pair(name, gate, gate_far, up, up_far, back, back_far, gate_t, up_t, experts, slot_grads=None, kept=()):
    total, hidden = gate.shape
    width = gate_t.shape[1]
    slots = total // experts
    extra = not kept
    peers = PEERS if extra else SECOND_PEERS
    rows = width // LANE * slots + (0 if extra else TILE)
    first = 0 if extra else experts * FIRST // (peers * slots)
    block = pl.BlockSpec((peers * slots, hidden), lambda i: (i, 0))
    placed = pl.BlockSpec((peers * slots, hidden), lambda i: (first + i, 0))
    whole = pl.BlockSpec(gate_t.shape, lambda i: (0, 0))
    small = pl.BlockSpec((peers, LANE), lambda i: (i, 0))
    more = () if extra else (slot_grads, *kept)
    return pl.pallas_call(
        functools.partial(pair_kernel, extra),
        grid=(experts // peers,),
        out_shape=[jax.ShapeDtypeStruct((experts, rows, LANE), BF)]
        + [jax.ShapeDtypeStruct((experts * CAP, hidden), BF)] * 3
        + [jax.ShapeDtypeStruct((experts, LANE), F32)] * extra,
        in_specs=[block] * 6
        + [whole] * 2
        + ([] if extra else [small] + [pl.BlockSpec(memory_space=pl.ANY)] * len(kept)),
        out_specs=[pl.BlockSpec((peers, rows, LANE), lambda i: (i, 0, 0))] + [placed] * 3 + [small] * extra,
        input_output_aliases={9 + k: 1 + k for k in range(len(kept))},
        compiler_params=pltpu.CompilerParams(vmem_limit_bytes=VMEM),
        cost_estimate=pl.CostEstimate(
            flops=4 * total * width * hidden,
            bytes_accessed=2 * (total * width + 9 * total * hidden + 2 * width * hidden),
            transcendentals=total * hidden,
        ),
        name=name,
    )(gate, gate_far, up, up_far, back, back_far, gate_t, up_t, *more)


def combine_first_kernel(ids_ref, in_ref, total_ref, rank_ref, rows_ref):
    step = pl.program_id(0)
    experts = rank_ref.shape[0]
    peers, tiles = in_ref.shape[0], total_ref.shape[1] // LANE

    @pl.when(step == 0)
    def _():
        rank_ref[...] = expert_ranks(ids_ref[...], experts)
        total_ref[...] = jnp.zeros_like(total_ref)

    unpack_half(in_ref, 0, rows_ref, 0, tiles)
    unpack_extra(in_ref, tiles * HALF, rows_ref, peers * HALF)
    rank = rank_ref[pl.ds(pl.multiple_of(step * peers, peers), peers), :]
    which = jnp.concatenate([half_rows(rank, None, 0), extra_rows(rank, None)], axis=0)
    total_ref[...] += contract(which, rows_ref[...])


def combine_second_kernel(
    ids_ref, probs_ref, in_ref, slots_ref, before_ref, rank_ref, out_ref, probs_out_ref, rows_ref, total_ref
):
    step = pl.program_id(0)
    experts, tokens = rank_ref.shape
    peers, tiles = in_ref.shape[0], out_ref.shape[1] // LANE

    @pl.when(step == 0)
    def _():
        total_ref[...] = before_ref[...]
        slots = slots_ref[:, 0, :].astype(F32)
        rank = rank_ref[...]
        found = jnp.zeros((experts, tokens), F32)
        for s in range(CAP):
            found = found + jnp.where(rank == float(s), slots[:, s : s + 1], 0.0)
        ids = ids_ref[...]
        expert = iota((experts, tokens), 0)
        grads = [
            jnp.sum(jnp.where(ids[k : k + 1] == expert, found, 0.0), axis=0, keepdims=True)
            for k in range(ids.shape[0])
        ]
        probs_out_ref[...] = (jnp.concatenate(grads, axis=0) / probs_ref[...].astype(F32)).astype(BF)

    unpack_half(in_ref, 0, rows_ref, 0, tiles)
    rank = rank_ref[pl.ds(pl.multiple_of(step * peers, peers), peers), :]
    total_ref[...] += contract(half_rows(rank, None, HALF), rows_ref[...])

    @pl.when(step == pl.num_programs(0) - 1)
    def _():
        out_ref[...] = total_ref[...].astype(BF)


def combine_first(ids, got, width):
    experts, rows, _ = got.shape
    tokens = ids.shape[1]
    whole = lambda shape: pl.BlockSpec(shape, lambda i: (0, 0))
    return pl.pallas_call(
        combine_first_kernel,
        grid=(experts // PEERS,),
        out_shape=[jax.ShapeDtypeStruct((tokens, width), F32), jax.ShapeDtypeStruct((experts, tokens), F32)],
        in_specs=[whole(ids.shape), pl.BlockSpec((PEERS, rows, LANE), lambda i: (i, 0, 0))],
        out_specs=[whole((tokens, width)), whole((experts, tokens))],
        scratch_shapes=[pltpu.VMEM((PEERS * FIRST, width), BF)],
        compiler_params=pltpu.CompilerParams(vmem_limit_bytes=SUM_VMEM),
        cost_estimate=pl.CostEstimate(
            flops=2 * experts * FIRST * tokens * width, bytes_accessed=2 * experts * rows * LANE, transcendentals=0
        ),
        name="combine_a",
    )(ids, got)


def combine_second(ids, probs, got, before, rank):
    experts, rows, _ = got.shape
    tokens, width = before.shape
    whole = lambda a: pl.BlockSpec(a.shape, lambda i: (0, 0))
    return pl.pallas_call(
        combine_second_kernel,
        grid=(experts // SUM_PEERS,),
        out_shape=[jax.ShapeDtypeStruct(before.shape, BF), jax.ShapeDtypeStruct(ids.shape, BF)],
        in_specs=[
            whole(ids),
            whole(probs),
            pl.BlockSpec((SUM_PEERS, rows - TILE, LANE), lambda i: (i, 0, 0)),
            pl.BlockSpec((experts, TILE, LANE), lambda i: (0, rows // TILE - 1, 0)),
            whole(before),
            whole(rank),
        ],
        out_specs=[whole(before), whole(ids)],
        scratch_shapes=[pltpu.VMEM((SUM_PEERS * HALF, width), BF), pltpu.VMEM((tokens, width), F32)],
        compiler_params=pltpu.CompilerParams(vmem_limit_bytes=SUM_VMEM),
        cost_estimate=pl.CostEstimate(
            flops=2 * experts * HALF * tokens * width, bytes_accessed=2 * experts * rows * LANE, transcendentals=0
        ),
        name="combine_b",
    )(ids, probs, got, got, before, rank)


def exchange(x):
    return lax.all_to_all(x, ("ctx", "tp"), split_axis=0, concat_axis=0, tiled=True)


def other_core(x):
    return lax.ppermute(x, "dp", [(0, 1), (1, 0)])


def per_device(tokens, cotangent, probs, expert_ids, gate_weight, up_weight, down_weight):
    experts = lax.axis_size("ctx") * lax.axis_size("tp")
    gate_mat, up_mat, down_mat = gate_weight[0], up_weight[0], down_weight[0]
    ids, weights = expert_ids.T, probs.T
    mats = (gate_mat, up_mat, down_mat)
    sent_a, sent_b, *turned = lax.optimization_barrier(
        (*pack(ids, weights, tokens, cotangent, experts), *turn("turn_1", 1, mats))
    )
    got_a, sent_b, turned, mats = lax.optimization_barrier((exchange(sent_a), sent_b, turned, mats))
    got_b = exchange(sent_b)
    gate_t, up_t, down_t = turn("turn_0", 0, mats, turned)
    mats = (gate_mat, up_mat, down_t)

    def part(name, got, slot_grads=None, kept=()):
        rows, gate, up = project("gate_up_" + name, got, 0, mats[:2], kept[:1])
        far = other_core(gate), other_core(up)
        got, gate, up = lax.optimization_barrier((got, gate, up))
        cot_rows, back = project("back_" + name, got, 1, mats[2:], kept[1:2])
        far = *far, other_core(back)
        sent, act, gate_grad, up_grad, *slot_grads = pair(
            "pair_" + name, gate, far[0], up, far[1], back, far[2], gate_t, up_t, experts, slot_grads, kept[2:]
        )
        return sent, slot_grads, (rows, cot_rows, act, gate_grad, up_grad)

    pairs_a, (slot_grads,), kept = part("a", got_a)
    got_b, pairs_a = lax.optimization_barrier((got_b, pairs_a))
    back_a = exchange(pairs_a)
    pairs_b, _, (rows, cot_rows, act, gate_grad, up_grad) = part("b", got_b, slot_grads, kept)
    back_b = exchange(pairs_b)
    grad_down = contract(act, cot_rows).astype(BF)
    grad_gate = contract(rows, gate_grad).astype(BF)
    grad_up = contract(rows, up_grad).astype(BF)
    before, rank = combine_first(ids, back_a, tokens.shape[1])
    grad_tokens, grad_probs = combine_second(ids, weights, back_b, before, rank)
    return (grad_tokens, grad_probs.T, grad_gate[None], grad_up[None], grad_down[None])


def solution(mesh):
    return jax.shard_map(
        per_device,
        mesh=mesh,
        in_specs=(
            P(("ctx", "tp"), "dp"),
            P(("ctx", "tp"), "dp"),
            P(("ctx", "tp"), None),
            P(("ctx", "tp"), None),
            P(("ctx", "tp"), "dp", None),
            P(("ctx", "tp"), "dp", None),
            P(("ctx", "tp"), None, "dp"),
        ),
        out_specs=(
            P(("ctx", "tp"), "dp"),
            P(("ctx", "tp"), None),
            P(("ctx", "tp"), "dp", None),
            P(("ctx", "tp"), "dp", None),
            P(("ctx", "tp"), None, "dp"),
        ),
        check_vma=False,
    )
```

```python
import functools

import jax
import jax.numpy as jnp
from jax import lax
from jax.experimental import pallas as pl
from jax.experimental.pallas import tpu as pltpu
from jax.sharding import PartitionSpec as P

BF = jnp.bfloat16
F32 = jnp.float32
LANE = 128
HALF = 8
EXTRA = 2
CAP = 2 * HALF + EXTRA
FIRST = HALF + EXTRA
TILE = 16
GROUP = 16
PEERS = 32
SECOND_PEERS = 16
PACK_PEERS = 32
SUM_PEERS = 64
VMEM = 62 * 2**20
SUM_VMEM = 24 * 2**20


def iota(shape, dim):
    return lax.broadcasted_iota(jnp.int32, shape, dim)


def dot(a, b):
    return jnp.dot(a, b, preferred_element_type=F32)


def contract(left, right):
    return lax.dot_general(left, right, (((0,), (0,)), ((), ())), preferred_element_type=F32)


def expert_ranks(ids, experts):
    top, tokens = ids.shape
    expert = iota((experts, tokens), 0)
    hit = jnp.zeros((experts, tokens), F32)
    for k in range(top):
        hit = hit + jnp.where(ids[k : k + 1] == expert, 1.0, 0.0)
    earlier = jnp.where(iota((tokens, tokens), 0) < iota((tokens, tokens), 1), 1.0, 0.0)
    rank = dot(hit.astype(BF), earlier.astype(BF))
    return jnp.where(hit > 0.0, rank, -1.0)


def expert_probs(ids, probs, experts):
    top, tokens = ids.shape
    expert = iota((experts, tokens), 0)
    out = jnp.zeros((experts, tokens), F32)
    for k in range(top):
        out = out + jnp.where(ids[k : k + 1] == expert, probs[k : k + 1], 0.0)
    return out


def by_slot(a, slots):
    peers, tokens = a.shape
    return jnp.broadcast_to(a[:, None, :], (peers, slots, tokens)).reshape(peers * slots, tokens)


def extra_order(pack):
    shape = (GROUP * TILE, GROUP * TILE)
    row, col = iota(shape, 0), iota(shape, 1)
    step = GROUP * EXTRA
    if pack:
        source = (row % TILE) // EXTRA * step + row // TILE * EXTRA + row % EXTRA
    else:
        source = (row % step) // EXTRA * TILE + row // step * EXTRA + row % EXTRA
    return jnp.where(col == source, 1.0, 0.0).astype(BF)


def store_half(out_ref, start, values):
    for c in range(0, values.shape[1] // LANE, 2):
        pair = [values[:, k * LANE : (k + 1) * LANE].reshape(-1, HALF, LANE) for k in (c, c + 1)]
        at = start + c * HALF
        out_ref[:, at : at + TILE, :] = jnp.concatenate(pair, axis=1).astype(BF)


def store_extra(out_ref, start, values):
    for g in range(values.shape[1] // LANE):
        at = start + g * TILE
        out_ref[:, at : at + TILE, :] = values[:, g * LANE : (g + 1) * LANE].reshape(-1, TILE, LANE)


def order_extra(out_ref, start, values):
    groups = values.shape[1] // LANE // 8
    order = extra_order(True)
    step = GROUP * EXTRA
    parts = []
    for p in range(values.shape[0] // step):
        some = values[p * step : (p + 1) * step]
        columns = [
            jnp.concatenate([some[:, (g * 8 + c) * LANE : (g * 8 + c + 1) * LANE] for g in range(groups)], axis=1)
            for c in range(8)
        ]
        parts.append(dot(order, jnp.concatenate(columns, axis=0)).astype(BF))
    store_extra(out_ref, start, jnp.concatenate(parts, axis=0))


def unpack_half(in_ref, start, out_ref, first, count):
    rows = in_ref.shape[0] * HALF
    for c in range(0, count, 2):
        at = start + c * HALF
        pair = in_ref[:, at : at + TILE, :].astype(F32)
        for k in range(2):
            column = first + c + k
            out_ref[:rows, column * LANE : (column + 1) * LANE] = (
                pair[:, k * HALF : (k + 1) * HALF, :].reshape(rows, LANE).astype(BF)
            )


def unpack_extra(in_ref, start, out_ref, base):
    groups = out_ref.shape[1] // LANE // 8
    order = extra_order(False)
    step = GROUP * EXTRA
    for p in range(in_ref.shape[0] // GROUP):
        some = in_ref.at[p * GROUP : (p + 1) * GROUP]
        values = jnp.concatenate(
            [some[:, start + g * TILE : start + (g + 1) * TILE, :].reshape(-1, LANE) for g in range(groups)], axis=1
        )
        ordered = dot(order, values).astype(BF)
        for g in range(groups):
            for c in range(8):
                at = (g * 8 + c) * LANE
                out_ref[base + p * step : base + (p + 1) * step, at : at + LANE] = ordered[
                    c * step : (c + 1) * step, g * LANE : (g + 1) * LANE
                ]


def half_rows(rank, value, start):
    rank = by_slot(rank, HALF)
    hit = rank == (start + iota(rank.shape, 0) % HALF).astype(F32)
    return jnp.where(hit, 1.0 if value is None else by_slot(value, HALF), 0.0).astype(BF)


def extra_rows(rank, value):
    peers = rank.shape[0]
    rank = by_slot(rank, 8)
    hit = rank == (2 * HALF + iota(rank.shape, 0) % 8).astype(F32)
    eight = jnp.where(hit, 1.0 if value is None else by_slot(value, 8), 0.0).astype(BF)
    shape = (peers * EXTRA, peers * 8)
    keep = iota(shape, 1) == iota(shape, 0) // EXTRA * 8 + iota(shape, 0) % EXTRA
    return dot(jnp.where(keep, 1.0, 0.0).astype(BF), eight).astype(BF)


def wide_extra_rows(rank, value):
    rank = by_slot(rank, TILE)
    row = iota(rank.shape, 0)
    hit = rank == (2 * HALF + row % EXTRA).astype(F32)
    extra = jnp.where(hit, 1.0 if value is None else by_slot(value, TILE), 0.0)
    column = (row % TILE) // EXTRA
    return jnp.concatenate([jnp.where(column == c, extra, 0.0).astype(BF) for c in range(8)], axis=1)


def stack_columns(x_ref, side_ref):
    tokens, width = x_ref.shape
    groups = width // LANE // 8
    for c in range(8):
        for g in range(groups):
            at = (g * 8 + c) * LANE
            side_ref[c * tokens : (c + 1) * tokens, g * LANE : (g + 1) * LANE] = x_ref[:, at : at + LANE]


def start_pack(ids_ref, probs_ref, rank_ref, prob_ref):
    experts = rank_ref.shape[0]
    rank_ref[...] = expert_ranks(ids_ref[...], experts)
    prob_ref[...] = expert_probs(ids_ref[...], probs_ref[...].astype(F32), experts)


def pack_first_kernel(ids_ref, probs_ref, x_ref, cot_ref, out_ref, rank_ref, prob_ref, side_ref, cot_side_ref):
    step = pl.program_id(0)
    half = x_ref.shape[1] // LANE * HALF
    part = x_ref.shape[1] // LANE * FIRST
    count = out_ref.shape[0]

    @pl.when(step == 0)
    def _():
        start_pack(ids_ref, probs_ref, rank_ref, prob_ref)
        stack_columns(x_ref, side_ref)
        stack_columns(cot_ref, cot_side_ref)

    peers = pl.ds(pl.multiple_of(step * count, count), count)
    rank, prob = rank_ref[peers, :], prob_ref[peers, :]
    for start, value, ref, side in ((0, None, x_ref, side_ref), (part, prob, cot_ref, cot_side_ref)):
        store_half(out_ref, start, dot(half_rows(rank, value, 0), ref[...]))
        store_extra(out_ref, start + half, dot(wide_extra_rows(rank, value), side[...]).astype(BF))


def pack(name, kernel, slots, sides, ids, probs, values, experts):
    tokens, width = values[0].shape
    rows = width // LANE * slots
    return pl.pallas_call(
        kernel,
        grid=(experts // PACK_PEERS,),
        out_shape=jax.ShapeDtypeStruct((experts, rows, LANE), BF),
        in_specs=[pl.BlockSpec(a.shape, lambda i: (0, 0)) for a in (ids, probs, *values)],
        out_specs=pl.BlockSpec((PACK_PEERS, rows, LANE), lambda i: (i, 0, 0)),
        scratch_shapes=[pltpu.VMEM((experts, tokens), F32)] * 2 + [pltpu.VMEM((8 * tokens, width // 8), BF)] * sides,
        compiler_params=pltpu.CompilerParams(vmem_limit_bytes=VMEM),
        cost_estimate=pl.CostEstimate(
            flops=4 * experts * slots * tokens * width, bytes_accessed=2 * experts * rows * LANE, transcendentals=0
        ),
        name=name,
    )(ids, probs, *values)


def ahead_kernel(core, count, ids_ref, probs_ref, *refs):
    mats, (x_ref, cot_ref), refs = refs[:count], refs[count : count + 2], refs[-(4 * count + 9) :]
    outs, out_ref, refs = refs[:count], refs[count], refs[count + 1 :]
    held, turned, refs = refs[:count], refs[count : 2 * count], refs[2 * count :]
    x, cot, packed, rank_ref, prob_ref = refs[:5]
    mat_sems, x_sem, cot_sem, pack_sems = refs[5 : 5 + count], refs[5 + count], refs[6 + count], refs[7 + count]
    experts = out_ref.shape[0]

    @pl.when(lax.axis_index("dp") == core)
    def _():
        values = [pltpu.make_async_copy(x_ref, x, x_sem), pltpu.make_async_copy(cot_ref, cot, cot_sem)]
        for copy in values:
            copy.start()
        for mat, a, b, out, sem in zip(mats, held, turned, outs, mat_sems):
            load = pltpu.make_async_copy(mat, a, sem)
            load.start()
            load.wait()
            for at in range(0, a.shape[0], 256):
                b[:, at : at + 256] = a[at : at + 256, :].T
            store = pltpu.make_async_copy(b, out, sem)
            store.start()
            store.wait()
        for copy in values:
            copy.wait()
        start_pack(ids_ref, probs_ref, rank_ref, prob_ref)
        half = x.shape[1] // LANE * HALF
        stores = []
        for n in range(experts // PACK_PEERS):
            peers = pl.ds(n * PACK_PEERS, PACK_PEERS)
            rank, prob = rank_ref[peers, :], prob_ref[peers, :]
            slot = packed.at[n]
            store_half(slot, 0, dot(half_rows(rank, None, HALF), x[...]))
            store_half(slot, half, dot(half_rows(rank, prob, HALF), cot[...]))
            stores.append(pltpu.make_async_copy(slot, out_ref.at[peers], pack_sems.at[n]))
            stores[-1].start()
        for store in stores:
            store.wait()


def ahead(name, core, ids, probs, mats, values, experts, before=()):
    tokens, width = values[0].shape
    rows = width // LANE * 2 * HALF
    steps = experts // PACK_PEERS
    shapes = [m.shape for m in mats]
    outs = [shape[::-1] for shape in shapes] + [(experts, rows, LANE)]
    anywhere = pl.BlockSpec(memory_space=pl.ANY)
    given = (*mats, *values, *before)
    return pl.pallas_call(
        functools.partial(ahead_kernel, core, len(mats)),
        out_shape=[jax.ShapeDtypeStruct(shape, BF) for shape in outs],
        in_specs=[pl.BlockSpec(memory_space=pltpu.VMEM)] * 2 + [anywhere] * len(given),
        out_specs=[anywhere] * len(outs),
        input_output_aliases={2 + len(given) - len(before) + k: k for k in range(len(before))},
        scratch_shapes=[pltpu.VMEM(shape, BF) for shape in shapes]
        + [pltpu.VMEM(shape[::-1], BF) for shape in shapes]
        + [pltpu.VMEM((tokens, width), BF)] * 2
        + [pltpu.VMEM((steps, PACK_PEERS, rows, LANE), BF)]
        + [pltpu.VMEM((experts, tokens), F32)] * 2
        + [pltpu.SemaphoreType.DMA] * (len(mats) + 2)
        + [pltpu.SemaphoreType.DMA((steps,))],
        compiler_params=pltpu.CompilerParams(vmem_limit_bytes=VMEM),
        cost_estimate=pl.CostEstimate(
            flops=4 * experts * HALF * tokens * width,
            bytes_accessed=sum(8 * a * b for a, b in shapes) + 2 * experts * rows * LANE,
            transcendentals=0,
        ),
        name=name,
    )(ids, probs, *given)


def turn_kernel(core, count, *refs):
    ins, outs = refs[:count], refs[-5 * count : -4 * count]
    held, turned = refs[-4 * count : -3 * count], refs[-3 * count : -2 * count]
    in_sems, out_sems = refs[-2 * count : -count], refs[-count:]

    @pl.when(lax.axis_index("dp") == core)
    def _():
        loads = [pltpu.make_async_copy(a, b, sem) for a, b, sem in zip(ins, held, in_sems)]
        stores = [pltpu.make_async_copy(a, b, sem) for a, b, sem in zip(turned, outs, out_sems)]
        for load in loads:
            load.start()
        for load, store, a, b in zip(loads, stores, held, turned):
            load.wait()
            for at in range(0, a.shape[0], 256):
                b[:, at : at + 256] = a[at : at + 256, :].T
            store.start()
        for store in stores:
            store.wait()


def turn(name, core, mats, before=()):
    shapes = [m.shape for m in mats]
    anywhere = pl.BlockSpec(memory_space=pl.ANY)
    return pl.pallas_call(
        functools.partial(turn_kernel, core, len(mats)),
        out_shape=[jax.ShapeDtypeStruct(shape[::-1], BF) for shape in shapes],
        in_specs=[anywhere] * (len(mats) + len(before)),
        out_specs=[anywhere] * len(mats),
        input_output_aliases={len(mats) + k: k for k in range(len(before))},
        scratch_shapes=[pltpu.VMEM(shape, BF) for shape in shapes]
        + [pltpu.VMEM(shape[::-1], BF) for shape in shapes]
        + [pltpu.SemaphoreType.DMA] * (2 * len(mats)),
        compiler_params=pltpu.CompilerParams(vmem_limit_bytes=VMEM),
        cost_estimate=pl.CostEstimate(flops=0, bytes_accessed=sum(4 * a * b for a, b in shapes), transcendentals=0),
        name=name,
    )(*mats, *before)


def project_kernel(extra, x_in, cot_in, gate_w, up_w, down_w, *refs):
    x_ref, cot_ref, gate_ref, up_ref, back_ref = refs[-5:]
    peers = x_in.shape[0]
    tiles = x_ref.shape[1] // LANE
    for in_ref, rows_ref in ((x_in, x_ref), (cot_in, cot_ref)):
        unpack_half(in_ref, 0, rows_ref, 0, tiles)
        if extra:
            unpack_extra(in_ref, tiles * HALF, rows_ref, peers * HALF)
    gate_ref[...] = dot(x_ref[...], gate_w[...]).astype(BF)
    up_ref[...] = dot(x_ref[...], up_w[...]).astype(BF)
    back_ref[...] = dot(cot_ref[...], down_w[...]).astype(BF)


def project(name, got, weights, kept=()):
    experts, both, _ = got.shape
    width, hidden = weights[0].shape
    part = both // 2
    slots = part * LANE // width
    peers = SECOND_PEERS if kept else PEERS
    total, rows = experts * slots, peers * slots
    first = experts * FIRST // rows if kept else 0
    whole = experts * CAP
    return pl.pallas_call(
        functools.partial(project_kernel, not kept),
        grid=(experts // peers,),
        out_shape=[jax.ShapeDtypeStruct((whole, width), BF)] * 2 + [jax.ShapeDtypeStruct((total, hidden), BF)] * 3,
        in_specs=[pl.BlockSpec((peers, part, LANE), lambda i, at=at: (i, at, 0)) for at in range(2)]
        + [pl.BlockSpec(w.shape, lambda i: (0, 0)) for w in weights]
        + [pl.BlockSpec(memory_space=pl.ANY) for _ in kept],
        out_specs=[pl.BlockSpec((rows, width), lambda i: (first + i, 0))] * 2
        + [pl.BlockSpec((rows, hidden), lambda i: (i, 0))] * 3,
        input_output_aliases={5 + k: k for k in range(len(kept))},
        compiler_params=pltpu.CompilerParams(vmem_limit_bytes=VMEM),
        cost_estimate=pl.CostEstimate(
            flops=6 * total * width * hidden,
            bytes_accessed=2 * (4 * total * width + 3 * (width + total) * hidden),
            transcendentals=0,
        ),
        name=name,
    )(got, got, *weights, *kept)


def slots_of(prob_grad, peers, extra):
    total = prob_grad.shape[0]
    main = peers * HALF
    row, lane = iota((total, LANE), 0), iota((total, LANE), 1)
    peer, of = iota((peers, total), 0), iota((peers, total), 1)
    slot, owner = row % HALF, of // HALF
    if extra:
        slot = jnp.where(row < main, slot, 2 * HALF + row % EXTRA)
        owner = jnp.where(of < main, owner, (of - main) // EXTRA)
    else:
        slot = slot + HALF
    by_lane = jnp.where(lane == slot, prob_grad, 0.0).astype(BF)
    return dot(jnp.where(peer == owner, 1.0, 0.0).astype(BF), by_lane)


def pair_kernel(extra, *refs):
    if extra:
        *refs, out_ref, act_ref, gg_ref, ug_ref, slots_out_ref = refs
    else:
        *refs, slots_ref, _, _, _, out_ref, act_ref, gg_ref, ug_ref = refs
    gate, gate_far, up, up_far, back, back_far, gate_t, up_t = refs
    g = gate[...].astype(F32) + gate_far[...].astype(F32)
    u = up[...].astype(F32) + up_far[...].astype(F32)
    b = back[...].astype(F32) + back_far[...].astype(F32)
    sigmoid = jax.nn.sigmoid(g)
    silu = g * sigmoid
    act = silu * u
    act_ref[...] = act.astype(BF)
    gg_ref[...] = (b * u * sigmoid * (1.0 + g * (1.0 - sigmoid))).astype(BF)
    ug_ref[...] = (b * silu).astype(BF)
    prob_grad = jnp.sum(act * b, axis=1, keepdims=True)
    y = dot(gg_ref[...], gate_t[...]) + dot(ug_ref[...], up_t[...])
    half = y.shape[1] // LANE * HALF
    peers = out_ref.shape[0]
    main = peers * HALF
    store_half(out_ref, 0, y[:main])
    slots = slots_of(prob_grad, peers, extra)
    if extra:
        order_extra(out_ref, half, y[main:].astype(BF))
        slots_out_ref[...] = slots
    else:
        grads = by_slot(slots + slots_ref[...], TILE)
        out_ref[:, half:, :] = grads.astype(BF).reshape(peers, TILE, LANE)


def pair(name, gate, gate_far, up, up_far, back, back_far, gate_t, up_t, experts, slot_grads=None, kept=()):
    total, hidden = gate.shape
    width = gate_t.shape[1]
    slots = total // experts
    extra = not kept
    peers = PEERS if extra else SECOND_PEERS
    rows = width // LANE * slots + (0 if extra else TILE)
    first = 0 if extra else experts * FIRST // (peers * slots)
    block = pl.BlockSpec((peers * slots, hidden), lambda i: (i, 0))
    placed = pl.BlockSpec((peers * slots, hidden), lambda i: (first + i, 0))
    whole = pl.BlockSpec(gate_t.shape, lambda i: (0, 0))
    small = pl.BlockSpec((peers, LANE), lambda i: (i, 0))
    more = () if extra else (slot_grads, *kept)
    return pl.pallas_call(
        functools.partial(pair_kernel, extra),
        grid=(experts // peers,),
        out_shape=[jax.ShapeDtypeStruct((experts, rows, LANE), BF)]
        + [jax.ShapeDtypeStruct((experts * CAP, hidden), BF)] * 3
        + [jax.ShapeDtypeStruct((experts, LANE), F32)] * extra,
        in_specs=[block] * 6
        + [whole] * 2
        + ([] if extra else [small] + [pl.BlockSpec(memory_space=pl.ANY)] * len(kept)),
        out_specs=[pl.BlockSpec((peers, rows, LANE), lambda i: (i, 0, 0))] + [placed] * 3 + [small] * extra,
        input_output_aliases={9 + k: 1 + k for k in range(len(kept))},
        compiler_params=pltpu.CompilerParams(vmem_limit_bytes=VMEM),
        cost_estimate=pl.CostEstimate(
            flops=4 * total * width * hidden,
            bytes_accessed=2 * (total * width + 9 * total * hidden + 2 * width * hidden),
            transcendentals=total * hidden,
        ),
        name=name,
    )(gate, gate_far, up, up_far, back, back_far, gate_t, up_t, *more)


def combine_first_kernel(ids_ref, in_ref, total_ref, rank_ref, rows_ref):
    step = pl.program_id(0)
    experts = rank_ref.shape[0]
    peers, tiles = in_ref.shape[0], total_ref.shape[1] // LANE

    @pl.when(step == 0)
    def _():
        rank_ref[...] = expert_ranks(ids_ref[...], experts)
        total_ref[...] = jnp.zeros_like(total_ref)

    unpack_half(in_ref, 0, rows_ref, 0, tiles)
    unpack_extra(in_ref, tiles * HALF, rows_ref, peers * HALF)
    rank = rank_ref[pl.ds(pl.multiple_of(step * peers, peers), peers), :]
    which = jnp.concatenate([half_rows(rank, None, 0), extra_rows(rank, None)], axis=0)
    total_ref[...] += contract(which, rows_ref[...])


def combine_second_kernel(
    ids_ref, probs_ref, in_ref, slots_ref, before_ref, rank_ref, out_ref, probs_out_ref, rows_ref, total_ref
):
    step = pl.program_id(0)
    experts, tokens = rank_ref.shape
    peers, tiles = in_ref.shape[0], out_ref.shape[1] // LANE

    @pl.when(step == 0)
    def _():
        total_ref[...] = before_ref[...]
        slots = slots_ref[:, 0, :].astype(F32)
        rank = rank_ref[...]
        found = jnp.zeros((experts, tokens), F32)
        for s in range(CAP):
            found = found + jnp.where(rank == float(s), slots[:, s : s + 1], 0.0)
        ids = ids_ref[...]
        expert = iota((experts, tokens), 0)
        grads = [
            jnp.sum(jnp.where(ids[k : k + 1] == expert, found, 0.0), axis=0, keepdims=True)
            for k in range(ids.shape[0])
        ]
        probs_out_ref[...] = (jnp.concatenate(grads, axis=0) / probs_ref[...].astype(F32)).astype(BF)

    unpack_half(in_ref, 0, rows_ref, 0, tiles)
    rank = rank_ref[pl.ds(pl.multiple_of(step * peers, peers), peers), :]
    total_ref[...] += contract(half_rows(rank, None, HALF), rows_ref[...])

    @pl.when(step == pl.num_programs(0) - 1)
    def _():
        out_ref[...] = total_ref[...].astype(BF)


def combine_first(ids, got, width):
    experts, rows, _ = got.shape
    tokens = ids.shape[1]
    whole = lambda shape: pl.BlockSpec(shape, lambda i: (0, 0))
    return pl.pallas_call(
        combine_first_kernel,
        grid=(experts // PEERS,),
        out_shape=[jax.ShapeDtypeStruct((tokens, width), F32), jax.ShapeDtypeStruct((experts, tokens), F32)],
        in_specs=[whole(ids.shape), pl.BlockSpec((PEERS, rows, LANE), lambda i: (i, 0, 0))],
        out_specs=[whole((tokens, width)), whole((experts, tokens))],
        scratch_shapes=[pltpu.VMEM((PEERS * FIRST, width), BF)],
        compiler_params=pltpu.CompilerParams(vmem_limit_bytes=SUM_VMEM),
        cost_estimate=pl.CostEstimate(
            flops=2 * experts * FIRST * tokens * width, bytes_accessed=2 * experts * rows * LANE, transcendentals=0
        ),
        name="combine_a",
    )(ids, got)


def combine_second(ids, probs, got, before, rank):
    experts, rows, _ = got.shape
    tokens, width = before.shape
    whole = lambda a: pl.BlockSpec(a.shape, lambda i: (0, 0))
    return pl.pallas_call(
        combine_second_kernel,
        grid=(experts // SUM_PEERS,),
        out_shape=[jax.ShapeDtypeStruct(before.shape, BF), jax.ShapeDtypeStruct(ids.shape, BF)],
        in_specs=[
            whole(ids),
            whole(probs),
            pl.BlockSpec((SUM_PEERS, rows - TILE, LANE), lambda i: (i, 0, 0)),
            pl.BlockSpec((experts, TILE, LANE), lambda i: (0, rows // TILE - 1, 0)),
            whole(before),
            whole(rank),
        ],
        out_specs=[whole(before), whole(ids)],
        scratch_shapes=[pltpu.VMEM((SUM_PEERS * HALF, width), BF), pltpu.VMEM((tokens, width), F32)],
        compiler_params=pltpu.CompilerParams(vmem_limit_bytes=SUM_VMEM),
        cost_estimate=pl.CostEstimate(
            flops=2 * experts * HALF * tokens * width, bytes_accessed=2 * experts * rows * LANE, transcendentals=0
        ),
        name="combine_b",
    )(ids, probs, got, got, before, rank)


def exchange(x):
    return lax.all_to_all(x, ("ctx", "tp"), split_axis=0, concat_axis=0, tiled=True)


def other_core(x):
    return lax.ppermute(x, "dp", [(0, 1), (1, 0)])


def per_device(tokens, cotangent, probs, expert_ids, gate_weight, up_weight, down_weight):
    experts = lax.axis_size("ctx") * lax.axis_size("tp")
    gate_mat, up_mat, down_mat = gate_weight[0], up_weight[0], down_weight[0]
    ids, weights = expert_ids.T, probs.T
    mats, values = (gate_mat, up_mat, down_mat), (tokens, cotangent)
    sent_a, *turned, sent_b = lax.optimization_barrier(
        (
            pack("pack_a", pack_first_kernel, 2 * FIRST, 2, ids, weights, values, experts),
            *ahead("ahead_1", 1, ids, weights, mats, values, experts),
        )
    )
    got_a, sent_b, turned, mats, values = lax.optimization_barrier((exchange(sent_a), sent_b, turned, mats, values))
    (sent_b,) = ahead("pack_b_0", 0, ids, weights, (), values, experts, (sent_b,))
    sent_b, turned, mats = lax.optimization_barrier((sent_b, turned, mats))
    got_b = exchange(sent_b)
    gate_t, up_t, down_t = turn("turn_0", 0, mats, turned)
    mats = (gate_mat, up_mat, down_t)

    def part(name, got, slot_grads=None, kept=()):
        rows, cot_rows, gate, up, back = project("project_" + name, got, mats, kept[:2])
        far = other_core(gate), other_core(up), other_core(back)
        sent, act, gate_grad, up_grad, *slot_grads = pair(
            "pair_" + name, gate, far[0], up, far[1], back, far[2], gate_t, up_t, experts, slot_grads, kept[2:]
        )
        return sent, slot_grads, (rows, cot_rows, act, gate_grad, up_grad)

    pairs_a, (slot_grads,), kept = part("a", got_a)
    got_b, pairs_a = lax.optimization_barrier((got_b, pairs_a))
    back_a = exchange(pairs_a)
    pairs_b, _, (rows, cot_rows, act, gate_grad, up_grad) = part("b", got_b, slot_grads, kept)
    back_b = exchange(pairs_b)
    grad_down = contract(act, cot_rows).astype(BF)
    grad_gate = contract(rows, gate_grad).astype(BF)
    grad_up = contract(rows, up_grad).astype(BF)
    before, rank = combine_first(ids, back_a, tokens.shape[1])
    grad_tokens, grad_probs = combine_second(ids, weights, back_b, before, rank)
    return (grad_tokens, grad_probs.T, grad_gate[None], grad_up[None], grad_down[None])


def solution(mesh):
    return jax.shard_map(
        per_device,
        mesh=mesh,
        in_specs=(
            P(("ctx", "tp"), "dp"),
            P(("ctx", "tp"), "dp"),
            P(("ctx", "tp"), None),
            P(("ctx", "tp"), None),
            P(("ctx", "tp"), "dp", None),
            P(("ctx", "tp"), "dp", None),
            P(("ctx", "tp"), None, "dp"),
        ),
        out_specs=(
            P(("ctx", "tp"), "dp"),
            P(("ctx", "tp"), None),
            P(("ctx", "tp"), "dp", None),
            P(("ctx", "tp"), "dp", None),
            P(("ctx", "tp"), None, "dp"),
        ),
        check_vma=False,
    )
```
